32 devices in a mesh: dp: 8 (over y, x, core), mp: 4 (over z).
Axes of the slice: x: 2, y: 2, z: 4, core: 2. Of those that a mesh axis runs over, the one named last changes fastest.
Arguments:
- ids: int32 [32768], P('dp'), may hold values from 0 to 32767
- hash_mult: int32 [1024], replicated, may hold values from 1 to 65520
- hash_add: int32 [1024], replicated, may hold values from 0 to 65520
- weight_first: bfloat16 [1800, 1024], P('mp'), may hold values from -0.1875 to 0.1875
- bias_first: float32 [1800], P('mp'), may hold values from -4 to 4
- scale_first: float32 [1800], P('mp'), may hold values from 0.1 to 1.9
- shift_first: float32 [1800], P('mp'), may hold values from -3 to 3
- weight_second: bfloat16 [1800, 1800], P('mp'), may hold values from -0.125 to 0.125
- bias_second: float32 [1800], P('mp'), may hold values from -4 to 4
- scale_second: float32 [1800], P('mp'), may hold values from 0.1 to 1.9
- shift_second: float32 [1800], P('mp'), may hold values from -3 to 3
- cotangent: bfloat16 [1800, 32768], P('mp', 'dp'), may hold values from -6 to 6
Outputs:
- output: bfloat16 [1800, 32768], P('mp', 'dp')
- grad_weight_first: float32 [1800, 1024], P('mp')
- grad_bias_first: float32 [1800], P('mp')
- grad_scale_first: float32 [1800], P('mp')
- grad_shift_first: float32 [1800], P('mp')
- grad_weight_second: float32 [1800, 1800], P('mp')
- grad_bias_second: float32 [1800], P('mp')
- grad_scale_second: float32 [1800], P('mp')
- grad_shift_second: float32 [1800], P('mp')
The draws below stay inside these ranges and needn't reach their ends.
All inputs are finite; a program needn't handle non-finite values.
Results may differ from the reference program's by a relative error of at most 0.03.
Values may be sent and summed in bfloat16 or wider, within the bound.
A program may use at most 192 MiB of HBM per device.

```python
import jax
import jax.numpy as jnp
from jax import lax

ENC = 1024
HID = 1800
ROWS_DEV = 4096
TOTAL = 32768


def draw_ids(key, part):
    key = jax.random.fold_in(key, 11)
    shards = TOTAL // ROWS_DEV
    key_table, key_cold, key_pick, key_coin = jax.random.split(key, 4)
    hot_table = jax.random.randint(key_table, (shards, 4), 0, 32768, dtype=jnp.int32)
    cold_ids = jax.random.randint(key_cold, (TOTAL,), 0, 32768, dtype=jnp.int32)
    picked = jax.random.randint(key_pick, (TOTAL,), 0, 4, dtype=jnp.int32)
    coin = jax.random.randint(key_coin, (TOTAL,), 0, 32, dtype=jnp.int32)
    shard_of = jnp.arange(TOTAL, dtype=jnp.int32) // ROWS_DEV
    limit = 5 + 10 * shard_of // max(shards - 1, 1)
    hot_ids = hot_table[shard_of, picked]
    return jnp.where(coin < limit, hot_ids, cold_ids).astype(jnp.int32)


def set_ends(values, rng, least, largest):
    extent = values.shape
    index_at = [jax.random.randint(jax.random.fold_in(rng, axis), (), 0, extent[axis]) for axis in range(len(extent))]
    values = values.at[tuple(index_at)].set(least)
    longest = extent.index(max(extent))
    index_at[longest] = (index_at[longest] + 1) % extent[longest]
    return values.at[tuple(index_at)].set(largest)


def block_scale(rng, dims, cuts, smallest, high):
    gain, own = 1.0, jax.random.fold_in(rng, 6)
    for dim, blocks in cuts:
        draws = jnp.exp(jax.random.uniform(jax.random.fold_in(own, dim), (blocks,), jnp.float32, smallest / len(cuts), high / len(cuts)))
        gain = gain * jnp.repeat(draws, dims[dim] // blocks).reshape([-1 if axis == dim else 1 for axis in range(len(dims))])
    return gain


def normal_values(key, shape, scale, reach, pieces=(), held_as=jnp.bfloat16):
    values = jax.random.normal(key, shape, jnp.float32) * scale
    if len(pieces) > 0:
        values = block_scale(key, shape, pieces, -0.22, 0.18) * values
    return jnp.clip(values, min=-reach, max=reach).astype(held_as)


def setup_inputs(seed: int = 0) -> dict:
    key_list = jax.random.split(jax.random.key(seed), 13)
    return {
        "ids": draw_ids(jax.random.fold_in(key_list[12], 71), 0),
        "hash_mult": set_ends(jax.random.randint(key_list[1], (ENC,), 1, 65521), jax.random.fold_in(key_list[1], 1), 1, 65520).astype(jnp.int32),
        "hash_add": set_ends(jax.random.randint(key_list[2], (ENC,), 0, 65521), jax.random.fold_in(key_list[2], 1), 0, 65520).astype(jnp.int32),
        "weight_first": normal_values(key_list[3], (HID, ENC), ENC ** -0.5, 0.1875, ((0, 4),)),
        "bias_first": normal_values(key_list[4], (HID,), 1.0, 4.0, ((0, 4),), jnp.float32),
        "scale_first": jnp.clip(1.0 + 0.18 * jax.random.normal(key_list[5], (HID,), jnp.float32), 0.1, 1.9),
        "shift_first": normal_values(key_list[6], (HID,), 0.5, 3.0, ((0, 4),), jnp.float32),
        "weight_second": normal_values(key_list[7], (HID, HID), HID ** -0.5, 0.125, ((0, 4),)),
        "bias_second": normal_values(key_list[8], (HID,), 1.0, 4.0, ((0, 4),), jnp.float32),
        "scale_second": jnp.clip(1.0 + 0.18 * jax.random.normal(key_list[9], (HID,), jnp.float32), 0.1, 1.9),
        "shift_second": normal_values(key_list[10], (HID,), 0.5, 3.0, ((0, 4),), jnp.float32),
        "cotangent": normal_values(key_list[11], (HID, TOTAL), 1.0, 6.0, ((0, 4), (1, 8))),
    }


@jax.custom_vjp
def low(v):
    return lax.optimization_barrier(v.astype(jnp.bfloat16)).astype(jnp.float32)

@jax.custom_vjp
def low_back(v):
    return v

def low_keep(v):
    return (low(v), None)

def low_pass(kept, grad):
    return (grad,)

def back_keep(v):
    return (v, None)

def back_low(kept, grad):
    return (low(grad),)
low.defvjp(low_keep, low_pass)
low_back.defvjp(back_keep, back_low)
epsilon = 1e-05

def mish(value):
    return value * jnp.tanh(jax.nn.softplus(value))

def batch_norm(acts, scale, shift):
    mean = lax.optimization_barrier(jnp.mean(acts, 0))
    var = lax.optimization_barrier(jnp.mean(acts * acts, 0)) - mean * mean
    return (acts - mean) * lax.rsqrt(var + epsilon) * scale + shift

def reference(ids, hash_mult, hash_add, weight_first, bias_first, scale_first, shift_first, weight_second, bias_second, scale_second, shift_second, cotangent):
    hashed = (ids[:, None] * hash_mult[None, :] + hash_add[None, :]) % 65521
    encoding = low(hashed.astype(jnp.float32) * (2.0 / 65520.0) - 1.0)

    def forward(w_one, b_one, g_one, s_one, w_two, b_two, g_two, s_two):
        pre_first = low_back(jnp.dot(encoding, w_one.T, precision=lax.Precision.HIGHEST) + b_one)
        hidden = low(batch_norm(mish(pre_first), g_one, s_one))
        pre_second = low_back(jnp.dot(hidden, w_two, precision=lax.Precision.HIGHEST) + b_two)
        return batch_norm(mish(pre_second), g_two, s_two)
    params = (weight_first.astype(jnp.float32), bias_first, scale_first, shift_first, weight_second.astype(jnp.float32), bias_second, scale_second, shift_second)
    output, pullback = jax.vjp(forward, *params)
    grads = pullback(cotangent.astype(jnp.float32).T)
    return (output.T.astype(jnp.bfloat16), grads[0], grads[1], grads[2], grads[3], grads[4], grads[5], grads[6], grads[7])
```

```python
import functools

import jax
import jax.numpy as jnp
from jax import lax
from jax.experimental import pallas as pl
from jax.experimental.pallas import tpu as pltpu
from jax.sharding import PartitionSpec as P

MESH = pl.DeviceIdType.MESH
F32, BF16, I32 = jnp.float32, jnp.bfloat16, jnp.int32
epsilon = 1e-05


def dot(a, b):
    return lax.dot_general(a, b, (((1,), (0,)), ((), ())), preferred_element_type=F32)


def dot_nt(a, b):
    return lax.dot_general(a, b, (((1,), (1,)), ((), ())), preferred_element_type=F32)


def mish_parts(v):
    u = jnp.exp(jnp.minimum(v, 20.0))
    n = u * (u + 2.0)
    d = n + 2.0
    r = pl.reciprocal(d, approx=True)
    r = r * (2.0 - d * r)
    t = n * r
    return v * t, t + v * ((4.0 * (n - u) * r) * r)


def mish(v):
    u = jnp.exp(jnp.minimum(v, 20.0))
    n = u * (u + 2.0)
    d = n + 2.0
    r = pl.reciprocal(d, approx=True)
    r = r * (2.0 - d * r)
    return v * (n * r)


def lane_part(x):
    out = x[:, :128]
    for at in range(128, x.shape[1], 128):
        out = out + x[:, at : at + 128]
    return out


def kernel(
    D, M, U, LP, K, R,
    ids_ref, mult_ref, add_ref, par_ref, w1_ref, w2_ref, cot_ref,
    out_ref, gw1_ref, gw2_ref, vec_ref,
    A, B, C, W2, E1, F, H, act2, slo2, G1, col, RW, acc, T, hcol,
    pv, ar1, ar2, ar2z, ar3, ar3z, ar4, ar4s, ar4z,
    w1s, w1r, w2s, w2r, pvs, pvr, cts, ctr, loc,
    a1s, a1r, a2s, a2r, a2zs, a2zr, a3s, a3r, a3zs, a3zr, a4s, a4r, a4zs, a4zr,
    g1s, g1r, g2s, g2r, *extra,
):
    Q = R // M
    G = D // 8
    TL = min(512, Q)
    NT = Q // TL
    PER = K // LP
    NA = M // PER
    K8 = K // 8
    J8 = M * LP // 8
    S8 = LP // 8
    N = float(R * D)
    d = lax.axis_index("dp")
    m = lax.axis_index("mp")
    i = lax.rem(d, 8)
    c = lax.rem(i, 2)
    x = lax.rem(i // 2, 2)
    y = i // 4
    hi = (1 - c) * x + c * y
    lo = (1 - c) * y + c * x
    p = 4 * c + 2 * hi + lo
    core_dev = (d + 1 - 2 * c, m)
    flip_x = d + 2 - 4 * x
    flip_y = d + 4 - 8 * y
    hi_dev = ((1 - c) * flip_x + c * flip_y, m)
    lo_dev = ((1 - c) * flip_y + c * flip_x, m)
    up = [lax.rem(m + k, M) for k in range(M)]
    down = [lax.rem(m - k + M, M) for k in range(M)]
    others = [lax.rem(d + k, D) for k in range(D)]
    sent = []

    def remote(src, dst, ss, rs, dev):
        cp = pltpu.make_async_remote_copy(
            src_ref=src, dst_ref=dst, send_sem=ss, recv_sem=rs, device_id=dev, device_id_type=MESH
        )
        return cp

    def send(src, dst, ss, rs, dev):
        cp = remote(src, dst, ss, rs, dev)
        cp.start()
        sent.append(cp)
        return cp

    def gone(cp):
        cp.wait_send()
        sent[:] = [other for other in sent if other is not cp]

    def lanes(ref, at, size):
        return ref.at[:, pl.ds(pl.multiple_of(at, 128), size)]

    def rows(ref, at, size):
        return ref.at[pl.ds(pl.multiple_of(at, 16), size)]

    bar = pltpu.get_barrier_semaphore()
    for k in range(1, D):
        pl.semaphore_signal(bar, inc=1, device_id=(others[k], m), device_id_type=MESH)
    for k in range(1, M):
        pl.semaphore_signal(bar, inc=1, device_id=(d, up[k]), device_id_type=MESH)

    w1_loc = pltpu.make_async_copy(w1_ref, C.at[m], loc.at[0])
    w1_loc.start()
    w2_loc = pltpu.make_async_copy(w2_ref, W2.at[m], loc.at[1])
    w2_loc.start()
    cot_loc = pltpu.make_async_copy(lanes(cot_ref, m * Q, Q), lanes(F.at[m], 0, Q), loc.at[2])
    cot_loc.start()
    pv[m] = par_ref[...]
    pl.semaphore_wait(bar, D - 1 + M - 1)

    ag1, ag2, agp, ct = {}, {}, {}, {}
    for k in range(1, M):
        agp[k] = send(par_ref, pv.at[m], pvs.at[k], pvr.at[k], (d, up[k]))
    for k in range(1, M):
        ag1[0, k] = send(
            lanes(w1_ref, p * K8, K8), lanes(C.at[m], p * K8, K8), w1s.at[0, k], w1r.at[0, k], (d, up[k])
        )
    for k in range(1, M):
        ag2[0, k] = send(
            lanes(w2_ref, p * J8, J8), lanes(W2.at[m], p * J8, J8), w2s.at[0, k], w2r.at[0, k], (d, up[k])
        )
    for k in range(1, M):
        ct[k] = send(lanes(cot_ref, up[k] * Q, Q), lanes(F.at[m], 0, Q), cts.at[k], ctr.at[k], (d, up[k]))

    def gather_stage(step, ag, buf, size, ss, rs):
        dev, at, width = {
            1: (lo_dev, p * size, size),
            2: (hi_dev, (4 * c + 2 * hi) * size, 2 * size),
            3: (core_dev, 4 * c * size, 4 * size),
        }[step]
        for k in range(1, M):
            ag[step - 1, k].wait_recv()
            part = lanes(buf.at[down[k]], at, width)
            ag[step, k] = send(part, part, ss.at[step, k], rs.at[step, k], dev)

    def stage1(step):
        gather_stage(step, ag1, C, K8, w1s, w1r)

    def stage2(step):
        gather_stage(step, ag2, W2, J8, w2s, w2r)

    hrow = jnp.concatenate(
        [mult_ref[...].astype(F32), add_ref[...].astype(F32), jnp.zeros((126, K), F32)], axis=0
    )
    hcol[...] = hrow.T

    HT = 128

    def encode(q, slot):
        def step(t, _):
            at = pl.multiple_of(t * HT, HT)
            both = hcol[pl.ds(at, HT), :].astype(I32)
            v = both[:, 0:1] * ids_ref[:, pl.ds(pl.multiple_of(q * Q, 128), Q)] + both[:, 1:2]
            for _ in range(2):
                top = lax.shift_right_logical(v, 16)
                v = (v & 65535) + ((top << 4) - top)
            v = jnp.where(v >= 65521, v - 65521, v)
            A[slot, pl.ds(at, HT), :] = (v.astype(F32) * (2.0 / 65520.0) - 1.0).astype(BF16)
            return 0

        lax.fori_loop(0, K // HT, step, 0)

    def make_cols():
        def step(b, _):
            col[b] = jnp.concatenate([RW[b], jnp.zeros((128 - RW.shape[1], LP), F32)], axis=0).T
            return 0

        lax.fori_loop(0, M, step, 0)

    def row_of(slot):
        return jnp.sum(acc[slot].T, axis=0, keepdims=True)

    acc[...] = jnp.zeros_like(acc)
    for b in range(M):
        B[pl.ds(b * LP + U // 16 * 16, LP - U // 16 * 16), :] = jnp.zeros((LP - U // 16 * 16, R), BF16)

    encode(m, m)
    encode(down[1], down[1])
    stage1(1)

    def enc_step(k, _):
        q = lax.rem(m + M - k, M)
        encode(q, q)
        return 0

    lax.fori_loop(2, M, enc_step, 0)
    stage1(2)
    for k in range(1, M):
        agp[k].wait_recv()
    for b in range(M):
        RW[b, 0:8] = pv[b]
        RW[b, 8:32] = jnp.zeros((24, LP), F32)
    make_cols()
    w1_loc.wait()

    def mm1_own(b):
        def step(t, _):
            at = pl.multiple_of(t * TL, TL)
            v = dot(C[b], A[m, :, pl.ds(at, TL)]) + col[b, :U, 0:1]
            act, slope = mish_parts(v)
            H[b, :, pl.ds(at, TL)] = slope.astype(BF16)
            B[pl.ds(pl.multiple_of(b * LP, LP), U), pl.ds(pl.multiple_of(m * Q + t * TL, TL), TL)] = act.astype(BF16)
            acc[0, :U] += lane_part(act)
            acc[1, :U] += lane_part(act * act)
            return 0

        lax.fori_loop(0, NT, step, 0)

    def mm1_rest(b):
        def step(t, _):
            q = lax.rem(m + 1 + t // NT, M)
            at = pl.multiple_of(lax.rem(t, NT) * TL, TL)
            act = mish(dot(C[b], A[q, :, pl.ds(at, TL)]) + col[b, :U, 0:1])
            B[pl.ds(pl.multiple_of(b * LP, LP), U), pl.ds(pl.multiple_of(q * Q + at, TL), TL)] = act.astype(BF16)
            acc[0, :U] += lane_part(act)
            acc[1, :U] += lane_part(act * act)
            return 0

        lax.fori_loop(0, (M - 1) * NT, step, 0)

    def mm1(b):
        mm1_own(b)
        mm1_rest(b)
        ar1[d, pl.ds(b, 1), :] = row_of(0)
        ar1[d, pl.ds(b + M, 1), :] = row_of(1)
        acc[0:2] = jnp.zeros((2, LP, 128), F32)

    mm1(m)
    stage2(1)
    stage1(3)
    for k in range(1, M):
        ag1[3, k].wait_recv()
        mm1(down[k])
        if k == 1:
            stage2(2)
        if k == 2:
            stage2(3)

    def all_dp(buf, ss, rs):
        cps = []
        for k in range(1, D):
            cps.append(send(buf.at[d], buf.at[d], ss.at[k], rs.at[k], (others[k], m)))
        return cps

    def total(buf, cps):
        for cp in cps:
            cp.wait_recv()
        out = buf[0]
        for k in range(1, D):
            out = out + buf[k]
        return out

    cps1 = all_dp(ar1, a1s, a1r)
    for step in range(1, 4):
        for k in range(1, M):
            gone(ag1[step, k])
    cot_all = []
    for q in range(M):
        cp = pltpu.make_async_copy(lanes(cot_ref, q * Q, Q), lanes(C.at[q], 0, Q), loc.at[3 + q])
        cot_all.append(cp)
        cp.start()
    w2_loc.wait()
    for k in range(1, M):
        ag2[3, k].wait_recv()

    T[...] = jnp.zeros_like(T)

    def make_e1(b):
        def step(h, _):
            T[:U, :] = W2[h, :, pl.ds(pl.multiple_of(b * LP, LP), LP)].astype(F32) * col[h, :U, 1:2]
            E1[:, pl.ds(pl.multiple_of(h * LP, LP), LP)] = T[...].T.astype(BF16)
            return 0

        lax.fori_loop(0, M, step, 0)

    const = jnp.zeros((8, M * LP), F32)
    for b in range(M):
        shift = jnp.broadcast_to(pv[b, 2:3, :U], (8, U))
        upper = shift.astype(BF16)
        lower = (shift - upper.astype(F32)).astype(BF16)
        const = const + dot(upper, W2[b]) + dot(lower, W2[b])
    for b in range(M):
        RW[b, 8:9] = const[0:1, b * LP : (b + 1) * LP] + pv[b, 3:4]
    make_e1(m)

    tot = total(ar1, cps1)
    mean = tot[:M] / N
    inv = lax.rsqrt(tot[M:] / N - mean * mean + epsilon)
    for b in range(M):
        RW[b, 9:10] = inv[b : b + 1]
        RW[b, 10:11] = -mean[b : b + 1] * inv[b : b + 1]
    make_cols()
    for cp in cot_all:
        cp.wait()

    def mm2(t, _):
        at = pl.multiple_of(t * TL, TL)
        for b in range(M):
            part = B[b * LP : b * LP + U, pl.ds(at, TL)].astype(F32)
            B[b * LP : b * LP + U, pl.ds(at, TL)] = (part * col[b, :U, 9:10] + col[b, :U, 10:11]).astype(BF16)
        v = dot(E1[:U], B[:, pl.ds(at, TL)]) + col[m, :U, 8:9]
        act, slope = mish_parts(v)
        act2[:, pl.ds(at, TL)] = act.astype(BF16)
        slo2[:, pl.ds(at, TL)] = slope.astype(BF16)
        g = C[t // NT, :, pl.ds(pl.multiple_of(lax.rem(t, NT) * TL, TL), TL)].astype(F32)
        acc[0, :U] += lane_part(act)
        acc[1, :U] += lane_part(act * act)
        acc[2, :U] += lane_part(g)
        acc[3, :U] += lane_part(g * act)
        return 0

    lax.fori_loop(0, M * NT, mm2, 0)
    for s in range(4):
        ar2[d, s : s + 1, :] = row_of(s)
    ar2[d, 4:8, :] = jnp.zeros((4, LP), F32)
    acc[...] = jnp.zeros_like(acc)
    cps2 = all_dp(ar2, a2s, a2r)

    def a_at(base, b):
        return base + b // PER, pl.multiple_of(lax.rem(b, PER) * LP, LP)

    def mm2_own(b):
        make_e1(b)
        act_at, row = a_at(0, b)

        def step(t, _):
            at = pl.multiple_of(t * TL, TL)
            v = dot(E1[:U], B[:, pl.ds(pl.multiple_of(m * Q + t * TL, TL), TL)]) + col[b, :U, 8:9]
            act, slope = mish_parts(v)
            A[act_at, pl.ds(row, U), pl.ds(at, TL)] = act.astype(BF16)
            A[act_at + NA, pl.ds(row, U), pl.ds(at, TL)] = slope.astype(BF16)
            return 0

        lax.fori_loop(0, NT, step, 0)

    def own_loop(k, _):
        mm2_own(lax.rem(m + k, M))
        return 0

    mm2_own(up[1])
    tot = total(ar2, cps2)
    mean = tot[0:1] / N
    inv = lax.rsqrt(tot[1:2] / N - mean * mean + epsilon)
    sum_g = tot[2:3]
    sum_gn = inv * (tot[3:4] - mean * sum_g)
    k1 = pv[m, 4:5] * inv
    k2 = -k1 * inv * sum_gn / N
    k3 = -k1 * sum_g / N - mean * k2
    ar2z[m, 0:1] = k1
    ar2z[m, 1:2] = k2
    ar2z[m, 2:3] = k3
    ar2z[m, 3:4] = k1
    ar2z[m, 4:5] = pv[m, 5:6] - mean * k1
    ar2z[m, 5:6] = sum_g
    ar2z[m, 6:7] = sum_gn
    ar2z[m, 7:8] = jnp.zeros((1, LP), F32)
    cps2z = [send(ar2z.at[m], ar2z.at[m], a2zs.at[k], a2zr.at[k], (d, up[k])) for k in range(1, M)]
    lax.fori_loop(2, M, own_loop, 0)
    for cp in cps2z:
        cp.wait_recv()
    for b in range(M):
        RW[b, 16:24] = ar2z[b]
    make_cols()

    def back2(t, _):
        at = pl.multiple_of(t * TL, TL)
        a = act2[:, pl.ds(at, TL)].astype(F32)
        g = C[t // NT, :, pl.ds(pl.multiple_of(lax.rem(t, NT) * TL, TL), TL)].astype(F32)
        act2[:, pl.ds(at, TL)] = (a * col[m, :U, 19:20] + col[m, :U, 20:21]).astype(BF16)
        grad = (g * col[m, :U, 16:17] + a * col[m, :U, 17:18] + col[m, :U, 18:19]) * slo2[:, pl.ds(at, TL)].astype(F32)
        grad = grad.astype(BF16)
        slo2[:, pl.ds(at, TL)] = grad
        acc[0, :U] += lane_part(grad.astype(F32))
        return 0

    lax.fori_loop(0, M * NT, back2, 0)
    out_copy = pltpu.make_async_copy(act2, out_ref, loc.at[0])
    out_copy.start()
    gb2 = row_of(0)
    ar3[d, 2 * M : 2 * M + 1, :] = gb2
    ar3[d, 2 * M + 1 : 2 * M + 8, :] = jnp.zeros((7, LP), F32)
    acc[0:1] = jnp.zeros((1, LP, 128), F32)

    PADAT = U // 16 * 16

    def put_grad(b, value, at, size):
        slot, row = a_at(NA, b)
        A[slot, pl.ds(row, U), pl.ds(at, size)] = value

    for b in range(M):
        slot, row = NA + b // PER, (b % PER) * LP
        A[slot, row + PADAT : row + LP, :] = jnp.where(
            lax.broadcasted_iota(I32, (LP - PADAT, Q), 0) < U - PADAT,
            A[slot, row + PADAT : row + LP, :].astype(F32),
            0.0,
        ).astype(BF16)
    cot_loc.wait()

    def back2_own(b):
        act_at, row = a_at(0, b)

        def step(t, _):
            at = pl.multiple_of(t * TL, TL)
            a = A[act_at, pl.ds(row, U), pl.ds(at, TL)].astype(F32)
            s = A[act_at + NA, pl.ds(row, U), pl.ds(at, TL)].astype(F32)
            g = F[b, :, pl.ds(at, TL)].astype(F32)
            grad = (g * col[b, :U, 16:17] + a * col[b, :U, 17:18] + col[b, :U, 18:19]) * s
            A[act_at + NA, pl.ds(row, U), pl.ds(at, TL)] = grad.astype(BF16)
            return 0

        lax.fori_loop(0, NT, step, 0)

    def copy_own(t, _):
        at = pl.multiple_of(t * TL, TL)
        put_grad(m, slo2[:, pl.ds(pl.multiple_of(m * Q + t * TL, TL), TL)], at, TL)
        return 0

    lax.fori_loop(0, NT, copy_own, 0)
    for k in range(1, M):
        ct[k].wait_recv()
        back2_own(down[k])

    def d_hidden(b):
        def step(t, _):
            at = pl.multiple_of(t * TL, TL)
            dh = dot(W2[b, :, 0:K], A[NA, :, pl.ds(at, TL)])
            for n in range(1, NA):
                dh = dh + dot(W2[b, :, n * K : (n + 1) * K], A[NA + n, :, pl.ds(at, TL)])
            norm = B[pl.ds(pl.multiple_of(b * LP, LP), U), pl.ds(pl.multiple_of(m * Q + t * TL, TL), TL)].astype(F32)
            F[b, :, pl.ds(at, TL)] = dh.astype(BF16)
            acc[0, :U] += lane_part(dh)
            acc[1, :U] += lane_part(dh * norm)
            return 0

        lax.fori_loop(0, NT, step, 0)
        ar3[d, pl.ds(b, 1), :] = row_of(0)
        ar3[d, pl.ds(b + M, 1), :] = row_of(1)
        acc[0:2] = jnp.zeros((2, LP, 128), F32)

    def d_hidden_step(b, _):
        d_hidden(b)
        return 0

    lax.fori_loop(0, M, d_hidden_step, 0)
    for step in range(1, 4):
        for k in range(1, M):
            gone(ag2[step, k])
    cps3 = all_dp(ar3, a3s, a3r)

    def grad_w2(b, _):
        g = dot_nt(B[pl.ds(pl.multiple_of(b * LP, LP), LP), :], slo2[...])
        g = g * col[b, :, 1:2] + col[b, :, 2:3] * gb2[:, :U]
        E1[:, pl.ds(pl.multiple_of(b * LP, LP), U)] = g.astype(BF16)
        return 0

    lax.fori_loop(0, M, grad_w2, 0)
    tot = total(ar3, cps3)
    ar3z[m] = tot[: 2 * M]
    gb2_all = tot[2 * M : 2 * M + 1]
    cps3z = [send(ar3z.at[m], ar3z.at[m], a3zs.at[k], a3zr.at[k], (d, up[k])) for k in range(1, M)]
    encode(m, 0)
    for cp in cps3z:
        cp.wait_recv()
    tot = ar3z[0]
    for b in range(1, M):
        tot = tot + ar3z[b]

    R2 = W2.at[0]
    h2 = LP // 2
    g2cp = {}
    g2cp[0] = send(rows(E1, (1 - c) * h2, h2), rows(R2, 0, h2), g2s.at[0], g2r.at[0], core_dev)

    for b in range(M):
        k1 = pv[b, 1:2] * RW[b, 9:10]
        k2 = -k1 * tot[M + b : M + b + 1] / N
        k3 = -k1 * tot[b : b + 1] / N
        RW[b, 16:17] = k1
        RW[b, 17:18] = k2
        RW[b, 18:19] = k3
    make_cols()
    pick = lax.broadcasted_iota(I32, (2 * M, 1), 0)
    vec_ref[0:1, :] = jnp.zeros((1, LP), F32)
    vec_ref[1:2, :] = jnp.sum(jnp.where(pick == M + m, tot, 0.0), axis=0, keepdims=True)
    vec_ref[2:3, :] = jnp.sum(jnp.where(pick == m, tot, 0.0), axis=0, keepdims=True)
    vec_ref[3:4, :] = gb2_all
    vec_ref[4:5, :] = ar2z[m, 6:7]
    vec_ref[5:6, :] = ar2z[m, 5:6]
    vec_ref[6:8, :] = jnp.zeros((2, LP), F32)

    def back1(b):
        def step(t, _):
            at = pl.multiple_of(t * TL, TL)
            norm = B[pl.ds(pl.multiple_of(b * LP, LP), U), pl.ds(pl.multiple_of(m * Q + t * TL, TL), TL)].astype(F32)
            dh = F[b, :, pl.ds(at, TL)].astype(F32)
            grad = dh * col[b, :U, 16:17] + norm * col[b, :U, 17:18] + col[b, :U, 18:19]
            grad = (grad * H[b, :, pl.ds(at, TL)].astype(F32)).astype(BF16)
            H[b, :, pl.ds(at, TL)] = grad
            acc[0, :U] += lane_part(grad.astype(F32))
            return 0

        lax.fori_loop(0, NT, step, 0)
        ar4[d, pl.ds(b, 1), :] = row_of(0)
        acc[0:1] = jnp.zeros((1, LP, 128), F32)

        def mm(t, _):
            at = pl.multiple_of(t * TL, TL)
            F[b, :, pl.ds(at, TL)] = dot_nt(H[b], A[0, pl.ds(at, TL), :]).astype(BF16)
            return 0

        lax.fori_loop(0, K // TL, mm, 0)

    ar4[d] = jnp.zeros((ar4.shape[1], LP), F32)
    K4, K2, half = 2 * K8, 4 * K8, K // 2
    g1cp = {}
    for b in range(M):
        back1(b)
        g1cp[0, b] = send(
            lanes(F.at[b], (1 - c) * K2, K2), lanes(C.at[b], 0, K2), g1s.at[0, b], g1r.at[0, b], core_dev
        )
    cps4 = all_dp(ar4, a4s, a4r)

    def add_rows(to, at, other, size):
        def step(t, _):
            s = pl.multiple_of(t * 16, 16)
            to[pl.ds(pl.multiple_of(at + s, 16), 16), :] = (
                to[pl.ds(pl.multiple_of(at + s, 16), 16), :].astype(F32) + other(s).astype(F32)
            ).astype(BF16)
            return 0

        lax.fori_loop(0, size // 16, step, 0)

    def g2_step(n):
        g2cp[n - 1].wait_recv()
        size = h2 >> (n - 1)
        at = {1: 4 * c, 2: 4 * c + 2 * hi, 3: p}[n] * S8
        start = {1: 0, 2: h2, 3: h2 + h2 // 2}[n]
        add_rows(E1, at, lambda s: W2[0, pl.ds(pl.multiple_of(start + s, 16), 16), :], size)

    def g1_step(n, b):
        g1cp[n - 1, b].wait_recv()
        size = K2 >> (n - 1)
        at = pl.multiple_of({1: 4 * c, 2: 4 * c + 2 * hi, 3: p}[n] * K8, 128)
        start = {1: 0, 2: K2, 3: K2 + K4}[n]
        F[b, :, pl.ds(at, size)] = (
            F[b, :, pl.ds(at, size)].astype(F32) + C[b, :, start : start + size].astype(F32)
        ).astype(BF16)

    g2_step(1)
    g2cp[1] = send(
        rows(E1, (4 * c + 2 * (1 - hi)) * S8, 2 * S8), rows(R2, h2, 2 * S8), g2s.at[1], g2r.at[1], hi_dev
    )
    for b in range(M):
        g1_step(1, b)
        g1cp[1, b] = send(
            lanes(F.at[b], (4 * c + 2 * (1 - hi)) * K8, K4), lanes(C.at[b], K2, K4), g1s.at[1, b], g1r.at[1, b], hi_dev
        )
    tot4 = total(ar4, cps4)
    for b in range(M):
        ar4s[b] = jnp.broadcast_to(tot4[b : b + 1], (8, LP))
    ar4z[m] = ar4s[m]
    cps4z = [send(ar4s.at[up[k]], ar4z.at[m], a4zs.at[k], a4zr.at[k], (d, up[k])) for k in range(1, M)]
    g2_step(2)
    g2cp[2] = send(
        rows(E1, (4 * c + 2 * hi + 1 - lo) * S8, S8), rows(R2, h2 + 2 * S8, S8), g2s.at[2], g2r.at[2], lo_dev
    )
    for b in range(M):
        g1_step(2, b)
        g1cp[2, b] = send(
            lanes(F.at[b], (4 * c + 2 * hi + 1 - lo) * K8, K8), lanes(C.at[b], K2 + K4, K8), g1s.at[2, b], g1r.at[2, b], lo_dev
        )
    g2_step(3)
    for b in range(M):
        g1_step(3, b)
    if G > 1:
        x1, x2, x1s, x1r, x2s, x2r = extra
        cpsx = []
        for k in range(1, G):
            to = (lax.rem(d + 8 * k, D), m)
            cpsx.append(send(rows(E1, p * S8, S8), x2.at[d // 8], x2s.at[k], x2r.at[k], to))
            for b in range(M):
                cpsx.append(send(lanes(F.at[b], p * K8, K8), x1.at[d // 8, b], x1s.at[k, b], x1r.at[k, b], to))
        x2[d // 8] = E1[pl.ds(pl.multiple_of(p * S8, 16), S8), :]
        for b in range(M):
            x1[d // 8, b] = F[b, :, pl.ds(pl.multiple_of(p * K8, 128), K8)]
        for cp in cpsx:
            cp.wait()
        v = x2[0].astype(F32)
        for k in range(1, G):
            v = v + x2[k].astype(F32)
        E1[pl.ds(pl.multiple_of(p * S8, 16), S8), :] = v.astype(BF16)
        for b in range(M):
            v = x1[0, b].astype(F32)
            for k in range(1, G):
                v = v + x1[k, b].astype(F32)
            F[b, :, pl.ds(pl.multiple_of(p * K8, 128), K8)] = v.astype(BF16)

    g1z = [
        send(
            lanes(F.at[up[k]], p * K8, K8), C.at[m, :, pl.ds(K2 + K4 + K8, K8)], g1s.at[3, k], g1r.at[3, k], (d, up[k])
        )
        for k in range(1, M)
    ]
    Z2 = W2.at[1]
    p64 = pl.multiple_of(p * S8, 16)
    g2z = [
        send(
            E1.at[pl.ds(p64, S8), pl.ds(pl.multiple_of(up[k] * LP, LP), LP)],
            Z2.at[pl.ds(0, S8), pl.ds(pl.multiple_of(m * LP, LP), LP)],
            g2s.at[3 + k], g2r.at[3 + k], (d, up[k]),
        )
        for k in range(1, M)
    ]
    C[m, :, K2 + K4 + K8 : K] = F[m, :, pl.ds(pl.multiple_of(p * K8, 128), K8)]
    W2[1, 0:S8, pl.ds(pl.multiple_of(m * LP, LP), LP)] = E1[
        pl.ds(p64, S8), pl.ds(pl.multiple_of(m * LP, LP), LP)
    ]
    for cp in g1z:
        cp.wait_recv()
    v = C[0, :, K2 + K4 + K8 : K].astype(F32)
    for b in range(1, M):
        v = v + C[b, :, K2 + K4 + K8 : K].astype(F32)
    G1[:, pl.ds(pl.multiple_of(p * K8, 128), K8)] = v.astype(BF16)
    ga = send(lanes(G1, p * K8, K8), lanes(G1, p * K8, K8), g1s.at[4, 0], g1r.at[4, 0], lo_dev)
    for cp in g2z:
        cp.wait_recv()
    at2 = pl.multiple_of((2 * hi + lo) * S8, 16)
    W2[2 + c, pl.ds(at2, S8), :] = W2[1, 0:S8, :]
    gb = send(rows(W2.at[2 + c], at2, S8), rows(W2.at[2 + c], at2, S8), g2s.at[3 + M], g2r.at[3 + M], lo_dev)
    ga.wait_recv()
    part = lanes(G1, (4 * c + 2 * hi) * K8, K4)
    ga = send(part, part, g1s.at[4, 1], g1r.at[4, 1], hi_dev)
    gb.wait_recv()
    part = rows(W2.at[2 + c], 2 * hi * S8, 2 * S8)
    gb = send(part, part, g2s.at[4 + M], g2r.at[4 + M], hi_dev)
    ga.wait_recv()
    part = lanes(G1, 4 * c * K8, K2)
    ga = send(part, part, g1s.at[4, 2], g1r.at[4, 2], core_dev)
    gb.wait_recv()
    part = rows(W2.at[2 + c], 0, 4 * S8)
    gb = send(part, part, g2s.at[5 + M], g2r.at[5 + M], core_dev)
    for cp in cps4z:
        cp.wait_recv()
    v = ar4z[0]
    for b in range(1, M):
        v = v + ar4z[b]
    vec_ref[0:1, :] = v[0:1]
    ga.wait_recv()
    gw1_copy = pltpu.make_async_copy(G1, gw1_ref, loc.at[1])
    gw1_copy.start()
    gb.wait_recv()
    top = min(4 * S8, U)
    for b in range(M):
        slo2[0:top, b * U : (b + 1) * U] = W2[2, 0:top, b * LP : b * LP + U]
        if U > top:
            slo2[top:U, b * U : (b + 1) * U] = W2[3, 0 : U - top, b * LP : b * LP + U]
    gw2_copy = pltpu.make_async_copy(lanes(slo2, 0, gw2_ref.shape[1]), gw2_ref, loc.at[2])
    gw2_copy.start()
    out_copy.wait()
    gw1_copy.wait()
    gw2_copy.wait()
    for cp in sent:
        cp.wait_send()


def per_device(ids, hash_mult, hash_add, w1, b1, s1, t1, w2, b2, s2, t2, cot):
    D, M = lax.axis_size("dp"), lax.axis_size("mp")
    U, K = w1.shape
    R = ids.shape[0]
    Q = R // M
    LP = -(-U // 128) * 128
    G = D // 8
    par = jnp.pad(jnp.stack([b1, s1, t1, b2, s2, t2]), ((0, 2), (0, LP - U)))
    zeros = jnp.zeros((U, LP - U), BF16)
    pieces = []
    for b in range(M):
        pieces += [w2[:, b * U : (b + 1) * U], zeros]
    w2p = jnp.concatenate(pieces, axis=1)
    dma = pltpu.SemaphoreType.DMA
    vmem = pl.BlockSpec(memory_space=pltpu.VMEM)
    hbm = pl.BlockSpec(memory_space=pl.ANY)
    AR = -(-2 * M // 8) * 8
    scratch = [
        pltpu.VMEM((M, K, Q), BF16),
        pltpu.VMEM((M * LP, R), BF16),
        pltpu.VMEM((M, U, max(K, Q)), BF16),
        pltpu.VMEM((M, U, M * LP), BF16),
        pltpu.VMEM((LP, M * LP), BF16),
        pltpu.VMEM((M, U, max(K, Q)), BF16),
        pltpu.VMEM((M, U, Q), BF16),
        pltpu.VMEM((U, R), BF16),
        pltpu.VMEM((U, R), BF16),
        pltpu.VMEM((U, K), BF16),
        pltpu.VMEM((M, LP, 128), F32),
        pltpu.VMEM((M, 32, LP), F32),
        pltpu.VMEM((4, LP, 128), F32),
        pltpu.VMEM((LP, LP), F32),
        pltpu.VMEM((K, 128), F32),
        pltpu.VMEM((M, 8, LP), F32),
        pltpu.VMEM((D, AR, LP), F32),
        pltpu.VMEM((D, 8, LP), F32),
        pltpu.VMEM((M, 8, LP), F32),
        pltpu.VMEM((D, AR + 8, LP), F32),
        pltpu.VMEM((M, AR, LP), F32),
        pltpu.VMEM((D, 8, LP), F32),
        pltpu.VMEM((M, 8, LP), F32),
        pltpu.VMEM((M, 8, LP), F32),
        dma((4, M)), dma((4, M)), dma((4, M)), dma((4, M)),
        dma((M,)), dma((M,)), dma((M,)), dma((M,)), dma((3 + M,)),
        dma((D,)), dma((D,)), dma((D,)), dma((D,)), dma((M,)), dma((M,)),
        dma((D,)), dma((D,)), dma((M,)), dma((M,)), dma((D,)), dma((D,)), dma((M,)), dma((M,)),
        dma((5, M)), dma((5, M)), dma((6 + M,)), dma((6 + M,)),
    ]
    if G > 1:
        scratch += [
            pltpu.VMEM((G, M, U, K // 8), BF16),
            pltpu.VMEM((G, LP // 8, M * LP), BF16),
            dma((G, M)), dma((G, M)), dma((G,)), dma((G,)),
        ]
    out, gw1, gw2, vec = pl.pallas_call(
        functools.partial(kernel, D, M, U, LP, K, R),
        out_shape=[
            jax.ShapeDtypeStruct((U, R), BF16),
            jax.ShapeDtypeStruct((U, K), BF16),
            jax.ShapeDtypeStruct((U, -(-M * U // 128) * 128), BF16),
            jax.ShapeDtypeStruct((8, LP), F32),
        ],
        in_specs=[vmem] * 4 + [hbm] * 3,
        out_specs=[hbm, hbm, hbm, vmem],
        scratch_shapes=scratch,
        compiler_params=pltpu.CompilerParams(
            collective_id=0, has_side_effects=True, vmem_limit_bytes=64 * 2**20 - 2**18
        ),
    )(ids[None, :], hash_mult[None, :], hash_add[None, :], par, w1, w2p, cot)
    v = vec[:, :U]
    return (out, gw1.astype(F32), v[0], v[1], v[2], gw2[:, : M * U].astype(F32), v[3], v[4], v[5])


def solution(mesh):
    return jax.shard_map(
        per_device,
        mesh=mesh,
        in_specs=(
            P("dp"), P(), P(), P("mp", None), P("mp"), P("mp"), P("mp"),
            P("mp", None), P("mp"), P("mp"), P("mp"), P("mp", "dp"),
        ),
        out_specs=(
            P("mp", "dp"), P("mp", None), P("mp"), P("mp"), P("mp"),
            P("mp", None), P("mp"), P("mp"), P("mp"),
        ),
        check_vma=False,
    )
```

```python
import functools

import jax
import jax.numpy as jnp
from jax import lax
from jax.experimental import pallas as pl
from jax.experimental.pallas import tpu as pltpu
from jax.sharding import PartitionSpec as P

MESH = pl.DeviceIdType.MESH
F32, BF16, I32 = jnp.float32, jnp.bfloat16, jnp.int32
epsilon = 1e-05


def dot(a, b):
    return lax.dot_general(a, b, (((1,), (0,)), ((), ())), preferred_element_type=F32)


def dot_nt(a, b):
    return lax.dot_general(a, b, (((1,), (1,)), ((), ())), preferred_element_type=F32)


def mish_parts(v):
    u = jnp.exp(jnp.minimum(v, 20.0))
    n = u * (u + 2.0)
    d = n + 2.0
    r = pl.reciprocal(d, approx=True)
    r = r * (2.0 - d * r)
    t = n * r
    return v * t, t + v * ((4.0 * (n - u) * r) * r)


def mish(v):
    u = jnp.exp(jnp.minimum(v, 20.0))
    n = u * (u + 2.0)
    d = n + 2.0
    r = pl.reciprocal(d, approx=True)
    r = r * (2.0 - d * r)
    return v * (n * r)


def lane_part(x):
    out = x[:, :128]
    for at in range(128, x.shape[1], 128):
        out = out + x[:, at : at + 128]
    return out


def kernel(
    D, M, U, LP, K, R,
    ids_ref, mult_ref, add_ref, par_ref, w1_ref, w2_ref, cot_ref,
    out_ref, gw1_ref, gw2_ref, vec_ref,
    A, B, C, W2, E1, F, H, act2, slo2, G1, col, RW, acc, T, hcol,
    pv, ar1, ar2, ar2z, ar3, ar3z, ar4, ar4s, ar4z,
    w1s, w1r, w2s, w2r, pvs, pvr, cts, ctr, loc,
    a1s, a1r, a2s, a2r, a2zs, a2zr, a3s, a3r, a3zs, a3zr, a4s, a4r, a4zs, a4zr,
    g1s, g1r, g2s, g2r, free, *extra,
):
    Q = R // M
    G = D // 8
    TL = min(512, Q)
    NT = Q // TL
    PER = K // LP
    NA = M // PER
    K8 = K // 8
    J8 = M * LP // 8
    S8 = LP // 8
    N = float(R * D)
    d = lax.axis_index("dp")
    m = lax.axis_index("mp")
    i = lax.rem(d, 8)
    c = lax.rem(i, 2)
    x = lax.rem(i // 2, 2)
    y = i // 4
    hi = (1 - c) * x + c * y
    lo = (1 - c) * y + c * x
    p = 4 * c + 2 * hi + lo
    core_dev = (d + 1 - 2 * c, m)
    flip_x = d + 2 - 4 * x
    flip_y = d + 4 - 8 * y
    hi_dev = ((1 - c) * flip_x + c * flip_y, m)
    lo_dev = ((1 - c) * flip_y + c * flip_x, m)
    up = [lax.rem(m + k, M) for k in range(M)]
    down = [lax.rem(m - k + M, M) for k in range(M)]
    others = [lax.rem(d + k, D) for k in range(D)]
    sent = []

    def remote(src, dst, ss, rs, dev):
        cp = pltpu.make_async_remote_copy(
            src_ref=src, dst_ref=dst, send_sem=ss, recv_sem=rs, device_id=dev, device_id_type=MESH
        )
        return cp

    def send(src, dst, ss, rs, dev):
        cp = remote(src, dst, ss, rs, dev)
        cp.start()
        sent.append(cp)
        return cp

    def gone(cp):
        cp.wait_send()
        sent[:] = [other for other in sent if other is not cp]

    def lanes(ref, at, size):
        return ref.at[:, pl.ds(pl.multiple_of(at, 128), size)]

    def rows(ref, at, size):
        return ref.at[pl.ds(pl.multiple_of(at, 16), size)]

    bar = pltpu.get_barrier_semaphore()
    for k in range(1, D):
        pl.semaphore_signal(bar, inc=1, device_id=(others[k], m), device_id_type=MESH)
    for k in range(1, M):
        pl.semaphore_signal(bar, inc=1, device_id=(d, up[k]), device_id_type=MESH)

    w1_loc = pltpu.make_async_copy(w1_ref, C.at[m], loc.at[0])
    w1_loc.start()
    cot_loc = pltpu.make_async_copy(lanes(cot_ref, m * Q, Q), lanes(F.at[m], 0, Q), loc.at[2])
    cot_loc.start()
    pv[m] = par_ref[...]
    for b in range(M):
        W2[m, :, (b + 1) * LP - 128 : (b + 1) * LP] = jnp.zeros((U, 128), BF16)
        W2[m, :, b * LP : b * LP + U] = w2_ref[:, b * U : (b + 1) * U]
    pl.semaphore_wait(bar, D - 1 + M - 1)

    ag1, ag2, agp, ct = {}, {}, {}, {}
    for k in range(1, M):
        agp[k] = send(par_ref, pv.at[m], pvs.at[k], pvr.at[k], (d, up[k]))
    for k in range(1, M):
        ag1[0, k] = send(
            lanes(w1_ref, p * K8, K8), lanes(C.at[m], p * K8, K8), w1s.at[0, k], w1r.at[0, k], (d, up[k])
        )
    for k in range(1, M):
        ag2[0, k] = send(
            lanes(W2.at[m], p * J8, J8), lanes(W2.at[m], p * J8, J8), w2s.at[0, k], w2r.at[0, k], (d, up[k])
        )

    def gather_stage(step, ag, buf, size, ss, rs):
        dev, at, width = {
            1: (lo_dev, p * size, size),
            2: (hi_dev, (4 * c + 2 * hi) * size, 2 * size),
            3: (core_dev, 4 * c * size, 4 * size),
        }[step]
        for k in range(1, M):
            ag[step - 1, k].wait_recv()
            part = lanes(buf.at[down[k]], at, width)
            ag[step, k] = send(part, part, ss.at[step, k], rs.at[step, k], dev)

    def stage1(step):
        gather_stage(step, ag1, C, K8, w1s, w1r)

    def stage2(step):
        gather_stage(step, ag2, W2, J8, w2s, w2r)

    hrow = jnp.concatenate(
        [mult_ref[...].astype(F32), add_ref[...].astype(F32), jnp.zeros((126, K), F32)], axis=0
    )
    hcol[...] = hrow.T

    HT = 128

    def encode(q, put):
        def step(t, _):
            at = pl.multiple_of(t * HT, HT)
            both = hcol[pl.ds(at, HT), :].astype(I32)
            v = both[:, 0:1] * ids_ref[:, pl.ds(pl.multiple_of(q * Q, 128), Q)] + both[:, 1:2]
            for _ in range(2):
                top = lax.shift_right_logical(v, 16)
                v = (v & 65535) + ((top << 4) - top)
            v = jnp.where(v >= 65521, v - 65521, v)
            put(t, (v.astype(F32) * (2.0 / 65520.0) - 1.0).astype(BF16))
            return 0

        lax.fori_loop(0, K // HT, step, 0)

    def make_col(b):
        col[b] = jnp.concatenate([RW[b], jnp.zeros((128 - RW.shape[1], LP), F32)], axis=0).T

    def make_cols():
        def step(b, _):
            make_col(b)
            return 0

        lax.fori_loop(0, M, step, 0)

    def to_a(q):
        def put(t, value):
            A[q, pl.ds(pl.multiple_of(t * HT, HT), HT), :] = value

        return put

    def to_e1(t, value):
        E1[pl.ds(pl.multiple_of(lax.rem(t, LP // HT) * HT, HT), HT), pl.ds(pl.multiple_of(t // (LP // HT) * Q, 128), Q)] = value

    def row_of(slot):
        return jnp.sum(acc[slot].T, axis=0, keepdims=True)

    acc[...] = jnp.zeros_like(acc)
    for b in range(M):
        B[pl.ds(b * LP + U // 16 * 16, LP - U // 16 * 16), :] = jnp.zeros((LP - U // 16 * 16, R), BF16)

    RW[...] = jnp.zeros_like(RW)
    RW[m, 0:8] = par_ref[...]
    make_col(m)
    encode(m, to_a(m))
    w1_loc.wait()

    def mm1_own(b):
        def step(t, _):
            at = pl.multiple_of(t * TL, TL)
            v = dot(C[b], A[m, :, pl.ds(at, TL)]) + col[b, :U, 0:1]
            act, slope = mish_parts(v)
            H[b, :, pl.ds(at, TL)] = slope.astype(BF16)
            B[pl.ds(pl.multiple_of(b * LP, LP), U), pl.ds(pl.multiple_of(m * Q + t * TL, TL), TL)] = act.astype(BF16)
            acc[0, :U] += lane_part(act)
            acc[1, :U] += lane_part(act * act)
            return 0

        lax.fori_loop(0, NT, step, 0)

    def mm1_rest(b):
        def step(t, _):
            q = lax.rem(m + 1 + t // NT, M)
            at = pl.multiple_of(lax.rem(t, NT) * TL, TL)
            act = mish(dot(C[b], A[q, :, pl.ds(at, TL)]) + col[b, :U, 0:1])
            B[pl.ds(pl.multiple_of(b * LP, LP), U), pl.ds(pl.multiple_of(q * Q + at, TL), TL)] = act.astype(BF16)
            acc[0, :U] += lane_part(act)
            acc[1, :U] += lane_part(act * act)
            return 0

        lax.fori_loop(0, (M - 1) * NT, step, 0)

    def mm1_sums(b):
        ar1[d, pl.ds(b, 1), :] = row_of(0)
        ar1[d, pl.ds(b + M, 1), :] = row_of(1)
        acc[0:2] = jnp.zeros((2, LP, 128), F32)

    mm1_own(m)
    stage1(1)

    def enc_step(k, _):
        q = lax.rem(m + M - k, M)
        encode(q, to_a(q))
        return 0

    lax.fori_loop(1, M, enc_step, 0)
    stage1(2)
    mm1_rest(m)
    mm1_sums(m)
    stage1(3)
    stage2(1)
    for k in range(1, M):
        ct[k] = send(lanes(cot_ref, up[k] * Q, Q), lanes(F.at[m], 0, Q), cts.at[k], ctr.at[k], (d, up[k]))
    for k in range(1, M):
        agp[k].wait_recv()
    for b in range(M):
        RW[b, 0:8] = pv[b]
    make_cols()
    for k in range(1, M):
        ag1[3, k].wait_recv()
        mm1_own(down[k])
        mm1_rest(down[k])
        mm1_sums(down[k])
        if k == 1:
            stage2(2)

    def all_dp(buf, ss, rs):
        cps = []
        for k in range(1, D):
            cps.append(send(buf.at[d], buf.at[d], ss.at[k], rs.at[k], (others[k], m)))
        return cps

    def total(buf, cps):
        for cp in cps:
            cp.wait_recv()
        out = buf[0]
        for k in range(1, D):
            out = out + buf[k]
        return out

    cps1 = all_dp(ar1, a1s, a1r)
    stage2(3)
    for step in range(1, 4):
        for k in range(1, M):
            gone(ag1[step, k])
    cot_all = []
    for q in range(M):
        cp = pltpu.make_async_copy(lanes(cot_ref, q * Q, Q), lanes(C.at[q], 0, Q), loc.at[3 + q])
        cot_all.append(cp)
        cp.start()
    for k in range(1, M):
        ag2[3, k].wait_recv()

    T[...] = jnp.zeros_like(T)

    def make_e1(b):
        def step(h, _):
            T[:U, :] = W2[h, :, pl.ds(pl.multiple_of(b * LP, LP), LP)].astype(F32) * col[h, :U, 1:2]
            E1[:, pl.ds(pl.multiple_of(h * LP, LP), LP)] = T[...].T.astype(BF16)
            return 0

        lax.fori_loop(0, M, step, 0)

    const = jnp.zeros((8, M * LP), F32)
    for b in range(M):
        shift = jnp.broadcast_to(pv[b, 2:3, :U], (8, U))
        upper = shift.astype(BF16)
        lower = (shift - upper.astype(F32)).astype(BF16)
        const = const + dot(upper, W2[b]) + dot(lower, W2[b])
    for b in range(M):
        RW[b, 8:9] = const[0:1, b * LP : (b + 1) * LP] + pv[b, 3:4]
    make_e1(m)

    tot = total(ar1, cps1)
    mean = tot[:M] / N
    inv = lax.rsqrt(tot[M:] / N - mean * mean + epsilon)
    for b in range(M):
        RW[b, 9:10] = inv[b : b + 1]
        RW[b, 10:11] = -mean[b : b + 1] * inv[b : b + 1]
    make_cols()
    for cp in cot_all:
        cp.wait()

    def mm2(t, _):
        at = pl.multiple_of(t * TL, TL)
        for b in range(M):
            part = B[b * LP : b * LP + U, pl.ds(at, TL)].astype(F32)
            B[b * LP : b * LP + U, pl.ds(at, TL)] = (part * col[b, :U, 9:10] + col[b, :U, 10:11]).astype(BF16)
        v = dot(E1[:U], B[:, pl.ds(at, TL)]) + col[m, :U, 8:9]
        act, slope = mish_parts(v)
        act2[:, pl.ds(at, TL)] = act.astype(BF16)
        slo2[:, pl.ds(at, TL)] = slope.astype(BF16)
        g = C[t // NT, :, pl.ds(pl.multiple_of(lax.rem(t, NT) * TL, TL), TL)].astype(F32)
        acc[0, :U] += lane_part(act)
        acc[1, :U] += lane_part(act * act)
        acc[2, :U] += lane_part(g)
        acc[3, :U] += lane_part(g * act)
        return 0

    lax.fori_loop(0, M * NT, mm2, 0)
    for s in range(4):
        ar2[d, s : s + 1, :] = row_of(s)
    ar2[d, 4:8, :] = jnp.zeros((4, LP), F32)
    acc[...] = jnp.zeros_like(acc)
    cps2 = all_dp(ar2, a2s, a2r)

    def a_at(base, b):
        return base + b // PER, pl.multiple_of(lax.rem(b, PER) * LP, LP)

    def mm2_own(b):
        make_e1(b)
        act_at, row = a_at(0, b)

        def step(t, _):
            at = pl.multiple_of(t * TL, TL)
            v = dot(E1[:U], B[:, pl.ds(pl.multiple_of(m * Q + t * TL, TL), TL)]) + col[b, :U, 8:9]
            act, slope = mish_parts(v)
            A[act_at, pl.ds(row, U), pl.ds(at, TL)] = act.astype(BF16)
            A[act_at + NA, pl.ds(row, U), pl.ds(at, TL)] = slope.astype(BF16)
            return 0

        lax.fori_loop(0, NT, step, 0)

    def own_loop(k, _):
        mm2_own(lax.rem(m + k, M))
        return 0

    mm2_own(up[1])
    tot = total(ar2, cps2)
    mean = tot[0:1] / N
    inv = lax.rsqrt(tot[1:2] / N - mean * mean + epsilon)
    sum_g = tot[2:3]
    sum_gn = inv * (tot[3:4] - mean * sum_g)
    k1 = pv[m, 4:5] * inv
    k2 = -k1 * inv * sum_gn / N
    k3 = -k1 * sum_g / N - mean * k2
    ar2z[m, 0:1] = k1
    ar2z[m, 1:2] = k2
    ar2z[m, 2:3] = k3
    ar2z[m, 3:4] = k1
    ar2z[m, 4:5] = pv[m, 5:6] - mean * k1
    ar2z[m, 5:6] = sum_g
    ar2z[m, 6:7] = sum_gn
    ar2z[m, 7:8] = jnp.zeros((1, LP), F32)
    cps2z = [send(ar2z.at[m], ar2z.at[m], a2zs.at[k], a2zr.at[k], (d, up[k])) for k in range(1, M)]
    RW[m, 16:24] = ar2z[m]
    make_col(m)

    def back2(t, _):
        at = pl.multiple_of(t * TL, TL)
        a = act2[:, pl.ds(at, TL)].astype(F32)
        g = C[t // NT, :, pl.ds(pl.multiple_of(lax.rem(t, NT) * TL, TL), TL)].astype(F32)
        act2[:, pl.ds(at, TL)] = (a * col[m, :U, 19:20] + col[m, :U, 20:21]).astype(BF16)
        grad = (g * col[m, :U, 16:17] + a * col[m, :U, 17:18] + col[m, :U, 18:19]) * slo2[:, pl.ds(at, TL)].astype(F32)
        grad = grad.astype(BF16)
        slo2[:, pl.ds(at, TL)] = grad
        acc[0, :U] += lane_part(grad.astype(F32))
        return 0

    lax.fori_loop(0, M * NT, back2, 0)
    out_copy = pltpu.make_async_copy(act2, out_ref, loc.at[0])
    out_copy.start()
    gb2 = row_of(0)
    ar3[d, 2 * M : 2 * M + 1, :] = gb2
    ar3[d, 2 * M + 1 : 2 * M + 8, :] = jnp.zeros((7, LP), F32)
    acc[0:1] = jnp.zeros((1, LP, 128), F32)

    L1 = pl.multiple_of(lax.rem(m + 1, M) * Q, 128)
    LR = pl.multiple_of(L1 + LP, 128)

    def rowsum(x):
        acc[0, :U] = lane_part(x[:, : U // 128 * 128]) + jnp.where(
            lax.broadcasted_iota(I32, (U, 128), 1) >= 128 - U % 128, x[:, U - 128 :], 0.0
        )
        return row_of(0)

    def grad_w2(b, _):
        at = pl.multiple_of(b * LP, LP)
        g = dot_nt(B[pl.ds(at, LP), :], slo2[...])
        w = W2[b, :, pl.ds(pl.multiple_of(m * LP, LP), LP)].astype(F32)[:, :U]
        ar3[d, pl.ds(b, 1), :] = rowsum(w * gb2[:, :U])
        ar3[d, pl.ds(b + M, 1), :] = rowsum(w * g[:U])
        g = g * col[b, :, 1:2] + col[b, :, 2:3] * gb2[:, :U]
        B[pl.ds(at, LP), pl.ds(L1, U)] = g.astype(BF16)
        B[pl.ds(at, LP), pl.ds(L1 + U // 128 * 128, LP - U // 128 * 128)] = jnp.where(
            lax.broadcasted_iota(I32, (LP, LP - U // 128 * 128), 1) < U - U // 128 * 128,
            B[pl.ds(at, LP), pl.ds(L1 + U // 128 * 128, LP - U // 128 * 128)].astype(F32),
            0.0,
        ).astype(BF16)
        return 0

    lax.fori_loop(0, M, grad_w2, 0)
    cps3 = all_dp(ar3, a3s, a3r)
    for n, dev in ((0, core_dev), (1, hi_dev), (2, lo_dev)):
        pl.semaphore_signal(free.at[n], inc=1, device_id=dev, device_id_type=MESH)
    for k in range(1, M):
        pl.semaphore_signal(free.at[2 + k], inc=1, device_id=(d, up[k]), device_id_type=MESH)

    HALF = {0: (1 - c) * 4, 1: 4 * c + 2 * (1 - hi), 2: 4 * c + 2 * hi + 1 - lo}
    KEEP = {0: 4 * c, 1: 4 * c + 2 * hi, 2: p}
    START = {0: 0, 1: 4, 2: 6}
    PARTNER = {0: core_dev, 1: hi_dev, 2: lo_dev}
    g2cp = {}

    def b_rows(b, at, size, lane):
        return B.at[pl.ds(pl.multiple_of(b * LP + at * S8, 16), size * S8), pl.ds(lane, LP)]

    def g2_send(n):
        pl.semaphore_wait(free.at[n], 1)
        for b in range(M):
            g2cp[n, b] = send(
                b_rows(b, HALF[n], 4 >> n, L1), b_rows(b, START[n], 4 >> n, LR), g2s.at[n, b], g2r.at[n, b], PARTNER[n]
            )

    def g2_add(n):
        for b in range(M):
            g2cp[n, b].wait_recv()
            size = (4 >> n) * S8
            keep = pl.ds(pl.multiple_of(b * LP + KEEP[n] * S8, 16), size)
            came = pl.ds(b * LP + START[n] * S8, size)
            B[keep, pl.ds(L1, LP)] = (
                B[keep, pl.ds(L1, LP)].astype(F32) + B[came, pl.ds(LR, LP)].astype(F32)
            ).astype(BF16)

    def l2_of(z):
        return pl.multiple_of(lax.rem(z + 2, M) * Q, 128)

    L2 = l2_of(m)

    if G > 1:
        x1, x2, x1s, x1r, x2s, x2r = extra

    def g2_groups():
        cps = []
        for k in range(1, G):
            to = (lax.rem(d + 8 * k, D), m)
            for b in range(M):
                cps.append(send(b_rows(b, p, 1, L1), x2.at[d // 8, b], x2s.at[k, b], x2r.at[k, b], to))
        for b in range(M):
            x2[d // 8, b] = B[pl.ds(pl.multiple_of(b * LP + p * S8, 16), S8), pl.ds(L1, LP)]
        for cp in cps:
            cp.wait_recv()
        for cp in cps:
            gone(cp)
        for b in range(M):
            v = x2[0, b].astype(F32)
            for k in range(1, G):
                v = v + x2[k, b].astype(F32)
            B[pl.ds(pl.multiple_of(b * LP + p * S8, 16), S8), pl.ds(L1, LP)] = v.astype(BF16)

    def g2_z():
        if G > 1:
            g2_groups()
        for k in range(1, M):
            pl.semaphore_wait(free.at[2 + M - k], 1)
            g2cp[3, k] = send(
                b_rows(up[k], p, 1, L1),
                B.at[pl.ds(pl.multiple_of(m * LP + p * S8, 16), S8), pl.ds(l2_of(up[k]), LP)],
                g2s.at[3, k], g2r.at[3, k], (d, up[k]),
            )
        mine = pl.ds(pl.multiple_of(m * LP + p * S8, 16), S8)
        B[mine, pl.ds(L2, LP)] = B[mine, pl.ds(L1, LP)]

    def g2_gather(n):
        at, size, dev = {4: (p, 1, lo_dev), 5: (4 * c + 2 * hi, 2, hi_dev), 6: (4 * c, 4, core_dev)}[n]
        if n == 4:
            for k in range(1, M):
                g2cp[3, k].wait_recv()
        else:
            for b in range(M):
                g2cp[n - 1, b].wait_recv()
        for b in range(M):
            part = b_rows(b, at, size, L2)
            g2cp[n, b] = send(part, part, g2s.at[n, b], g2r.at[n, b], dev)

    g2_send(0)
    lax.fori_loop(2, M, own_loop, 0)
    tot = total(ar3, cps3)
    ar3z[m] = tot[: 2 * M]
    gb2_all = tot[2 * M : 2 * M + 1]
    cps3z = [send(ar3z.at[m], ar3z.at[m], a3zs.at[k], a3zr.at[k], (d, up[k])) for k in range(1, M)]
    g2_add(0)
    g2_send(1)
    encode(m, to_e1)
    for cp in cps2z:
        cp.wait_recv()
    for b in range(M):
        RW[b, 16:24] = ar2z[b]
    for cp in cps3z:
        cp.wait_recv()
    tot = ar3z[0]
    for b in range(1, M):
        tot = tot + ar3z[b]
    for b in range(M):
        k1 = pv[b, 1:2] * RW[b, 9:10]
        RW[b, 24:25] = k1
        RW[b, 25:26] = -k1 * tot[M + b : M + b + 1] / N
        RW[b, 26:27] = -k1 * tot[b : b + 1] / N
    make_cols()
    pick = lax.broadcasted_iota(I32, (2 * M, 1), 0)
    vec_ref[0:1, :] = jnp.zeros((1, LP), F32)
    vec_ref[1:2, :] = jnp.sum(jnp.where(pick == M + m, tot, 0.0), axis=0, keepdims=True)
    vec_ref[2:3, :] = jnp.sum(jnp.where(pick == m, tot, 0.0), axis=0, keepdims=True)
    vec_ref[3:4, :] = gb2_all
    vec_ref[4:5, :] = ar2z[m, 6:7]
    vec_ref[5:6, :] = ar2z[m, 5:6]
    vec_ref[6:8, :] = jnp.zeros((2, LP), F32)

    PADAT = U // 16 * 16

    def put_grad(b, value, at, size):
        slot, row = a_at(NA, b)
        A[slot, pl.ds(row, U), pl.ds(at, size)] = value

    for b in range(M):
        slot, row = NA + b // PER, (b % PER) * LP
        A[slot, row + PADAT : row + LP, :] = jnp.where(
            lax.broadcasted_iota(I32, (LP - PADAT, Q), 0) < U - PADAT,
            A[slot, row + PADAT : row + LP, :].astype(F32),
            0.0,
        ).astype(BF16)
    cot_loc.wait()

    def back2_own(b):
        act_at, row = a_at(0, b)

        def step(t, _):
            at = pl.multiple_of(t * TL, TL)
            a = A[act_at, pl.ds(row, U), pl.ds(at, TL)].astype(F32)
            s = A[act_at + NA, pl.ds(row, U), pl.ds(at, TL)].astype(F32)
            g = F[b, :, pl.ds(at, TL)].astype(F32)
            grad = (g * col[b, :U, 16:17] + a * col[b, :U, 17:18] + col[b, :U, 18:19]) * s
            A[act_at + NA, pl.ds(row, U), pl.ds(at, TL)] = grad.astype(BF16)
            return 0

        lax.fori_loop(0, NT, step, 0)

    def copy_own(t, _):
        at = pl.multiple_of(t * TL, TL)
        put_grad(m, slo2[:, pl.ds(pl.multiple_of(m * Q + t * TL, TL), TL)], at, TL)
        return 0

    lax.fori_loop(0, NT, copy_own, 0)
    for k in range(1, M):
        ct[k].wait_recv()
        back2_own(down[k])

    g2_add(1)
    g2_send(2)

    def back1(b):
        def step(t, _):
            at = pl.multiple_of(t * TL, TL)
            dh = dot(W2[b, :, 0:K], A[NA, :, pl.ds(at, TL)])
            for n in range(1, NA):
                dh = dh + dot(W2[b, :, n * K : (n + 1) * K], A[NA + n, :, pl.ds(at, TL)])
            norm = B[pl.ds(pl.multiple_of(b * LP, LP), U), pl.ds(pl.multiple_of(m * Q + t * TL, TL), TL)].astype(F32)
            grad = dh * col[b, :U, 24:25] + norm * col[b, :U, 25:26] + col[b, :U, 26:27]
            grad = (grad * H[b, :, pl.ds(at, TL)].astype(F32)).astype(BF16)
            H[b, :, pl.ds(at, TL)] = grad
            acc[0, :U] += lane_part(grad.astype(F32))
            return 0

        lax.fori_loop(0, NT, step, 0)
        ar4[d, pl.ds(b, 1), :] = row_of(0)
        acc[0:1] = jnp.zeros((1, LP, 128), F32)

        def mm(t, _):
            F[b, :, pl.ds(pl.multiple_of(t * LP, LP), LP)] = dot_nt(
                H[b], E1[:, pl.ds(pl.multiple_of(t * Q, Q), Q)]
            ).astype(BF16)
            return 0

        lax.fori_loop(0, PER, mm, 0)

    acc[0:1] = jnp.zeros((1, LP, 128), F32)
    ar4[d] = jnp.zeros((ar4.shape[1], LP), F32)
    K2 = 4 * K8
    FROM = {0: 0, 1: K2, 2: K2 + 2 * K8}
    order = [up[(j + 1) % M] for j in range(M)]
    g1cp = {}

    def g1_send(n, j):
        b = order[j]
        g1cp[n, j] = send(
            lanes(F.at[b], HALF[n] * K8, K2 >> n), lanes(C.at[b], FROM[n], K2 >> n), g1s.at[n, j], g1r.at[n, j], PARTNER[n]
        )

    def g1_add(n, j):
        b = order[j]
        g1cp[n, j].wait_recv()
        keep = pl.ds(pl.multiple_of(KEEP[n] * K8, 128), K2 >> n)
        F[b, :, keep] = (F[b, :, keep].astype(F32) + C[b, :, FROM[n] : FROM[n] + (K2 >> n)].astype(F32)).astype(BF16)

    def g1_groups(j):
        b = order[j]
        mine = pl.ds(pl.multiple_of(p * K8, 128), K8)
        cps = []
        for k in range(1, G):
            to = (lax.rem(d + 8 * k, D), m)
            cps.append(send(lanes(F.at[b], p * K8, K8), x1.at[d // 8, j], x1s.at[k, j], x1r.at[k, j], to))
        x1[d // 8, j] = F[b, :, mine]
        for cp in cps:
            cp.wait_recv()
        for cp in cps:
            gone(cp)
        v = x1[0, j].astype(F32)
        for k in range(1, G):
            v = v + x1[k, j].astype(F32)
        F[b, :, mine] = v.astype(BF16)

    def g1_z(j):
        if G > 1:
            g1_groups(j)
        b, k = order[j], (j + 1) % M
        if k:
            g1cp[3, j] = send(
                lanes(F.at[b], p * K8, K8), C.at[m, :, pl.ds(K - K8, K8)], g1s.at[3, k], g1r.at[3, k], (d, b)
            )
        else:
            C[m, :, K - K8 : K] = F[m, :, pl.ds(pl.multiple_of(p * K8, 128), K8)]

    def g1_stage(n, j):
        if 0 <= j < M:
            g1_add(n - 1, j)
            if n < 3:
                g1_send(n, j)
            else:
                g1_z(j)

    for j in range(M + 3):
        if j < M:
            back1(order[j])
            g1_send(0, j)
        if j == M - 1:
            cps4 = all_dp(ar4, a4s, a4r)
        g1_stage(3, j - 3)
        g1_stage(2, j - 2)
        g1_stage(1, j - 1)
        if j == 0:
            g2_add(2)
            g2_z()
        if j == 1:
            g2_gather(4)
        if j == 2:
            g2_gather(5)
        if j == 3:
            g2_gather(6)
        if j == M:
            tot4 = total(ar4, cps4)
            for b in range(M):
                ar4s[b] = jnp.broadcast_to(tot4[b : b + 1], (8, LP))
            ar4z[m] = ar4s[m]
            cps4z = [send(ar4s.at[up[k]], ar4z.at[m], a4zs.at[k], a4zr.at[k], (d, up[k])) for k in range(1, M)]
    for b in range(M):
        g2cp[6, b].wait_recv()
    for b in range(M):
        slo2[:, b * U : (b + 1) * U] = B[b * LP : b * LP + U, pl.ds(L2, LP)][:, :U]
    gw2_copy = pltpu.make_async_copy(lanes(slo2, 0, gw2_ref.shape[1]), gw2_ref, loc.at[2])
    gw2_copy.start()
    for j in range(M - 1):
        g1cp[3, j].wait_recv()
    v = C[0, :, K - K8 : K].astype(F32)
    for b in range(1, M):
        v = v + C[b, :, K - K8 : K].astype(F32)
    G1[:, pl.ds(pl.multiple_of(p * K8, 128), K8)] = v.astype(BF16)
    ga = send(lanes(G1, p * K8, K8), lanes(G1, p * K8, K8), g1s.at[4, 0], g1r.at[4, 0], lo_dev)
    ga.wait_recv()
    part = lanes(G1, (4 * c + 2 * hi) * K8, 2 * K8)
    ga = send(part, part, g1s.at[4, 1], g1r.at[4, 1], hi_dev)
    ga.wait_recv()
    part = lanes(G1, 4 * c * K8, K2)
    ga = send(part, part, g1s.at[4, 2], g1r.at[4, 2], core_dev)
    for cp in cps4z:
        cp.wait_recv()
    v = ar4z[0]
    for b in range(1, M):
        v = v + ar4z[b]
    vec_ref[0:1, :] = v[0:1]
    ga.wait_recv()
    gw1_copy = pltpu.make_async_copy(G1, gw1_ref, loc.at[1])
    gw1_copy.start()
    out_copy.wait()
    gw1_copy.wait()
    gw2_copy.wait()
    for cp in sent:
        cp.wait_send()


def per_device(ids, hash_mult, hash_add, w1, b1, s1, t1, w2, b2, s2, t2, cot):
    D, M = lax.axis_size("dp"), lax.axis_size("mp")
    U, K = w1.shape
    R = ids.shape[0]
    Q = R // M
    LP = -(-U // 128) * 128
    G = D // 8
    par = jnp.pad(jnp.stack([b1, s1, t1, b2, s2, t2]), ((0, 2), (0, LP - U)))
    dma = pltpu.SemaphoreType.DMA
    vmem = pl.BlockSpec(memory_space=pltpu.VMEM)
    hbm = pl.BlockSpec(memory_space=pl.ANY)
    AR = -(-2 * M // 8) * 8
    scratch = [
        pltpu.VMEM((M, K, Q), BF16),
        pltpu.VMEM((M * LP, R), BF16),
        pltpu.VMEM((M, U, max(K, Q)), BF16),
        pltpu.VMEM((M, U, M * LP), BF16),
        pltpu.VMEM((LP, M * LP), BF16),
        pltpu.VMEM((M, U, max(K, Q)), BF16),
        pltpu.VMEM((M, U, Q), BF16),
        pltpu.VMEM((U, R), BF16),
        pltpu.VMEM((U, R), BF16),
        pltpu.VMEM((U, K), BF16),
        pltpu.VMEM((M, LP, 128), F32),
        pltpu.VMEM((M, 32, LP), F32),
        pltpu.VMEM((4, LP, 128), F32),
        pltpu.VMEM((LP, LP), F32),
        pltpu.VMEM((K, 128), F32),
        pltpu.VMEM((M, 8, LP), F32),
        pltpu.VMEM((D, AR, LP), F32),
        pltpu.VMEM((D, 8, LP), F32),
        pltpu.VMEM((M, 8, LP), F32),
        pltpu.VMEM((D, AR + 8, LP), F32),
        pltpu.VMEM((M, AR, LP), F32),
        pltpu.VMEM((D, 8, LP), F32),
        pltpu.VMEM((M, 8, LP), F32),
        pltpu.VMEM((M, 8, LP), F32),
        dma((4, M)), dma((4, M)), dma((4, M)), dma((4, M)),
        dma((M,)), dma((M,)), dma((M,)), dma((M,)), dma((3 + M,)),
        dma((D,)), dma((D,)), dma((D,)), dma((D,)), dma((M,)), dma((M,)),
        dma((D,)), dma((D,)), dma((M,)), dma((M,)), dma((D,)), dma((D,)), dma((M,)), dma((M,)),
        dma((5, M)), dma((5, M)), dma((7, M)), dma((7, M)), pltpu.SemaphoreType.REGULAR((2 + M,)),
    ]
    if G > 1:
        scratch += [
            pltpu.VMEM((G, M, U, K // 8), BF16),
            pltpu.VMEM((G, M, LP // 8, LP), BF16),
            dma((G, M)), dma((G, M)), dma((G, M)), dma((G, M)),
        ]
    out, gw1, gw2, vec = pl.pallas_call(
        functools.partial(kernel, D, M, U, LP, K, R),
        out_shape=[
            jax.ShapeDtypeStruct((U, R), BF16),
            jax.ShapeDtypeStruct((U, K), BF16),
            jax.ShapeDtypeStruct((U, -(-M * U // 128) * 128), BF16),
            jax.ShapeDtypeStruct((8, LP), F32),
        ],
        in_specs=[vmem] * 4 + [hbm, vmem, hbm],
        out_specs=[hbm, hbm, hbm, vmem],
        scratch_shapes=scratch,
        compiler_params=pltpu.CompilerParams(
            collective_id=0, has_side_effects=True, vmem_limit_bytes=64 * 2**20 - 2**18
        ),
    )(ids[None, :], hash_mult[None, :], hash_add[None, :], par, w1, w2, cot)
    v = vec[:, :U]
    return (out, gw1.astype(F32), v[0], v[1], v[2], gw2[:, : M * U].astype(F32), v[3], v[4], v[5])


def solution(mesh):
    return jax.shard_map(
        per_device,
        mesh=mesh,
        in_specs=(
            P("dp"), P(), P(), P("mp", None), P("mp"), P("mp"), P("mp"),
            P("mp", None), P("mp"), P("mp"), P("mp"), P("mp", "dp"),
        ),
        out_specs=(
            P("mp", "dp"), P("mp", None), P("mp"), P("mp"), P("mp"),
            P("mp", None), P("mp"), P("mp"), P("mp"),
        ),
        check_vma=False,
    )
```

```python
import functools

import jax
import jax.numpy as jnp
from jax import lax
from jax.experimental import pallas as pl
from jax.experimental.pallas import tpu as pltpu
from jax.sharding import PartitionSpec as P

MESH = pl.DeviceIdType.MESH
F32, BF16, I32 = jnp.float32, jnp.bfloat16, jnp.int32
epsilon = 1e-05


def dot(a, b):
    return lax.dot_general(a, b, (((1,), (0,)), ((), ())), preferred_element_type=F32)


def dot_nt(a, b):
    return lax.dot_general(a, b, (((1,), (1,)), ((), ())), preferred_element_type=F32)


def mish_parts(v):
    u = jnp.exp(jnp.minimum(v, 20.0))
    n = u * (u + 2.0)
    d = n + 2.0
    r = pl.reciprocal(d, approx=True)
    t = n * r
    return v * t, t + v * ((4.0 * (n - u) * r) * r)


def mish(v):
    u = jnp.exp(jnp.minimum(v, 20.0))
    n = u * (u + 2.0)
    d = n + 2.0
    r = pl.reciprocal(d, approx=True)
    return v * (n * r)


def lane_part(x):
    out = x[:, :128]
    for at in range(128, x.shape[1], 128):
        out = out + x[:, at : at + 128]
    return out


def kernel(
    D, M, U, LP, K, R,
    ids_ref, mult_ref, add_ref, par_ref, w1_ref, w2_ref, cot_ref,
    out_ref, gw1_ref, gw2_ref, vec_ref,
    A, B, C, W2, G1, E1, F, H, act2, slo2, col, RW, acc, hcol,
    pv, ar1, ar2, ar2z, ar3, ar3z, ar4, ar4s, ar4z,
    w1s, w1r, w2s, w2r, pvs, pvr, cts, ctr, loc,
    a1s, a1r, a2s, a2r, a2zs, a2zr, a3s, a3r, a3zs, a3zr, a4s, a4r, a4zs, a4zr,
    g1s, g1r, g2s, g2r, free, *extra,
):
    Q = R // M
    G = D // 8
    TL = min(512, Q)
    NT = Q // TL
    PER = K // LP
    NA = M // PER
    K8 = K // 8
    J8 = M * LP // 8
    S8 = LP // 8
    N = float(R * D)
    d = lax.axis_index("dp")
    m = lax.axis_index("mp")
    i = lax.rem(d, 8)
    c = lax.rem(i, 2)
    x = lax.rem(i // 2, 2)
    y = i // 4
    hi = (1 - c) * x + c * y
    lo = (1 - c) * y + c * x
    p = 4 * c + 2 * hi + lo
    core_dev = (d + 1 - 2 * c, m)
    flip_x = d + 2 - 4 * x
    flip_y = d + 4 - 8 * y
    hi_dev = ((1 - c) * flip_x + c * flip_y, m)
    lo_dev = ((1 - c) * flip_y + c * flip_x, m)
    up = [lax.rem(m + k, M) for k in range(M)]
    down = [lax.rem(m - k + M, M) for k in range(M)]
    others = [lax.rem(d + k, D) for k in range(D)]
    sent = []

    def remote(src, dst, ss, rs, dev):
        cp = pltpu.make_async_remote_copy(
            src_ref=src, dst_ref=dst, send_sem=ss, recv_sem=rs, device_id=dev, device_id_type=MESH
        )
        return cp

    def send(src, dst, ss, rs, dev):
        cp = remote(src, dst, ss, rs, dev)
        cp.start()
        sent.append(cp)
        return cp

    def gone(cp):
        cp.wait_send()
        sent[:] = [other for other in sent if other is not cp]

    def lanes(ref, at, size):
        return ref.at[:, pl.ds(pl.multiple_of(at, 128), size)]

    def rows(ref, at, size):
        return ref.at[pl.ds(pl.multiple_of(at, 16), size)]

    bar = pltpu.get_barrier_semaphore()
    for k in range(1, D):
        pl.semaphore_signal(bar, inc=1, device_id=(others[k], m), device_id_type=MESH)
    for k in range(1, M):
        pl.semaphore_signal(bar, inc=1, device_id=(d, up[k]), device_id_type=MESH)

    w2_loc = pltpu.make_async_copy(w2_ref, G1, loc.at[1])
    w2_loc.start()
    w1_loc = pltpu.make_async_copy(w1_ref, C.at[m], loc.at[0])
    w1_loc.start()
    cot_loc = pltpu.make_async_copy(lanes(cot_ref, m * Q, Q), lanes(F.at[m], 0, Q), loc.at[2])
    pv[m] = par_ref[...]
    pl.semaphore_wait(bar, D - 1 + M - 1)

    ag1, ag2, agp, ct = {}, {}, {}, {}
    for k in range(1, M):
        agp[k] = send(par_ref, pv.at[m], pvs.at[k], pvr.at[k], (d, up[k]))
    for k in range(1, M):
        ag1[0, k] = send(
            lanes(w1_ref, p * K8, K8), lanes(C.at[m], p * K8, K8), w1s.at[0, k], w1r.at[0, k], (d, up[k])
        )
    w2_loc.wait()
    for b in range(M):
        W2[m, :, (b + 1) * LP - 128 : (b + 1) * LP] = jnp.zeros((U, 128), BF16)
        W2[m, :, b * LP : b * LP + U] = G1[:, b * U : (b + 1) * U]

    def gather_stage(step, ag, buf, size, ss, rs):
        dev, at, width = {
            1: (lo_dev, p * size, size),
            2: (hi_dev, (4 * c + 2 * hi) * size, 2 * size),
            3: (core_dev, 4 * c * size, 4 * size),
        }[step]
        for k in range(1, M):
            ag[step - 1, k].wait_recv()
            part = lanes(buf.at[down[k]], at, width)
            ag[step, k] = send(part, part, ss.at[step, k], rs.at[step, k], dev)

    def stage1(step):
        gather_stage(step, ag1, C, K8, w1s, w1r)

    def stage2(step):
        gather_stage(step, ag2, W2, J8, w2s, w2r)

    hrow = jnp.concatenate(
        [mult_ref[...].astype(F32), add_ref[...].astype(F32), jnp.zeros((126, K), F32)], axis=0
    )
    hcol[...] = hrow.T

    HT = 128

    def encode(q, put):
        def step(t, _):
            at = pl.multiple_of(t * HT, HT)
            both = hcol[pl.ds(at, HT), :].astype(I32)
            v = both[:, 0:1] * ids_ref[:, pl.ds(pl.multiple_of(q * Q, 128), Q)] + both[:, 1:2]
            for _ in range(2):
                top = lax.shift_right_logical(v, 16)
                v = (v & 65535) + ((top << 4) - top)
            v = jnp.where(v >= 65521, v - 65521, v)
            put(t, (v.astype(F32) * (2.0 / 65520.0) - 1.0).astype(BF16))
            return 0

        lax.fori_loop(0, K // HT, step, 0)

    def make_col(b):
        col[b] = jnp.concatenate([RW[b], jnp.zeros((128 - RW.shape[1], LP), F32)], axis=0).T

    def make_cols():
        def step(b, _):
            make_col(b)
            return 0

        lax.fori_loop(0, M, step, 0)

    def to_a(q):
        def put(t, value):
            A[q, pl.ds(pl.multiple_of(t * HT, HT), HT), :] = value

        return put

    def to_e1(t, value):
        E1[pl.ds(pl.multiple_of(lax.rem(t, LP // HT) * HT, HT), HT), pl.ds(pl.multiple_of(t // (LP // HT) * Q, 128), Q)] = value

    def row_of(slot):
        return jnp.sum(acc[slot].T, axis=0, keepdims=True)

    acc[...] = jnp.zeros_like(acc)
    for b in range(M):
        B[pl.ds(b * LP + U // 16 * 16, LP - U // 16 * 16), :] = jnp.zeros((LP - U // 16 * 16, R), BF16)

    RW[...] = jnp.zeros_like(RW)
    RW[m, 0:8] = par_ref[...]
    make_col(m)
    encode(m, to_a(m))
    w1_loc.wait()

    def mm1_own(b):
        act, slope = mish_parts(dot(C[b], A[m]) + col[b, :U, 0:1])
        H[b] = slope.astype(BF16)
        B[pl.ds(pl.multiple_of(b * LP, LP), U), pl.ds(pl.multiple_of(m * Q, Q), Q)] = act.astype(BF16)
        acc[0, :U] += lane_part(act)
        acc[1, :U] += lane_part(act * act)

    def mm1_rest(b):
        def step(t, _):
            q = lax.rem(m + t, M)
            act = mish(dot(C[b], A[q]) + col[b, :U, 0:1])
            B[pl.ds(pl.multiple_of(b * LP, LP), U), pl.ds(pl.multiple_of(q * Q, Q), Q)] = act.astype(BF16)
            acc[0, :U] += lane_part(act)
            acc[1, :U] += lane_part(act * act)
            return 0

        lax.fori_loop(1, M, step, 0)

    def mm1_sums(b):
        ar1[d, pl.ds(b, 1), :] = row_of(0)
        ar1[d, pl.ds(b + M, 1), :] = row_of(1)
        acc[0:2] = jnp.zeros((2, LP, 128), F32)

    mm1_own(m)
    stage1(1)
    for k in range(1, M):
        ag2[0, k] = send(
            lanes(W2.at[m], p * J8, J8), lanes(W2.at[m], p * J8, J8), w2s.at[0, k], w2r.at[0, k], (d, up[k])
        )

    def enc_step(k, _):
        q = lax.rem(m + M - k, M)
        encode(q, to_a(q))
        return 0

    lax.fori_loop(1, M, enc_step, 0)
    stage1(2)
    mm1_rest(m)
    mm1_sums(m)
    stage2(1)
    cot_loc.start()
    for q in range(1, M):
        ct[q] = send(
            lanes(cot_ref, up[q] * Q, Q), lanes(F.at[m], 0, Q), cts.at[q], ctr.at[q], (d, up[q])
        )
    stage1(3)
    for k in range(1, M):
        agp[k].wait_recv()
    for b in range(M):
        RW[b, 0:8] = pv[b]
    make_cols()
    for k in range(1, M):
        ag1[3, k].wait_recv()
        mm1_own(down[k])
        if k == 1:
            pass
        mm1_rest(down[k])
        mm1_sums(down[k])
        if k == 1:
            stage2(2)

    def all_dp(buf, ss, rs):
        cps = []
        for k in range(1, D):
            cps.append(send(buf.at[d], buf.at[d], ss.at[k], rs.at[k], (others[k], m)))
        return cps

    def total(buf, cps):
        for cp in cps:
            cp.wait_recv()
        out = buf[0]
        for k in range(1, D):
            out = out + buf[k]
        return out

    cps1 = all_dp(ar1, a1s, a1r)
    stage2(3)
    for step in range(1, 4):
        for k in range(1, M):
            gone(ag1[step, k])
    cot_all = []
    for q in range(M):
        cp = pltpu.make_async_copy(lanes(cot_ref, q * Q, Q), lanes(C.at[q], 0, Q), loc.at[3 + q])
        cot_all.append(cp)
        cp.start()
    for k in range(1, M):
        ag2[3, k].wait_recv()

    def make_e1(b):
        def step(h, _):
            part = W2[h, :, pl.ds(pl.multiple_of(b * LP, LP), LP)].astype(F32) * col[h, :U, 1:2]
            for n in range(LP // 128):
                acc[n, :U] = part[:, n * 128 : (n + 1) * 128]
            for n in range(LP // 128):
                E1[n * 128 : (n + 1) * 128, pl.ds(pl.multiple_of(h * LP, LP), LP)] = acc[n].T.astype(BF16)
            return 0

        lax.fori_loop(0, M, step, 0)
        acc[...] = jnp.zeros_like(acc)

    const = jnp.zeros((8, M * LP), F32)
    for b in range(M):
        shift = jnp.broadcast_to(pv[b, 2:3, :U], (8, U))
        upper = shift.astype(BF16)
        lower = (shift - upper.astype(F32)).astype(BF16)
        const = const + dot(upper, W2[b]) + dot(lower, W2[b])
    for b in range(M):
        RW[b, 8:9] = const[0:1, b * LP : (b + 1) * LP] + pv[b, 3:4]
    make_e1(m)

    tot = total(ar1, cps1)
    mean = tot[:M] / N
    inv = lax.rsqrt(tot[M:] / N - mean * mean + epsilon)
    for b in range(M):
        RW[b, 9:10] = inv[b : b + 1]
        RW[b, 10:11] = -mean[b : b + 1] * inv[b : b + 1]
    make_cols()
    for cp in cot_all:
        cp.wait()

    def mm2(t, _):
        at = pl.multiple_of(t * TL, TL)
        for b in range(M):
            part = B[b * LP : b * LP + U, pl.ds(at, TL)].astype(F32)
            B[b * LP : b * LP + U, pl.ds(at, TL)] = (part * col[b, :U, 9:10] + col[b, :U, 10:11]).astype(BF16)
        v = dot(E1[:U], B[:, pl.ds(at, TL)]) + col[m, :U, 8:9]
        act, slope = mish_parts(v)
        act2[:, pl.ds(at, TL)] = act.astype(BF16)
        slo2[:, pl.ds(at, TL)] = slope.astype(BF16)
        g = C[t // NT, :, pl.ds(pl.multiple_of(lax.rem(t, NT) * TL, TL), TL)].astype(F32)
        acc[0, :U] += lane_part(act)
        acc[1, :U] += lane_part(act * act)
        acc[2, :U] += lane_part(g)
        acc[3, :U] += lane_part(g * act)
        return 0

    lax.fori_loop(0, M * NT, mm2, 0)
    for s in range(4):
        ar2[d, s : s + 1, :] = row_of(s)
    ar2[d, 4:8, :] = jnp.zeros((4, LP), F32)
    acc[...] = jnp.zeros_like(acc)
    cps2 = all_dp(ar2, a2s, a2r)

    def a_at(base, b):
        return base + b // PER, pl.multiple_of(lax.rem(b, PER) * LP, LP)

    def mm2_own(b):
        make_e1(b)
        act_at, row = a_at(0, b)

        def step(t, _):
            at = pl.multiple_of(t * TL, TL)
            v = dot(E1[:U], B[:, pl.ds(pl.multiple_of(m * Q + t * TL, TL), TL)]) + col[b, :U, 8:9]
            act, slope = mish_parts(v)
            A[act_at, pl.ds(row, U), pl.ds(at, TL)] = act.astype(BF16)
            A[act_at + NA, pl.ds(row, U), pl.ds(at, TL)] = slope.astype(BF16)
            return 0

        lax.fori_loop(0, NT, step, 0)

    def own_loop(k, _):
        mm2_own(lax.rem(m + k, M))
        return 0

    mm2_own(up[1])
    tot = total(ar2, cps2)
    mean = tot[0:1] / N
    inv = lax.rsqrt(tot[1:2] / N - mean * mean + epsilon)
    sum_g = tot[2:3]
    sum_gn = inv * (tot[3:4] - mean * sum_g)
    k1 = pv[m, 4:5] * inv
    k2 = -k1 * inv * sum_gn / N
    k3 = -k1 * sum_g / N - mean * k2
    ar2z[m, 0:1] = k1
    ar2z[m, 1:2] = k2
    ar2z[m, 2:3] = k3
    ar2z[m, 3:4] = k1
    ar2z[m, 4:5] = pv[m, 5:6] - mean * k1
    ar2z[m, 5:6] = sum_g
    ar2z[m, 6:7] = sum_gn
    ar2z[m, 7:8] = jnp.zeros((1, LP), F32)
    cps2z = [send(ar2z.at[m], ar2z.at[m], a2zs.at[k], a2zr.at[k], (d, up[k])) for k in range(1, M)]
    RW[m, 16:24] = ar2z[m]
    make_col(m)

    def back2(t, _):
        at = pl.multiple_of(t * TL, TL)
        a = act2[:, pl.ds(at, TL)].astype(F32)
        g = C[t // NT, :, pl.ds(pl.multiple_of(lax.rem(t, NT) * TL, TL), TL)].astype(F32)
        act2[:, pl.ds(at, TL)] = (a * col[m, :U, 19:20] + col[m, :U, 20:21]).astype(BF16)
        grad = (g * col[m, :U, 16:17] + a * col[m, :U, 17:18] + col[m, :U, 18:19]) * slo2[:, pl.ds(at, TL)].astype(F32)
        grad = grad.astype(BF16)
        slo2[:, pl.ds(at, TL)] = grad
        acc[0, :U] += lane_part(grad.astype(F32))
        return 0

    lax.fori_loop(0, M * NT, back2, 0)
    out_copy = pltpu.make_async_copy(act2, out_ref, loc.at[0])
    out_copy.start()
    gb2 = row_of(0)
    ar3[d, 2 * M : 2 * M + 1, :] = gb2
    ar3[d, 2 * M + 1 : 2 * M + 8, :] = jnp.zeros((7, LP), F32)
    acc[0:1] = jnp.zeros((1, LP, 128), F32)

    L1 = pl.multiple_of(lax.rem(m + 1, M) * Q, 128)
    LR = pl.multiple_of(L1 + LP, 128)

    def rowsum(x):
        acc[0, :U] = lane_part(x[:, : U // 128 * 128]) + jnp.where(
            lax.broadcasted_iota(I32, (U, 128), 1) >= 128 - U % 128, x[:, U - 128 :], 0.0
        )
        return row_of(0)

    def grad_w2(b, _):
        at = pl.multiple_of(b * LP, LP)
        g = dot_nt(B[pl.ds(at, LP), :], slo2[...])
        w = W2[b, :, pl.ds(pl.multiple_of(m * LP, LP), LP)].astype(F32)[:, :U]
        ar3[d, pl.ds(b, 1), :] = rowsum(w * gb2[:, :U])
        ar3[d, pl.ds(b + M, 1), :] = rowsum(w * g[:U])
        g = g * col[b, :, 1:2] + col[b, :, 2:3] * gb2[:, :U]
        B[pl.ds(at, LP), pl.ds(L1, U)] = g.astype(BF16)
        B[pl.ds(at, LP), pl.ds(L1 + U // 128 * 128, LP - U // 128 * 128)] = jnp.where(
            lax.broadcasted_iota(I32, (LP, LP - U // 128 * 128), 1) < U - U // 128 * 128,
            B[pl.ds(at, LP), pl.ds(L1 + U // 128 * 128, LP - U // 128 * 128)].astype(F32),
            0.0,
        ).astype(BF16)
        return 0

    lax.fori_loop(0, M, grad_w2, 0)
    cps3 = all_dp(ar3, a3s, a3r)
    for n, dev in ((0, core_dev), (1, hi_dev), (2, lo_dev)):
        pl.semaphore_signal(free.at[n], inc=1, device_id=dev, device_id_type=MESH)
    for k in range(1, M):
        pl.semaphore_signal(free.at[2 + k], inc=1, device_id=(d, up[k]), device_id_type=MESH)

    HALF = {0: (1 - c) * 4, 1: 4 * c + 2 * (1 - hi), 2: 4 * c + 2 * hi + 1 - lo}
    KEEP = {0: 4 * c, 1: 4 * c + 2 * hi, 2: p}
    START = {0: 0, 1: 4, 2: 6}
    PARTNER = {0: core_dev, 1: hi_dev, 2: lo_dev}
    g2cp = {}

    def b_rows(b, at, size, lane):
        return B.at[pl.ds(pl.multiple_of(b * LP + at * S8, 16), size * S8), pl.ds(lane, LP)]

    def g2_send(n):
        pl.semaphore_wait(free.at[n], 1)
        for b in range(M):
            g2cp[n, b] = send(
                b_rows(b, HALF[n], 4 >> n, L1), b_rows(b, START[n], 4 >> n, LR), g2s.at[n, b], g2r.at[n, b], PARTNER[n]
            )

    def g2_add(n):
        for b in range(M):
            g2cp[n, b].wait_recv()
            size = (4 >> n) * S8
            keep = pl.ds(pl.multiple_of(b * LP + KEEP[n] * S8, 16), size)
            came = pl.ds(b * LP + START[n] * S8, size)
            B[keep, pl.ds(L1, LP)] = (
                B[keep, pl.ds(L1, LP)].astype(F32) + B[came, pl.ds(LR, LP)].astype(F32)
            ).astype(BF16)

    def l2_of(z):
        return pl.multiple_of(lax.rem(z + 2, M) * Q, 128)

    L2 = l2_of(m)

    if G > 1:
        x1, x2, x1s, x1r, x2s, x2r = extra

    def g2_groups():
        cps = []
        for k in range(1, G):
            to = (lax.rem(d + 8 * k, D), m)
            for b in range(M):
                cps.append(send(b_rows(b, p, 1, L1), x2.at[d // 8, b], x2s.at[k, b], x2r.at[k, b], to))
        for b in range(M):
            x2[d // 8, b] = B[pl.ds(pl.multiple_of(b * LP + p * S8, 16), S8), pl.ds(L1, LP)]
        for cp in cps:
            cp.wait_recv()
        for cp in cps:
            gone(cp)
        for b in range(M):
            v = x2[0, b].astype(F32)
            for k in range(1, G):
                v = v + x2[k, b].astype(F32)
            B[pl.ds(pl.multiple_of(b * LP + p * S8, 16), S8), pl.ds(L1, LP)] = v.astype(BF16)

    def g2_z():
        if G > 1:
            g2_groups()
        for k in range(1, M):
            pl.semaphore_wait(free.at[2 + M - k], 1)
            g2cp[3, k] = send(
                b_rows(up[k], p, 1, L1),
                B.at[pl.ds(pl.multiple_of(m * LP + p * S8, 16), S8), pl.ds(l2_of(up[k]), LP)],
                g2s.at[3, k], g2r.at[3, k], (d, up[k]),
            )
        mine = pl.ds(pl.multiple_of(m * LP + p * S8, 16), S8)
        B[mine, pl.ds(L2, LP)] = B[mine, pl.ds(L1, LP)]

    def g2_gather(n):
        at, size, dev = {4: (p, 1, lo_dev), 5: (4 * c + 2 * hi, 2, hi_dev), 6: (4 * c, 4, core_dev)}[n]
        if n == 4:
            for k in range(1, M):
                g2cp[3, k].wait_recv()
        else:
            for b in range(M):
                g2cp[n - 1, b].wait_recv()
        for b in range(M):
            part = b_rows(b, at, size, L2)
            g2cp[n, b] = send(part, part, g2s.at[n, b], g2r.at[n, b], dev)

    g2_send(0)
    lax.fori_loop(2, M, own_loop, 0)
    tot = total(ar3, cps3)
    ar3z[m] = tot[: 2 * M]
    gb2_all = tot[2 * M : 2 * M + 1]
    cps3z = [send(ar3z.at[m], ar3z.at[m], a3zs.at[k], a3zr.at[k], (d, up[k])) for k in range(1, M)]
    g2_add(0)
    g2_send(1)
    encode(m, to_e1)
    for cp in cps2z:
        cp.wait_recv()
    for b in range(M):
        RW[b, 16:24] = ar2z[b]
    for cp in cps3z:
        cp.wait_recv()
    tot = ar3z[0]
    for b in range(1, M):
        tot = tot + ar3z[b]
    for b in range(M):
        k1 = pv[b, 1:2] * RW[b, 9:10]
        RW[b, 24:25] = k1
        RW[b, 25:26] = -k1 * tot[M + b : M + b + 1] / N
        RW[b, 26:27] = -k1 * tot[b : b + 1] / N
    make_cols()
    pick = lax.broadcasted_iota(I32, (2 * M, 1), 0)
    vec_ref[0:1, :] = jnp.zeros((1, LP), F32)
    vec_ref[1:2, :] = jnp.sum(jnp.where(pick == M + m, tot, 0.0), axis=0, keepdims=True)
    vec_ref[2:3, :] = jnp.sum(jnp.where(pick == m, tot, 0.0), axis=0, keepdims=True)
    vec_ref[3:4, :] = gb2_all
    vec_ref[4:5, :] = ar2z[m, 6:7]
    vec_ref[5:6, :] = ar2z[m, 5:6]
    vec_ref[6:8, :] = jnp.zeros((2, LP), F32)

    PADAT = U // 16 * 16

    def put_grad(b, value, at, size):
        slot, row = a_at(NA, b)
        A[slot, pl.ds(row, U), pl.ds(at, size)] = value

    for b in range(M):
        slot, row = NA + b // PER, (b % PER) * LP
        A[slot, row + PADAT : row + LP, :] = jnp.where(
            lax.broadcasted_iota(I32, (LP - PADAT, Q), 0) < U - PADAT,
            A[slot, row + PADAT : row + LP, :].astype(F32),
            0.0,
        ).astype(BF16)
    cot_loc.wait()

    def back2_own(b):
        act_at, row = a_at(0, b)

        def step(t, _):
            at = pl.multiple_of(t * TL, TL)
            a = A[act_at, pl.ds(row, U), pl.ds(at, TL)].astype(F32)
            s = A[act_at + NA, pl.ds(row, U), pl.ds(at, TL)].astype(F32)
            g = F[b, :, pl.ds(at, TL)].astype(F32)
            grad = (g * col[b, :U, 16:17] + a * col[b, :U, 17:18] + col[b, :U, 18:19]) * s
            A[act_at + NA, pl.ds(row, U), pl.ds(at, TL)] = grad.astype(BF16)
            return 0

        lax.fori_loop(0, NT, step, 0)

    def copy_own(t, _):
        at = pl.multiple_of(t * TL, TL)
        put_grad(m, slo2[:, pl.ds(pl.multiple_of(m * Q + t * TL, TL), TL)], at, TL)
        return 0

    lax.fori_loop(0, NT, copy_own, 0)
    for k in range(1, M):
        ct[k].wait_recv()
        back2_own(down[k])

    g2_add(1)
    g2_send(2)

    def back1(b):
        def step(t, _):
            at = pl.multiple_of(t * TL, TL)
            dh = dot(W2[b, :, 0:K], A[NA, :, pl.ds(at, TL)])
            for n in range(1, NA):
                dh = dh + dot(W2[b, :, n * K : (n + 1) * K], A[NA + n, :, pl.ds(at, TL)])
            norm = B[pl.ds(pl.multiple_of(b * LP, LP), U), pl.ds(pl.multiple_of(m * Q + t * TL, TL), TL)].astype(F32)
            grad = dh * col[b, :U, 24:25] + norm * col[b, :U, 25:26] + col[b, :U, 26:27]
            grad = (grad * H[b, :, pl.ds(at, TL)].astype(F32)).astype(BF16)
            H[b, :, pl.ds(at, TL)] = grad
            acc[0, :U] += lane_part(grad.astype(F32))
            return 0

        lax.fori_loop(0, NT, step, 0)
        ar4[d, pl.ds(b, 1), :] = row_of(0)
        acc[0:1] = jnp.zeros((1, LP, 128), F32)

        def mm(t, _):
            F[b, :, pl.ds(pl.multiple_of(t * LP, LP), LP)] = dot_nt(
                H[b], E1[:, pl.ds(pl.multiple_of(t * Q, Q), Q)]
            ).astype(BF16)
            return 0

        lax.fori_loop(0, PER, mm, 0)

    acc[0:1] = jnp.zeros((1, LP, 128), F32)
    ar4[d] = jnp.zeros((ar4.shape[1], LP), F32)
    K2 = 4 * K8
    FROM = {0: 0, 1: K2, 2: K2 + 2 * K8}
    order = [up[(j + 1) % M] for j in range(M)]
    g1cp = {}

    def g1_send(n, j):
        b = order[j]
        g1cp[n, j] = send(
            lanes(F.at[b], HALF[n] * K8, K2 >> n), lanes(C.at[b], FROM[n], K2 >> n), g1s.at[n, j], g1r.at[n, j], PARTNER[n]
        )

    def g1_add(n, j):
        b = order[j]
        g1cp[n, j].wait_recv()
        keep = pl.ds(pl.multiple_of(KEEP[n] * K8, 128), K2 >> n)
        F[b, :, keep] = (F[b, :, keep].astype(F32) + C[b, :, FROM[n] : FROM[n] + (K2 >> n)].astype(F32)).astype(BF16)

    def g1_groups(j):
        b = order[j]
        mine = pl.ds(pl.multiple_of(p * K8, 128), K8)
        cps = []
        for k in range(1, G):
            to = (lax.rem(d + 8 * k, D), m)
            cps.append(send(lanes(F.at[b], p * K8, K8), x1.at[d // 8, j], x1s.at[k, j], x1r.at[k, j], to))
        x1[d // 8, j] = F[b, :, mine]
        for cp in cps:
            cp.wait_recv()
        for cp in cps:
            gone(cp)
        v = x1[0, j].astype(F32)
        for k in range(1, G):
            v = v + x1[k, j].astype(F32)
        F[b, :, mine] = v.astype(BF16)

    def g1_z(j):
        if G > 1:
            g1_groups(j)
        b, k = order[j], (j + 1) % M
        if k:
            g1cp[3, j] = send(
                lanes(F.at[b], p * K8, K8), C.at[m, :, pl.ds(K - K8, K8)], g1s.at[3, k], g1r.at[3, k], (d, b)
            )
        else:
            C[m, :, K - K8 : K] = F[m, :, pl.ds(pl.multiple_of(p * K8, 128), K8)]

    def g1_stage(n, j):
        if 0 <= j < M:
            g1_add(n - 1, j)
            if n < 3:
                g1_send(n, j)
            else:
                g1_z(j)

    for j in range(M + 3):
        if j < M:
            back1(order[j])
            g1_send(0, j)
        if j == M - 1:
            cps4 = all_dp(ar4, a4s, a4r)
        g1_stage(3, j - 3)
        g1_stage(2, j - 2)
        g1_stage(1, j - 1)
        if j == 1:
            g2_add(2)
            g2_z()
        if j == 2:
            g2_gather(4)
        if j == 3:
            g2_gather(5)
        if j == 4:
            g2_gather(6)
        if j == M:
            tot4 = total(ar4, cps4)
            for b in range(M):
                ar4s[b] = jnp.broadcast_to(tot4[b : b + 1], (8, LP))
            ar4z[m] = ar4s[m]
            cps4z = [send(ar4s.at[up[k]], ar4z.at[m], a4zs.at[k], a4zr.at[k], (d, up[k])) for k in range(1, M)]
    for b in range(M):
        g2cp[6, b].wait_recv()
    for b in range(M):
        slo2[:, b * U : (b + 1) * U] = B[b * LP : b * LP + U, pl.ds(L2, LP)][:, :U]
    gw2_copy = pltpu.make_async_copy(lanes(slo2, 0, gw2_ref.shape[1]), gw2_ref, loc.at[2])
    gw2_copy.start()
    for j in range(M - 1):
        g1cp[3, j].wait_recv()
    v = C[0, :, K - K8 : K].astype(F32)
    for b in range(1, M):
        v = v + C[b, :, K - K8 : K].astype(F32)
    G1[:, pl.ds(pl.multiple_of(p * K8, 128), K8)] = v.astype(BF16)
    ga = send(lanes(G1, p * K8, K8), lanes(G1, p * K8, K8), g1s.at[4, 0], g1r.at[4, 0], lo_dev)
    ga.wait_recv()
    part = lanes(G1, (4 * c + 2 * hi) * K8, 2 * K8)
    ga = send(part, part, g1s.at[4, 1], g1r.at[4, 1], hi_dev)
    ga.wait_recv()
    part = lanes(G1, 4 * c * K8, K2)
    ga = send(part, part, g1s.at[4, 2], g1r.at[4, 2], core_dev)
    for cp in cps4z:
        cp.wait_recv()
    v = ar4z[0]
    for b in range(1, M):
        v = v + ar4z[b]
    vec_ref[0:1, :] = v[0:1]
    ga.wait_recv()
    gw1_copy = pltpu.make_async_copy(lanes(G1, 0, K), gw1_ref, loc.at[1])
    gw1_copy.start()
    out_copy.wait()
    gw1_copy.wait()
    gw2_copy.wait()
    for cp in sent:
        cp.wait_send()


def finish(U, out_in, gw1_in, gw2_in, vec_in, out_ref, gw1_ref, gw2_ref, *tail):
    *vecs, held, held1, held2, wide1, wide2, sem_in, sem_out = tail
    n = 4
    width = held.shape[1] // n
    pieces = [pl.ds(k * width, width) for k in range(n)]
    ins = [
        pltpu.make_async_copy(gw2_in, held2, sem_in.at[n]),
        pltpu.make_async_copy(gw1_in, held1, sem_in.at[n + 1]),
    ] + [pltpu.make_async_copy(out_in.at[:, at], held.at[:, at], sem_in.at[k]) for k, at in enumerate(pieces)]
    for cp in ins:
        cp.start()
    outs = [
        pltpu.make_async_copy(wide2, gw2_ref, sem_out.at[n]),
        pltpu.make_async_copy(wide1, gw1_ref, sem_out.at[n + 1]),
    ] + [pltpu.make_async_copy(held.at[:, at], out_ref.at[:, at], sem_out.at[k]) for k, at in enumerate(pieces)]
    ins[0].wait()
    wide2[...] = held2[:, : wide2.shape[1]].astype(F32)
    outs[0].start()
    ins[1].wait()
    wide1[...] = held1[...].astype(F32)
    outs[1].start()
    for k in range(n):
        ins[2 + k].wait()
        outs[2 + k].start()
    for k, ref in enumerate(vecs):
        ref[...] = vec_in[k : k + 1, :U]
    for cp in outs:
        cp.wait()


def per_device(ids, hash_mult, hash_add, w1, b1, s1, t1, w2, b2, s2, t2, cot):
    D, M = lax.axis_size("dp"), lax.axis_size("mp")
    U, K = w1.shape
    R = ids.shape[0]
    Q = R // M
    LP = -(-U // 128) * 128
    G = D // 8
    par = jnp.pad(jnp.stack([b1, s1, t1, b2, s2, t2]), ((0, 2), (0, LP - U)))
    dma = pltpu.SemaphoreType.DMA
    vmem = pl.BlockSpec(memory_space=pltpu.VMEM)
    hbm = pl.BlockSpec(memory_space=pl.ANY)
    AR = -(-2 * M // 8) * 8
    scratch = [
        pltpu.VMEM((M, K, Q), BF16),
        pltpu.VMEM((M * LP, R), BF16),
        pltpu.VMEM((M, U, max(K, Q)), BF16),
        pltpu.VMEM((M, U, M * LP), BF16),
        pltpu.VMEM((U, max(K, M * U)), BF16),
        pltpu.VMEM((LP, M * LP), BF16),
        pltpu.VMEM((M, U, max(K, Q)), BF16),
        pltpu.VMEM((M, U, Q), BF16),
        pltpu.VMEM((U, R), BF16),
        pltpu.VMEM((U, R), BF16),
        pltpu.VMEM((M, LP, 128), F32),
        pltpu.VMEM((M, 32, LP), F32),
        pltpu.VMEM((4, LP, 128), F32),
        pltpu.VMEM((K, 128), F32),
        pltpu.VMEM((M, 8, LP), F32),
        pltpu.VMEM((D, AR, LP), F32),
        pltpu.VMEM((D, 8, LP), F32),
        pltpu.VMEM((M, 8, LP), F32),
        pltpu.VMEM((D, AR + 8, LP), F32),
        pltpu.VMEM((M, AR, LP), F32),
        pltpu.VMEM((D, 8, LP), F32),
        pltpu.VMEM((M, 8, LP), F32),
        pltpu.VMEM((M, 8, LP), F32),
        dma((4, M)), dma((4, M)), dma((4, M)), dma((4, M)),
        dma((M,)), dma((M,)), dma((M,)), dma((M,)), dma((3 + M,)),
        dma((D,)), dma((D,)), dma((D,)), dma((D,)), dma((M,)), dma((M,)),
        dma((D,)), dma((D,)), dma((M,)), dma((M,)), dma((D,)), dma((D,)), dma((M,)), dma((M,)),
        dma((5, M)), dma((5, M)), dma((7, M)), dma((7, M)), pltpu.SemaphoreType.REGULAR((2 + M,)),
    ]
    if G > 1:
        scratch += [
            pltpu.VMEM((G, M, U, K // 8), BF16),
            pltpu.VMEM((G, M, LP // 8, LP), BF16),
            dma((G, M)), dma((G, M)), dma((G, M)), dma((G, M)),
        ]
    out, gw1, gw2, vec = pl.pallas_call(
        functools.partial(kernel, D, M, U, LP, K, R),
        out_shape=[
            jax.ShapeDtypeStruct((U, R), BF16),
            jax.ShapeDtypeStruct((U, K), BF16),
            jax.ShapeDtypeStruct((U, -(-M * U // 128) * 128), BF16),
            jax.ShapeDtypeStruct((8, LP), F32),
        ],
        in_specs=[vmem] * 4 + [hbm, hbm, hbm],
        out_specs=[hbm, hbm, hbm, vmem],
        scratch_shapes=scratch,
        compiler_params=pltpu.CompilerParams(
            collective_id=0, has_side_effects=True, vmem_limit_bytes=64 * 2**20 - 2**18
        ),
    )(ids[None, :], hash_mult[None, :], hash_add[None, :], par, w1, w2, cot)
    out, gw1, gw2, *v = pl.pallas_call(
        functools.partial(finish, U),
        out_shape=[
            jax.ShapeDtypeStruct((U, R), BF16),
            jax.ShapeDtypeStruct((U, K), F32),
            jax.ShapeDtypeStruct((U, M * U), F32),
        ]
        + [jax.ShapeDtypeStruct((1, U), F32)] * 6,
        in_specs=[hbm, hbm, hbm, vmem],
        out_specs=[hbm, hbm, hbm] + [vmem] * 6,
        scratch_shapes=[
            pltpu.VMEM((U, R), BF16),
            pltpu.VMEM((U, K), BF16),
            pltpu.VMEM(gw2.shape, BF16),
            pltpu.VMEM((U, K), F32),
            pltpu.VMEM((U, M * U), F32),
            dma((6,)),
            dma((6,)),
        ],
        compiler_params=pltpu.CompilerParams(vmem_limit_bytes=63 * 2**20),
    )(out, gw1, gw2, vec)
    v = [x[0] for x in v]
    return (out, gw1, v[0], v[1], v[2], gw2, v[3], v[4], v[5])


def solution(mesh):
    return jax.shard_map(
        per_device,
        mesh=mesh,
        in_specs=(
            P("dp"), P(), P(), P("mp", None), P("mp"), P("mp"), P("mp"),
            P("mp", None), P("mp"), P("mp"), P("mp"), P("mp", "dp"),
        ),
        out_specs=(
            P("mp", "dp"), P("mp", None), P("mp"), P("mp"), P("mp"),
            P("mp", None), P("mp"), P("mp"), P("mp"),
        ),
        check_vma=False,
    )
```

```python
import functools

import jax
import jax.numpy as jnp
from jax import lax
from jax.experimental import pallas as pl
from jax.experimental.pallas import tpu as pltpu
from jax.sharding import PartitionSpec as P

MESH = pl.DeviceIdType.MESH
F32, BF16, I32 = jnp.float32, jnp.bfloat16, jnp.int32
epsilon = 1e-05


def dot(a, b):
    return lax.dot_general(a, b, (((1,), (0,)), ((), ())), preferred_element_type=F32)


def dot_nt(a, b):
    return lax.dot_general(a, b, (((1,), (1,)), ((), ())), preferred_element_type=F32)


def mish_parts(v):
    u = jnp.exp(jnp.minimum(v, 20.0))
    n = u * (u + 2.0)
    d = n + 2.0
    r = pl.reciprocal(d, approx=True)
    t = n * r
    return v * t, t + v * ((4.0 * (n - u) * r) * r)


def mish(v):
    u = jnp.exp(jnp.minimum(v, 20.0))
    n = u * (u + 2.0)
    d = n + 2.0
    r = pl.reciprocal(d, approx=True)
    return v * (n * r)


def lane_part(x):
    out = x[:, :128]
    for at in range(128, x.shape[1], 128):
        out = out + x[:, at : at + 128]
    return out


def kernel(
    D, M, U, LP, K, R,
    ids_ref, mult_ref, add_ref, par_ref, w1_ref, w2_ref, cot_ref,
    out_ref, gw1_ref, gw2_ref, vec_ref,
    A, B, C, W2, G1, E1, F, H, act2, slo2, col, RW, acc, hcol,
    pv, ar1, ar2, ar2z, ar3, ar3z, ar4, ar4s, ar4z,
    w1s, w1r, w2s, w2r, pvs, pvr, cts, ctr, loc,
    a1s, a1r, a2s, a2r, a2zs, a2zr, a3s, a3r, a3zs, a3zr, a4s, a4r, a4zs, a4zr,
    g1s, g1r, g2s, g2r, free, *extra,
):
    Q = R // M
    G = D // 8
    TL = min(512, Q)
    NT = Q // TL
    PER = K // LP
    NA = M // PER
    K8 = K // 8
    J8 = M * LP // 8
    S8 = LP // 8
    N = float(R * D)
    d = lax.axis_index("dp")
    m = lax.axis_index("mp")
    i = lax.rem(d, 8)
    c = lax.rem(i, 2)
    x = lax.rem(i // 2, 2)
    y = i // 4
    hi = (1 - c) * x + c * y
    lo = (1 - c) * y + c * x
    p = 4 * c + 2 * hi + lo
    core_dev = (d + 1 - 2 * c, m)
    flip_x = d + 2 - 4 * x
    flip_y = d + 4 - 8 * y
    hi_dev = ((1 - c) * flip_x + c * flip_y, m)
    lo_dev = ((1 - c) * flip_y + c * flip_x, m)
    up = [lax.rem(m + k, M) for k in range(M)]
    down = [lax.rem(m - k + M, M) for k in range(M)]
    others = [lax.rem(d + k, D) for k in range(D)]
    sent = []

    def remote(src, dst, ss, rs, dev):
        cp = pltpu.make_async_remote_copy(
            src_ref=src, dst_ref=dst, send_sem=ss, recv_sem=rs, device_id=dev, device_id_type=MESH
        )
        return cp

    def send(src, dst, ss, rs, dev):
        cp = remote(src, dst, ss, rs, dev)
        cp.start()
        sent.append(cp)
        return cp

    def gone(cp):
        cp.wait_send()
        sent[:] = [other for other in sent if other is not cp]

    def lanes(ref, at, size):
        return ref.at[:, pl.ds(pl.multiple_of(at, 128), size)]

    def rows(ref, at, size):
        return ref.at[pl.ds(pl.multiple_of(at, 16), size)]

    bar = pltpu.get_barrier_semaphore()
    greeted = [core_dev, hi_dev, lo_dev] if G == 1 else [(others[k], m) for k in range(1, D)]
    greeted += [(d, up[k]) for k in range(1, M)]
    for dev in greeted:
        pl.semaphore_signal(bar, inc=1, device_id=dev, device_id_type=MESH)

    w2_loc = pltpu.make_async_copy(w2_ref, G1, loc.at[1])
    w2_loc.start()
    w1_loc = pltpu.make_async_copy(w1_ref, C.at[m], loc.at[0])
    w1_loc.start()
    cot_loc = pltpu.make_async_copy(lanes(cot_ref, m * Q, Q), lanes(F.at[m], 0, Q), loc.at[2])
    pv[m] = par_ref[...]
    pl.semaphore_wait(bar, len(greeted))

    ag1, ag2, agp, ct = {}, {}, {}, {}
    for k in range(1, M):
        agp[k] = send(par_ref, pv.at[m], pvs.at[k], pvr.at[k], (d, up[k]))
    for k in range(1, M):
        ag1[0, k] = send(
            lanes(w1_ref, p * K8, K8), lanes(C.at[m], p * K8, K8), w1s.at[0, k], w1r.at[0, k], (d, up[k])
        )
    w2_loc.wait()
    for b in range(M):
        W2[m, :, (b + 1) * LP - 128 : (b + 1) * LP] = jnp.zeros((U, 128), BF16)
        W2[m, :, b * LP : b * LP + U] = G1[:, b * U : (b + 1) * U]

    def gather_stage(step, ag, buf, size, ss, rs):
        dev, at, width = {
            1: (lo_dev, p * size, size),
            2: (hi_dev, (4 * c + 2 * hi) * size, 2 * size),
            3: (core_dev, 4 * c * size, 4 * size),
        }[step]
        for k in range(1, M):
            ag[step - 1, k].wait_recv()
            part = lanes(buf.at[down[k]], at, width)
            ag[step, k] = send(part, part, ss.at[step, k], rs.at[step, k], dev)

    def stage1(step):
        gather_stage(step, ag1, C, K8, w1s, w1r)

    def stage2(step):
        gather_stage(step, ag2, W2, J8, w2s, w2r)

    hrow = jnp.concatenate(
        [mult_ref[...].astype(F32), add_ref[...].astype(F32), jnp.zeros((126, K), F32)], axis=0
    )
    hcol[...] = hrow.T

    HT = 128

    def encode(q, put):
        def step(t, _):
            at = pl.multiple_of(t * HT, HT)
            both = hcol[pl.ds(at, HT), :].astype(I32)
            v = both[:, 0:1] * ids_ref[:, pl.ds(pl.multiple_of(q * Q, 128), Q)] + both[:, 1:2]
            for _ in range(2):
                top = lax.shift_right_logical(v, 16)
                v = (v & 65535) + ((top << 4) - top)
            v = jnp.where(v >= 65521, v - 65521, v)
            put(t, (v.astype(F32) * (2.0 / 65520.0) - 1.0).astype(BF16))
            return 0

        lax.fori_loop(0, K // HT, step, 0)

    def make_col(b):
        col[b] = jnp.concatenate([RW[b], jnp.zeros((128 - RW.shape[1], LP), F32)], axis=0).T

    def make_cols():
        def step(b, _):
            make_col(b)
            return 0

        lax.fori_loop(0, M, step, 0)

    def to_a(q):
        def put(t, value):
            A[q, pl.ds(pl.multiple_of(t * HT, HT), HT), :] = value

        return put

    def to_e1(t, value):
        E1[pl.ds(pl.multiple_of(lax.rem(t, LP // HT) * HT, HT), HT), pl.ds(pl.multiple_of(t // (LP // HT) * Q, 128), Q)] = value

    def row_of(slot):
        return jnp.sum(acc[slot].T, axis=0, keepdims=True)

    acc[...] = jnp.zeros_like(acc)
    for b in range(M):
        B[pl.ds(b * LP + U // 16 * 16, LP - U // 16 * 16), :] = jnp.zeros((LP - U // 16 * 16, R), BF16)

    RW[...] = jnp.zeros_like(RW)
    RW[m, 0:8] = par_ref[...]
    make_col(m)
    encode(m, to_a(m))
    w1_loc.wait()

    def mm1_own(b):
        act, slope = mish_parts(dot(C[b], A[m]) + col[b, :U, 0:1])
        H[b] = slope.astype(BF16)
        B[pl.ds(pl.multiple_of(b * LP, LP), U), pl.ds(pl.multiple_of(m * Q, Q), Q)] = act.astype(BF16)
        acc[0, :U] += lane_part(act)
        acc[1, :U] += lane_part(act * act)

    def mm1_rest(b):
        def step(t, _):
            q = lax.rem(m + t, M)
            act = mish(dot(C[b], A[q]) + col[b, :U, 0:1])
            B[pl.ds(pl.multiple_of(b * LP, LP), U), pl.ds(pl.multiple_of(q * Q, Q), Q)] = act.astype(BF16)
            acc[0, :U] += lane_part(act)
            acc[1, :U] += lane_part(act * act)
            return 0

        lax.fori_loop(1, M, step, 0)

    def mm1_sums(b):
        ar1[d, pl.ds(b, 1), :] = row_of(0)
        ar1[d, pl.ds(b + M, 1), :] = row_of(1)
        acc[0:2] = jnp.zeros((2, LP, 128), F32)

    mm1_own(m)
    stage1(1)
    for k in range(1, M):
        ag2[0, k] = send(
            lanes(W2.at[m], p * J8, J8), lanes(W2.at[m], p * J8, J8), w2s.at[0, k], w2r.at[0, k], (d, up[k])
        )

    def enc_step(k, _):
        q = lax.rem(m + M - k, M)
        encode(q, to_a(q))
        return 0

    lax.fori_loop(1, M, enc_step, 0)
    stage1(2)
    mm1_rest(m)
    mm1_sums(m)
    stage2(1)
    cot_loc.start()
    for q in range(1, M):
        ct[q] = send(
            lanes(cot_ref, up[q] * Q, Q), lanes(F.at[m], 0, Q), cts.at[q], ctr.at[q], (d, up[q])
        )
    stage1(3)
    for k in range(1, M):
        agp[k].wait_recv()
    for b in range(M):
        RW[b, 0:8] = pv[b]
    make_cols()
    for k in range(1, M):
        ag1[3, k].wait_recv()
        mm1_own(down[k])
        if k == 1:
            pass
        mm1_rest(down[k])
        mm1_sums(down[k])
        if k == 1:
            stage2(2)

    def all_dp(buf, ss, rs):
        cps = []
        for k in range(1, D):
            cps.append(send(buf.at[d], buf.at[d], ss.at[k], rs.at[k], (others[k], m)))
        return cps

    def total(buf, cps):
        for cp in cps:
            cp.wait_recv()
        out = buf[0]
        for k in range(1, D):
            out = out + buf[k]
        return out

    cps1 = all_dp(ar1, a1s, a1r)
    stage2(3)
    for step in range(1, 4):
        for k in range(1, M):
            gone(ag1[step, k])
    cot_all = []
    for q in range(M):
        cp = pltpu.make_async_copy(lanes(cot_ref, q * Q, Q), lanes(C.at[q], 0, Q), loc.at[3 + q])
        cot_all.append(cp)
        cp.start()
    for k in range(1, M):
        ag2[3, k].wait_recv()

    def make_e1(b):
        def step(h, _):
            part = W2[h, :, pl.ds(pl.multiple_of(b * LP, LP), LP)].astype(F32) * col[h, :U, 1:2]
            for n in range(LP // 128):
                acc[n, :U] = part[:, n * 128 : (n + 1) * 128]
            for n in range(LP // 128):
                E1[n * 128 : (n + 1) * 128, pl.ds(pl.multiple_of(h * LP, LP), LP)] = acc[n].T.astype(BF16)
            return 0

        lax.fori_loop(0, M, step, 0)
        acc[...] = jnp.zeros_like(acc)

    const = jnp.zeros((8, M * LP), F32)
    for b in range(M):
        shift = jnp.broadcast_to(pv[b, 2:3, :U], (8, U))
        upper = shift.astype(BF16)
        lower = (shift - upper.astype(F32)).astype(BF16)
        const = const + dot(upper, W2[b]) + dot(lower, W2[b])
    for b in range(M):
        RW[b, 8:9] = const[0:1, b * LP : (b + 1) * LP] + pv[b, 3:4]
    make_e1(m)

    tot = total(ar1, cps1)
    mean = tot[:M] / N
    inv = lax.rsqrt(tot[M:] / N - mean * mean + epsilon)
    for b in range(M):
        RW[b, 9:10] = inv[b : b + 1]
        RW[b, 10:11] = -mean[b : b + 1] * inv[b : b + 1]
    make_cols()
    for cp in cot_all:
        cp.wait()

    def mm2(t, _):
        at = pl.multiple_of(t * TL, TL)
        for b in range(M):
            part = B[b * LP : b * LP + U, pl.ds(at, TL)].astype(F32)
            B[b * LP : b * LP + U, pl.ds(at, TL)] = (part * col[b, :U, 9:10] + col[b, :U, 10:11]).astype(BF16)
        v = dot(E1[:U], B[:, pl.ds(at, TL)]) + col[m, :U, 8:9]
        act, slope = mish_parts(v)
        act2[:, pl.ds(at, TL)] = act.astype(BF16)
        slo2[:, pl.ds(at, TL)] = slope.astype(BF16)
        g = C[t // NT, :, pl.ds(pl.multiple_of(lax.rem(t, NT) * TL, TL), TL)].astype(F32)
        acc[0, :U] += lane_part(act)
        acc[1, :U] += lane_part(act * act)
        acc[2, :U] += lane_part(g)
        acc[3, :U] += lane_part(g * act)
        return 0

    lax.fori_loop(0, M * NT, mm2, 0)
    for s in range(4):
        ar2[d, s : s + 1, :] = row_of(s)
    ar2[d, 4:8, :] = jnp.zeros((4, LP), F32)
    acc[...] = jnp.zeros_like(acc)
    cps2 = all_dp(ar2, a2s, a2r)

    def a_at(base, b):
        return base + b // PER, pl.multiple_of(lax.rem(b, PER) * LP, LP)

    def mm2_own(b):
        make_e1(b)
        act_at, row = a_at(0, b)
        v = dot(E1[:U], B[:, pl.ds(pl.multiple_of(m * Q, Q), Q)]) + col[b, :U, 8:9]
        act, slope = mish_parts(v)
        A[act_at, pl.ds(row, U)] = act.astype(BF16)
        A[act_at + NA, pl.ds(row, U)] = slope.astype(BF16)

    def own_loop(k, _):
        mm2_own(lax.rem(m + k, M))
        return 0

    mm2_own(up[1])
    tot = total(ar2, cps2)
    mean = tot[0:1] / N
    inv = lax.rsqrt(tot[1:2] / N - mean * mean + epsilon)
    sum_g = tot[2:3]
    sum_gn = inv * (tot[3:4] - mean * sum_g)
    k1 = pv[m, 4:5] * inv
    k2 = -k1 * inv * sum_gn / N
    k3 = -k1 * sum_g / N - mean * k2
    ar2z[m, 0:1] = k1
    ar2z[m, 1:2] = k2
    ar2z[m, 2:3] = k3
    ar2z[m, 3:4] = k1
    ar2z[m, 4:5] = pv[m, 5:6] - mean * k1
    ar2z[m, 5:6] = sum_g
    ar2z[m, 6:7] = sum_gn
    ar2z[m, 7:8] = jnp.zeros((1, LP), F32)
    cps2z = [send(ar2z.at[m], ar2z.at[m], a2zs.at[k], a2zr.at[k], (d, up[k])) for k in range(1, M)]
    RW[m, 16:24] = ar2z[m]
    make_col(m)

    def back2(t, _):
        at = pl.multiple_of(t * TL, TL)
        a = act2[:, pl.ds(at, TL)].astype(F32)
        g = C[t // NT, :, pl.ds(pl.multiple_of(lax.rem(t, NT) * TL, TL), TL)].astype(F32)
        grad = (g * col[m, :U, 16:17] + a * col[m, :U, 17:18] + col[m, :U, 18:19]) * slo2[:, pl.ds(at, TL)].astype(F32)
        grad = grad.astype(BF16)
        slo2[:, pl.ds(at, TL)] = grad
        acc[0, :U] += lane_part(grad.astype(F32))
        return 0

    lax.fori_loop(0, M * NT, back2, 0)
    gb2 = row_of(0)
    ar3[d, 2 * M : 2 * M + 1, :] = gb2
    ar3[d, 2 * M + 1 : 2 * M + 8, :] = jnp.zeros((7, LP), F32)
    acc[0:1] = jnp.zeros((1, LP, 128), F32)

    L1 = pl.multiple_of(lax.rem(m + 1, M) * Q, 128)
    LR = pl.multiple_of(L1 + LP, 128)

    def rowsum(x):
        acc[0, :U] = lane_part(x[:, : U // 128 * 128]) + jnp.where(
            lax.broadcasted_iota(I32, (U, 128), 1) >= 128 - U % 128, x[:, U - 128 :], 0.0
        )
        return row_of(0)

    gb2_all8 = jnp.broadcast_to(gb2[:, :U], (8, U))
    gb2_up = gb2_all8.astype(BF16)
    gb2_low = (gb2_all8 - gb2_up.astype(F32)).astype(BF16)
    ar3[d, 0 : 2 * M, :] = jnp.zeros((2 * M, LP), F32)

    def grad_w2(b, _):
        at = pl.multiple_of(b * LP, LP)
        g = dot_nt(B[pl.ds(at, LP), :], slo2[...])
        w16 = W2[b, :, pl.ds(pl.multiple_of(m * LP, LP), LP)][:, :U]
        w = w16.astype(F32)
        ar3[d, pl.ds(b, 1), :U] = dot_nt(gb2_up, w16)[0:1] + dot_nt(gb2_low, w16)[0:1]
        ar3[d, pl.ds(b + M, 1), :] = rowsum(w * g[:U])
        g = g * col[b, :, 1:2] + col[b, :, 2:3] * gb2[:, :U]
        B[pl.ds(at, LP), pl.ds(L1, U)] = g.astype(BF16)
        B[pl.ds(at, LP), pl.ds(L1 + U // 128 * 128, LP - U // 128 * 128)] = jnp.where(
            lax.broadcasted_iota(I32, (LP, LP - U // 128 * 128), 1) < U - U // 128 * 128,
            B[pl.ds(at, LP), pl.ds(L1 + U // 128 * 128, LP - U // 128 * 128)].astype(F32),
            0.0,
        ).astype(BF16)
        return 0

    lax.fori_loop(0, M, grad_w2, 0)
    cps3 = all_dp(ar3, a3s, a3r)
    for n, dev in ((0, core_dev), (1, hi_dev), (2, lo_dev)):
        pl.semaphore_signal(free.at[n], inc=1, device_id=dev, device_id_type=MESH)
    for k in range(1, M):
        pl.semaphore_signal(free.at[2 + k], inc=1, device_id=(d, up[k]), device_id_type=MESH)

    HALF = {0: (1 - c) * 4, 1: 4 * c + 2 * (1 - hi), 2: 4 * c + 2 * hi + 1 - lo}
    KEEP = {0: 4 * c, 1: 4 * c + 2 * hi, 2: p}
    START = {0: 0, 1: 4, 2: 6}
    PARTNER = {0: core_dev, 1: hi_dev, 2: lo_dev}
    g2cp = {}

    def b_rows(b, at, size, lane):
        return B.at[pl.ds(pl.multiple_of(b * LP + at * S8, 16), size * S8), pl.ds(lane, LP)]

    def g2_send(n):
        pl.semaphore_wait(free.at[n], 1)
        for b in range(M):
            g2cp[n, b] = send(
                b_rows(b, HALF[n], 4 >> n, L1), b_rows(b, START[n], 4 >> n, LR), g2s.at[n, b], g2r.at[n, b], PARTNER[n]
            )

    def g2_add(n):
        for b in range(M):
            g2cp[n, b].wait_recv()
            size = (4 >> n) * S8
            keep = pl.ds(pl.multiple_of(b * LP + KEEP[n] * S8, 16), size)
            came = pl.ds(b * LP + START[n] * S8, size)
            B[keep, pl.ds(L1, LP)] = (
                B[keep, pl.ds(L1, LP)].astype(F32) + B[came, pl.ds(LR, LP)].astype(F32)
            ).astype(BF16)

    def l2_of(z):
        return pl.multiple_of(lax.rem(z + 2, M) * Q, 128)

    L2 = l2_of(m)

    if G > 1:
        x1, x2, x1s, x1r, x2s, x2r = extra

    def g2_groups():
        cps = []
        for k in range(1, G):
            to = (lax.rem(d + 8 * k, D), m)
            for b in range(M):
                cps.append(send(b_rows(b, p, 1, L1), x2.at[d // 8, b], x2s.at[k, b], x2r.at[k, b], to))
        for b in range(M):
            x2[d // 8, b] = B[pl.ds(pl.multiple_of(b * LP + p * S8, 16), S8), pl.ds(L1, LP)]
        for cp in cps:
            cp.wait_recv()
        for cp in cps:
            gone(cp)
        for b in range(M):
            v = x2[0, b].astype(F32)
            for k in range(1, G):
                v = v + x2[k, b].astype(F32)
            B[pl.ds(pl.multiple_of(b * LP + p * S8, 16), S8), pl.ds(L1, LP)] = v.astype(BF16)

    def g2_z():
        if G > 1:
            g2_groups()
        for k in range(1, M):
            pl.semaphore_wait(free.at[2 + M - k], 1)
            g2cp[3, k] = send(
                b_rows(up[k], p, 1, L1),
                B.at[pl.ds(pl.multiple_of(m * LP + p * S8, 16), S8), pl.ds(l2_of(up[k]), LP)],
                g2s.at[3, k], g2r.at[3, k], (d, up[k]),
            )
        mine = pl.ds(pl.multiple_of(m * LP + p * S8, 16), S8)
        B[mine, pl.ds(L2, LP)] = B[mine, pl.ds(L1, LP)]

    def g2_gather(n):
        at, size, dev = {4: (p, 1, lo_dev), 5: (4 * c + 2 * hi, 2, hi_dev), 6: (4 * c, 4, core_dev)}[n]
        if n == 4:
            for k in range(1, M):
                g2cp[3, k].wait_recv()
        else:
            for b in range(M):
                g2cp[n - 1, b].wait_recv()
        for b in range(M):
            part = b_rows(b, at, size, L2)
            g2cp[n, b] = send(part, part, g2s.at[n, b], g2r.at[n, b], dev)

    g2_send(0)
    lax.fori_loop(2, M, own_loop, 0)
    tot = total(ar3, cps3)
    ar3z[m] = tot[: 2 * M]
    gb2_all = tot[2 * M : 2 * M + 1]
    cps3z = [send(ar3z.at[m], ar3z.at[m], a3zs.at[k], a3zr.at[k], (d, up[k])) for k in range(1, M)]
    g2_add(0)
    g2_send(1)
    encode(m, to_e1)
    for cp in cps2z:
        cp.wait_recv()
    for b in range(M):
        RW[b, 16:24] = ar2z[b]
    for cp in cps3z:
        cp.wait_recv()
    tot = ar3z[0]
    for b in range(1, M):
        tot = tot + ar3z[b]
    for b in range(M):
        k1 = pv[b, 1:2] * RW[b, 9:10]
        RW[b, 24:25] = k1
        RW[b, 25:26] = -k1 * tot[M + b : M + b + 1] / N
        RW[b, 26:27] = -k1 * tot[b : b + 1] / N
    make_cols()
    pick = lax.broadcasted_iota(I32, (2 * M, 1), 0)
    vec_ref[0:1, :] = jnp.zeros((1, LP), F32)
    vec_ref[1:2, :] = jnp.sum(jnp.where(pick == M + m, tot, 0.0), axis=0, keepdims=True)
    vec_ref[2:3, :] = jnp.sum(jnp.where(pick == m, tot, 0.0), axis=0, keepdims=True)
    vec_ref[3:4, :] = gb2_all
    vec_ref[4:5, :] = ar2z[m, 6:7]
    vec_ref[5:6, :] = ar2z[m, 5:6]
    vec_ref[6:8, :] = jnp.zeros((2, LP), F32)

    PADAT = U // 16 * 16

    def put_grad(b, value, at, size):
        slot, row = a_at(NA, b)
        A[slot, pl.ds(row, U), pl.ds(at, size)] = value

    for b in range(M):
        slot, row = NA + b // PER, (b % PER) * LP
        A[slot, row + PADAT : row + LP, :] = jnp.where(
            lax.broadcasted_iota(I32, (LP - PADAT, Q), 0) < U - PADAT,
            A[slot, row + PADAT : row + LP, :].astype(F32),
            0.0,
        ).astype(BF16)
    cot_loc.wait()

    def back2_own(b):
        act_at, row = a_at(0, b)

        def step(t, _):
            at = pl.multiple_of(t * TL, TL)
            a = A[act_at, pl.ds(row, U), pl.ds(at, TL)].astype(F32)
            s = A[act_at + NA, pl.ds(row, U), pl.ds(at, TL)].astype(F32)
            g = F[b, :, pl.ds(at, TL)].astype(F32)
            grad = (g * col[b, :U, 16:17] + a * col[b, :U, 17:18] + col[b, :U, 18:19]) * s
            A[act_at + NA, pl.ds(row, U), pl.ds(at, TL)] = grad.astype(BF16)
            return 0

        lax.fori_loop(0, NT, step, 0)

    def copy_own(t, _):
        at = pl.multiple_of(t * TL, TL)
        put_grad(m, slo2[:, pl.ds(pl.multiple_of(m * Q + t * TL, TL), TL)], at, TL)
        return 0

    lax.fori_loop(0, NT, copy_own, 0)
    for k in range(1, M):
        ct[k].wait_recv()
        back2_own(down[k])

    g2_add(1)
    g2_send(2)

    def back1(b):
        dh = dot(W2[b, :, 0:K], A[NA])
        for n in range(1, NA):
            dh = dh + dot(W2[b, :, n * K : (n + 1) * K], A[NA + n])
        norm = B[pl.ds(pl.multiple_of(b * LP, LP), U), pl.ds(pl.multiple_of(m * Q, Q), Q)].astype(F32)
        grad = dh * col[b, :U, 24:25] + norm * col[b, :U, 25:26] + col[b, :U, 26:27]
        grad = (grad * H[b].astype(F32)).astype(BF16)
        H[b] = grad
        acc[0, :U] += lane_part(grad.astype(F32))
        ar4[d, pl.ds(b, 1), :] = row_of(0)
        acc[0:1] = jnp.zeros((1, LP, 128), F32)

        def mm(t, _):
            F[b, :, pl.ds(pl.multiple_of(t * LP, LP), LP)] = dot_nt(
                H[b], E1[:, pl.ds(pl.multiple_of(t * Q, Q), Q)]
            ).astype(BF16)
            return 0

        lax.fori_loop(0, PER, mm, 0)

    acc[0:1] = jnp.zeros((1, LP, 128), F32)
    ar4[d] = jnp.zeros((ar4.shape[1], LP), F32)
    K2 = 4 * K8
    FROM = {0: 0, 1: K2, 2: K2 + 2 * K8}
    order = [up[(j + 1) % M] for j in range(M)]
    g1cp = {}

    def g1_send(n, j):
        b = order[j]
        g1cp[n, j] = send(
            lanes(F.at[b], HALF[n] * K8, K2 >> n), lanes(C.at[b], FROM[n], K2 >> n), g1s.at[n, j], g1r.at[n, j], PARTNER[n]
        )

    def g1_add(n, j):
        b = order[j]
        g1cp[n, j].wait_recv()
        keep = pl.ds(pl.multiple_of(KEEP[n] * K8, 128), K2 >> n)
        F[b, :, keep] = (F[b, :, keep].astype(F32) + C[b, :, FROM[n] : FROM[n] + (K2 >> n)].astype(F32)).astype(BF16)

    def g1_groups(j):
        b = order[j]
        mine = pl.ds(pl.multiple_of(p * K8, 128), K8)
        cps = []
        for k in range(1, G):
            to = (lax.rem(d + 8 * k, D), m)
            cps.append(send(lanes(F.at[b], p * K8, K8), x1.at[d // 8, j], x1s.at[k, j], x1r.at[k, j], to))
        x1[d // 8, j] = F[b, :, mine]
        for cp in cps:
            cp.wait_recv()
        for cp in cps:
            gone(cp)
        v = x1[0, j].astype(F32)
        for k in range(1, G):
            v = v + x1[k, j].astype(F32)
        F[b, :, mine] = v.astype(BF16)

    def g1_z(j):
        if G > 1:
            g1_groups(j)
        b, k = order[j], (j + 1) % M
        if k:
            g1cp[3, j] = send(
                lanes(F.at[b], p * K8, K8), C.at[m, :, pl.ds(K - K8, K8)], g1s.at[3, k], g1r.at[3, k], (d, b)
            )
        else:
            C[m, :, K - K8 : K] = F[m, :, pl.ds(pl.multiple_of(p * K8, 128), K8)]

    def g1_stage(n, j):
        if 0 <= j < M:
            g1_add(n - 1, j)
            if n < 3:
                g1_send(n, j)
            else:
                g1_z(j)

    for j in range(M + 3):
        if j < M:
            back1(order[j])
            g1_send(0, j)
        if j == M - 1:
            cps4 = all_dp(ar4, a4s, a4r)
        g1_stage(3, j - 3)
        g1_stage(2, j - 2)
        g1_stage(1, j - 1)
        if j == 1:
            g2_add(2)
            g2_z()
        if j == 2:
            g2_gather(4)
        if j == 3:
            g2_gather(5)
        if j == 4:
            g2_gather(6)
        if j == M - 1:

            def finish(t, _):
                at = pl.multiple_of(t * TL, TL)
                a = act2[:, pl.ds(at, TL)].astype(F32)
                act2[:, pl.ds(at, TL)] = (a * col[m, :U, 19:20] + col[m, :U, 20:21]).astype(BF16)
                return 0

            lax.fori_loop(0, M * NT, finish, 0)
            out_copy = pltpu.make_async_copy(act2, out_ref, loc.at[0])
            out_copy.start()
        if j == M:
            tot4 = total(ar4, cps4)
            for b in range(M):
                ar4s[b] = jnp.broadcast_to(tot4[b : b + 1], (8, LP))
            ar4z[m] = ar4s[m]
            cps4z = [send(ar4s.at[up[k]], ar4z.at[m], a4zs.at[k], a4zr.at[k], (d, up[k])) for k in range(1, M)]
    for b in range(M):
        g2cp[6, b].wait_recv()
    for b in range(M):
        slo2[:, b * U : (b + 1) * U] = B[b * LP : b * LP + U, pl.ds(L2, LP)][:, :U]
    gw2_copy = pltpu.make_async_copy(lanes(slo2, 0, gw2_ref.shape[1]), gw2_ref, loc.at[2])
    gw2_copy.start()
    for j in range(M - 1):
        g1cp[3, j].wait_recv()
    v = C[0, :, K - K8 : K].astype(F32)
    for b in range(1, M):
        v = v + C[b, :, K - K8 : K].astype(F32)
    G1[:, pl.ds(pl.multiple_of(p * K8, 128), K8)] = v.astype(BF16)
    ga = send(lanes(G1, p * K8, K8), lanes(G1, p * K8, K8), g1s.at[4, 0], g1r.at[4, 0], lo_dev)
    ga.wait_recv()
    part = lanes(G1, (4 * c + 2 * hi) * K8, 2 * K8)
    ga = send(part, part, g1s.at[4, 1], g1r.at[4, 1], hi_dev)
    ga.wait_recv()
    part = lanes(G1, 4 * c * K8, K2)
    ga = send(part, part, g1s.at[4, 2], g1r.at[4, 2], core_dev)
    for cp in cps4z:
        cp.wait_recv()
    v = ar4z[0]
    for b in range(1, M):
        v = v + ar4z[b]
    vec_ref[0:1, :] = v[0:1]
    ga.wait_recv()
    gw1_copy = pltpu.make_async_copy(lanes(G1, 0, K), gw1_ref, loc.at[1])
    gw1_copy.start()
    out_copy.wait()
    gw1_copy.wait()
    gw2_copy.wait()
    for cp in sent:
        cp.wait_send()


def per_device(ids, hash_mult, hash_add, w1, b1, s1, t1, w2, b2, s2, t2, cot):
    D, M = lax.axis_size("dp"), lax.axis_size("mp")
    U, K = w1.shape
    R = ids.shape[0]
    Q = R // M
    LP = -(-U // 128) * 128
    G = D // 8
    par = jnp.pad(jnp.stack([b1, s1, t1, b2, s2, t2]), ((0, 2), (0, LP - U)))
    dma = pltpu.SemaphoreType.DMA
    vmem = pl.BlockSpec(memory_space=pltpu.VMEM)
    hbm = pl.BlockSpec(memory_space=pl.ANY)
    AR = -(-2 * M // 8) * 8
    scratch = [
        pltpu.VMEM((M, K, Q), BF16),
        pltpu.VMEM((M * LP, R), BF16),
        pltpu.VMEM((M, U, max(K, Q)), BF16),
        pltpu.VMEM((M, U, M * LP), BF16),
        pltpu.VMEM((U, max(K, M * U)), BF16),
        pltpu.VMEM((LP, M * LP), BF16),
        pltpu.VMEM((M, U, max(K, Q)), BF16),
        pltpu.VMEM((M, U, Q), BF16),
        pltpu.VMEM((U, R), BF16),
        pltpu.VMEM((U, R), BF16),
        pltpu.VMEM((M, LP, 128), F32),
        pltpu.VMEM((M, 32, LP), F32),
        pltpu.VMEM((4, LP, 128), F32),
        pltpu.VMEM((K, 128), F32),
        pltpu.VMEM((M, 8, LP), F32),
        pltpu.VMEM((D, AR, LP), F32),
        pltpu.VMEM((D, 8, LP), F32),
        pltpu.VMEM((M, 8, LP), F32),
        pltpu.VMEM((D, AR + 8, LP), F32),
        pltpu.VMEM((M, AR, LP), F32),
        pltpu.VMEM((D, 8, LP), F32),
        pltpu.VMEM((M, 8, LP), F32),
        pltpu.VMEM((M, 8, LP), F32),
        dma((4, M)), dma((4, M)), dma((4, M)), dma((4, M)),
        dma((M,)), dma((M,)), dma((M,)), dma((M,)), dma((3 + M,)),
        dma((D,)), dma((D,)), dma((D,)), dma((D,)), dma((M,)), dma((M,)),
        dma((D,)), dma((D,)), dma((M,)), dma((M,)), dma((D,)), dma((D,)), dma((M,)), dma((M,)),
        dma((5, M)), dma((5, M)), dma((7, M)), dma((7, M)), pltpu.SemaphoreType.REGULAR((2 + M,)),
    ]
    if G > 1:
        scratch += [
            pltpu.VMEM((G, M, U, K // 8), BF16),
            pltpu.VMEM((G, M, LP // 8, LP), BF16),
            dma((G, M)), dma((G, M)), dma((G, M)), dma((G, M)),
        ]
    out, gw1, gw2, vec = pl.pallas_call(
        functools.partial(kernel, D, M, U, LP, K, R),
        out_shape=[
            jax.ShapeDtypeStruct((U, R), BF16),
            jax.ShapeDtypeStruct((U, K), BF16),
            jax.ShapeDtypeStruct((U, -(-M * U // 128) * 128), BF16),
            jax.ShapeDtypeStruct((8, LP), F32),
        ],
        in_specs=[vmem] * 4 + [hbm, hbm, hbm],
        out_specs=[hbm, hbm, hbm, vmem],
        scratch_shapes=scratch,
        compiler_params=pltpu.CompilerParams(
            collective_id=0, has_side_effects=True, vmem_limit_bytes=64 * 2**20 - 2**18
        ),
    )(ids[None, :], hash_mult[None, :], hash_add[None, :], par, w1, w2, cot)
    v = vec[:, :U]
    return (out, gw1.astype(F32), v[0], v[1], v[2], gw2[:, : M * U].astype(F32), v[3], v[4], v[5])


def solution(mesh):
    return jax.shard_map(
        per_device,
        mesh=mesh,
        in_specs=(
            P("dp"), P(), P(), P("mp", None), P("mp"), P("mp"), P("mp"),
            P("mp", None), P("mp"), P("mp"), P("mp"), P("mp", "dp"),
        ),
        out_specs=(
            P("mp", "dp"), P("mp", None), P("mp"), P("mp"), P("mp"),
            P("mp", None), P("mp"), P("mp"), P("mp"),
        ),
        check_vma=False,
    )
```

```python
import functools

import jax
import jax.numpy as jnp
from jax import lax
from jax.experimental import pallas as pl
from jax.experimental.pallas import tpu as pltpu
from jax.sharding import PartitionSpec as P

MESH = pl.DeviceIdType.MESH
F32, BF16, I32 = jnp.float32, jnp.bfloat16, jnp.int32
epsilon = 1e-05


def dot(a, b):
    return lax.dot_general(a, b, (((1,), (0,)), ((), ())), preferred_element_type=F32)


def dot_nt(a, b):
    return lax.dot_general(a, b, (((1,), (1,)), ((), ())), preferred_element_type=F32)


def mish_parts(v):
    u = jnp.exp(jnp.minimum(v, 20.0))
    n = u * (u + 2.0)
    d = n + 2.0
    r = pl.reciprocal(d, approx=True)
    t = n * r
    return v * t, t + v * ((4.0 * (n - u) * r) * r)


def mish(v):
    u = jnp.exp(jnp.minimum(v, 20.0))
    n = u * (u + 2.0)
    d = n + 2.0
    r = pl.reciprocal(d, approx=True)
    return v * (n * r)


def lane_part(x):
    out = x[:, :128]
    for at in range(128, x.shape[1], 128):
        out = out + x[:, at : at + 128]
    return out


def kernel(
    D, M, U, LP, K, R,
    ids_ref, mult_ref, add_ref, par_ref, w1_ref, w2_ref, cot_ref,
    out_ref, gw1_ref, gw2_ref, vec_ref,
    A, B, C, W2, G1, E1, F, H, act2, slo2, col, RW, acc, hcol,
    pv, ar1, ar2, ar2z, ar3, ar3z, ar4, ar4s, ar4z,
    w1s, w1r, w2s, w2r, pvs, pvr, cts, ctr, loc,
    a1s, a1r, a2s, a2r, a2zs, a2zr, a3s, a3r, a3zs, a3zr, a4s, a4r, a4zs, a4zr,
    g1s, g1r, g2s, g2r, free, *extra,
):
    Q = R // M
    G = D // 8
    TL = min(512, Q)
    NT = Q // TL
    PER = K // LP
    NA = M // PER
    K8 = K // 8
    J8 = M * LP // 8
    S8 = LP // 8
    N = float(R * D)
    d = lax.axis_index("dp")
    m = lax.axis_index("mp")
    i = lax.rem(d, 8)
    c = lax.rem(i, 2)
    x = lax.rem(i // 2, 2)
    y = i // 4
    hi = (1 - c) * x + c * y
    lo = (1 - c) * y + c * x
    p = 4 * c + 2 * hi + lo
    core_dev = (d + 1 - 2 * c, m)
    flip_x = d + 2 - 4 * x
    flip_y = d + 4 - 8 * y
    hi_dev = ((1 - c) * flip_x + c * flip_y, m)
    lo_dev = ((1 - c) * flip_y + c * flip_x, m)
    up = [lax.rem(m + k, M) for k in range(M)]
    down = [lax.rem(m - k + M, M) for k in range(M)]
    others = [lax.rem(d + k, D) for k in range(D)]
    sent = []

    def remote(src, dst, ss, rs, dev):
        cp = pltpu.make_async_remote_copy(
            src_ref=src, dst_ref=dst, send_sem=ss, recv_sem=rs, device_id=dev, device_id_type=MESH
        )
        return cp

    def send(src, dst, ss, rs, dev):
        cp = remote(src, dst, ss, rs, dev)
        cp.start()
        sent.append(cp)
        return cp

    def gone(cp):
        cp.wait_send()
        sent[:] = [other for other in sent if other is not cp]

    def lanes(ref, at, size):
        return ref.at[:, pl.ds(pl.multiple_of(at, 128), size)]

    def rows(ref, at, size):
        return ref.at[pl.ds(pl.multiple_of(at, 16), size)]

    bar = pltpu.get_barrier_semaphore()
    greeted = [core_dev, hi_dev, lo_dev] if G == 1 else [(others[k], m) for k in range(1, D)]
    greeted += [(d, up[k]) for k in range(1, M)]
    for dev in greeted:
        pl.semaphore_signal(bar, inc=1, device_id=dev, device_id_type=MESH)

    w2_loc = pltpu.make_async_copy(w2_ref, G1, loc.at[1])
    w2_loc.start()
    w1_loc = pltpu.make_async_copy(w1_ref, C.at[m], loc.at[0])
    w1_loc.start()
    cot_loc = pltpu.make_async_copy(lanes(cot_ref, m * Q, Q), lanes(F.at[m], 0, Q), loc.at[2])
    pv[m] = par_ref[...]
    pl.semaphore_wait(bar, len(greeted))

    ag1, ag2, agp, ct = {}, {}, {}, {}
    for k in range(1, M):
        agp[k] = send(par_ref, pv.at[m], pvs.at[k], pvr.at[k], (d, up[k]))
    for ag, own, buf, size, ss, rs in ((ag1, w1_ref, C, K8, w1s, w1r), (ag2, None, W2, J8, w2s, w2r)):
        for k in range(1, M):
            part = lanes(buf.at[m], p * size, size)
            mine = part if own is None else lanes(own, p * size, size)
            ag[0, k] = remote(mine, part, ss.at[0, k], rs.at[0, k], (d, up[k]))
            for step, dev, at, width in (
                (1, lo_dev, p, 1), (2, hi_dev, 4 * c + 2 * hi, 2), (3, core_dev, 4 * c, 4)
            ):
                part = lanes(buf.at[down[k]], at * size, width * size)
                ag[step, k] = remote(part, part, ss.at[step, k], rs.at[step, k], dev)
    for k in range(1, M):
        ag1[0, k].start()
    w2_loc.wait()
    for b in range(M):
        W2[m, :, (b + 1) * LP - 128 : (b + 1) * LP] = jnp.zeros((U, 128), BF16)
        W2[m, :, b * LP : b * LP + U] = G1[:, b * U : (b + 1) * U]

    def gather_stage(step, ag):
        for k in range(1, M):
            ag[step - 1, k].wait_recv()
            ag[step, k].start()

    def stage1(step):
        gather_stage(step, ag1)

    def stage2(step):
        gather_stage(step, ag2)

    hrow = jnp.concatenate(
        [mult_ref[...].astype(F32), add_ref[...].astype(F32), jnp.zeros((126, K), F32)], axis=0
    )
    hcol[...] = hrow.T

    HT = 128

    def encode(q, put):
        def step(t, _):
            at = pl.multiple_of(t * HT, HT)
            both = hcol[pl.ds(at, HT), :].astype(I32)
            v = both[:, 0:1] * ids_ref[:, pl.ds(pl.multiple_of(q * Q, 128), Q)] + both[:, 1:2]
            for _ in range(2):
                top = lax.shift_right_logical(v, 16)
                v = (v & 65535) + ((top << 4) - top)
            v = jnp.where(v >= 65521, v - 65521, v)
            put(t, (v.astype(F32) * (2.0 / 65520.0) - 1.0).astype(BF16))
            return 0

        lax.fori_loop(0, K // HT, step, 0)

    def make_col(b):
        col[b] = jnp.concatenate([RW[b], jnp.zeros((128 - RW.shape[1], LP), F32)], axis=0).T

    def make_cols():
        def step(b, _):
            make_col(b)
            return 0

        lax.fori_loop(0, M, step, 0)

    def to_a(q):
        def put(t, value):
            A[q, pl.ds(pl.multiple_of(t * HT, HT), HT), :] = value

        return put

    def to_e1(t, value):
        E1[pl.ds(pl.multiple_of(lax.rem(t, LP // HT) * HT, HT), HT), pl.ds(pl.multiple_of(t // (LP // HT) * Q, 128), Q)] = value

    def row_of(slot):
        return jnp.sum(acc[slot].T, axis=0, keepdims=True)

    acc[...] = jnp.zeros_like(acc)
    for b in range(M):
        B[pl.ds(b * LP + U // 16 * 16, LP - U // 16 * 16), :] = jnp.zeros((LP - U // 16 * 16, R), BF16)

    RW[...] = jnp.zeros_like(RW)
    RW[m, 0:8] = par_ref[...]
    make_col(m)
    encode(m, to_a(m))
    w1_loc.wait()

    def mm1_own(b):
        def step(t, _):
            at = pl.multiple_of(t * TL, TL)
            act, slope = mish_parts(dot(C[b], A[m, :, pl.ds(at, TL)]) + col[b, :U, 0:1])
            H[b, :, pl.ds(at, TL)] = slope.astype(BF16)
            B[pl.ds(pl.multiple_of(b * LP, LP), U), pl.ds(pl.multiple_of(m * Q + t * TL, TL), TL)] = act.astype(BF16)
            acc[0, :U] += lane_part(act)
            acc[1, :U] += lane_part(act * act)
            return 0

        lax.fori_loop(0, NT, step, 0)

    def mm1_rest(b):
        def step(t, _):
            q = lax.rem(m + t, M)
            act = mish(dot(C[b], A[q]) + col[b, :U, 0:1])
            B[pl.ds(pl.multiple_of(b * LP, LP), U), pl.ds(pl.multiple_of(q * Q, Q), Q)] = act.astype(BF16)
            acc[0, :U] += lane_part(act)
            acc[1, :U] += lane_part(act * act)
            return 0

        lax.fori_loop(1, M, step, 0)

    def mm1_sums(b):
        ar1[d, pl.ds(b, 1), :] = row_of(0)
        ar1[d, pl.ds(b + M, 1), :] = row_of(1)
        acc[0:2] = jnp.zeros((2, LP, 128), F32)

    mm1_own(m)
    stage1(1)
    for k in range(1, M):
        ag2[0, k].start()

    def enc_step(k, _):
        q = lax.rem(m + M - k, M)
        encode(q, to_a(q))
        return 0

    lax.fori_loop(1, M, enc_step, 0)
    stage1(2)
    mm1_rest(m)
    mm1_sums(m)
    stage2(1)
    cot_loc.start()
    for q in range(1, M):
        ct[q] = send(
            lanes(cot_ref, up[q] * Q, Q), lanes(F.at[m], 0, Q), cts.at[q], ctr.at[q], (d, up[q])
        )
    stage1(3)
    for k in range(1, M):
        agp[k].wait_recv()
    for b in range(M):
        RW[b, 0:8] = pv[b]
    make_cols()
    def mm1_other(k, _):
        b = lax.rem(m + M - k, M)
        part = lanes(C.at[b], 4 * c * K8, 4 * K8)
        remote(part, part, w1s.at[3, k], w1r.at[3, k], core_dev).wait_recv()
        mm1_own(b)
        mm1_rest(b)
        mm1_sums(b)
        pl.when(k == 1)(functools.partial(stage2, 2))
        return 0

    lax.fori_loop(1, M, mm1_other, 0)

    def all_dp(buf, ss, rs):
        cps = []
        for k in range(1, D):
            cps.append(send(buf.at[d], buf.at[d], ss.at[k], rs.at[k], (others[k], m)))
        return cps

    def total(buf, cps):
        for cp in cps:
            cp.wait_recv()
        out = buf[0]
        for k in range(1, D):
            out = out + buf[k]
        return out

    cps1 = all_dp(ar1, a1s, a1r)
    stage2(3)
    for cp in ag1.values():
        cp.wait_send()
    cot_all = []
    for q in range(M):
        cp = pltpu.make_async_copy(lanes(cot_ref, q * Q, Q), lanes(C.at[q], 0, Q), loc.at[3 + q])
        cot_all.append(cp)
        cp.start()
    for k in range(1, M):
        ag2[3, k].wait_recv()

    def make_e1(b):
        def step(h, _):
            part = W2[h, :, pl.ds(pl.multiple_of(b * LP, LP), LP)].astype(F32) * col[h, :U, 1:2]
            for n in range(LP // 128):
                acc[n, :U] = part[:, n * 128 : (n + 1) * 128]
            for n in range(LP // 128):
                E1[n * 128 : (n + 1) * 128, pl.ds(pl.multiple_of(h * LP, LP), LP)] = acc[n].T.astype(BF16)
            return 0

        lax.fori_loop(0, M, step, 0)
        acc[...] = jnp.zeros_like(acc)

    const = jnp.zeros((8, M * LP), F32)
    for b in range(M):
        shift = jnp.broadcast_to(pv[b, 2:3, :U], (8, U))
        upper = shift.astype(BF16)
        lower = (shift - upper.astype(F32)).astype(BF16)
        const = const + dot(upper, W2[b]) + dot(lower, W2[b])
    for b in range(M):
        RW[b, 8:9] = const[0:1, b * LP : (b + 1) * LP] + pv[b, 3:4]
    make_e1(m)

    tot = total(ar1, cps1)
    mean = tot[:M] / N
    inv = lax.rsqrt(tot[M:] / N - mean * mean + epsilon)
    for b in range(M):
        RW[b, 9:10] = inv[b : b + 1]
        RW[b, 10:11] = -mean[b : b + 1] * inv[b : b + 1]
    make_cols()
    for cp in cot_all:
        cp.wait()

    def mm2(t, _):
        at = pl.multiple_of(t * TL, TL)
        for b in range(M):
            part = B[b * LP : b * LP + U, pl.ds(at, TL)].astype(F32)
            B[b * LP : b * LP + U, pl.ds(at, TL)] = (part * col[b, :U, 9:10] + col[b, :U, 10:11]).astype(BF16)
        v = dot(E1[:U], B[:, pl.ds(at, TL)]) + col[m, :U, 8:9]
        act, slope = mish_parts(v)
        act2[:, pl.ds(at, TL)] = act.astype(BF16)
        slo2[:, pl.ds(at, TL)] = slope.astype(BF16)
        g = C[t // NT, :, pl.ds(pl.multiple_of(lax.rem(t, NT) * TL, TL), TL)].astype(F32)
        acc[0, :U] += lane_part(act)
        acc[1, :U] += lane_part(act * act)
        acc[2, :U] += lane_part(g)
        acc[3, :U] += lane_part(g * act)
        return 0

    lax.fori_loop(0, M * NT, mm2, 0)
    for s in range(4):
        ar2[d, s : s + 1, :] = row_of(s)
    ar2[d, 4:8, :] = jnp.zeros((4, LP), F32)
    acc[...] = jnp.zeros_like(acc)
    cps2 = all_dp(ar2, a2s, a2r)

    def a_at(base, b):
        return base + b // PER, pl.multiple_of(lax.rem(b, PER) * LP, LP)

    def mm2_own(b):
        make_e1(b)
        act_at, row = a_at(0, b)
        v = dot(E1[:U], B[:, pl.ds(pl.multiple_of(m * Q, Q), Q)]) + col[b, :U, 8:9]
        act, slope = mish_parts(v)
        A[act_at, pl.ds(row, U)] = act.astype(BF16)
        A[act_at + NA, pl.ds(row, U)] = slope.astype(BF16)

    def own_loop(k, _):
        mm2_own(lax.rem(m + k, M))
        return 0

    mm2_own(up[1])
    tot = total(ar2, cps2)
    mean = tot[0:1] / N
    inv = lax.rsqrt(tot[1:2] / N - mean * mean + epsilon)
    sum_g = tot[2:3]
    sum_gn = inv * (tot[3:4] - mean * sum_g)
    k1 = pv[m, 4:5] * inv
    k2 = -k1 * inv * sum_gn / N
    k3 = -k1 * sum_g / N - mean * k2
    ar2z[m, 0:1] = k1
    ar2z[m, 1:2] = k2
    ar2z[m, 2:3] = k3
    ar2z[m, 3:4] = k1
    ar2z[m, 4:5] = pv[m, 5:6] - mean * k1
    ar2z[m, 5:6] = sum_g
    ar2z[m, 6:7] = sum_gn
    ar2z[m, 7:8] = jnp.zeros((1, LP), F32)
    cps2z = [send(ar2z.at[m], ar2z.at[m], a2zs.at[k], a2zr.at[k], (d, up[k])) for k in range(1, M)]
    RW[m, 16:24] = ar2z[m]
    make_col(m)

    def back2(t, _):
        at = pl.multiple_of(t * TL, TL)
        a = act2[:, pl.ds(at, TL)].astype(F32)
        g = C[t // NT, :, pl.ds(pl.multiple_of(lax.rem(t, NT) * TL, TL), TL)].astype(F32)
        grad = (g * col[m, :U, 16:17] + a * col[m, :U, 17:18] + col[m, :U, 18:19]) * slo2[:, pl.ds(at, TL)].astype(F32)
        grad = grad.astype(BF16)
        slo2[:, pl.ds(at, TL)] = grad
        acc[0, :U] += lane_part(grad.astype(F32))
        return 0

    lax.fori_loop(0, M * NT, back2, 0)
    gb2 = row_of(0)
    ar3[d, 2 * M : 2 * M + 1, :] = gb2
    ar3[d, 2 * M + 1 : 2 * M + 8, :] = jnp.zeros((7, LP), F32)
    acc[0:1] = jnp.zeros((1, LP, 128), F32)

    L1 = pl.multiple_of(lax.rem(m + 1, M) * Q, 128)
    LR = pl.multiple_of(L1 + LP, 128)

    def rowsum(x):
        acc[0, :U] = lane_part(x[:, : U // 128 * 128]) + jnp.where(
            lax.broadcasted_iota(I32, (U, 128), 1) >= 128 - U % 128, x[:, U - 128 :], 0.0
        )
        return row_of(0)

    gb2_all8 = jnp.broadcast_to(gb2[:, :U], (8, U))
    gb2_up = gb2_all8.astype(BF16)
    gb2_low = (gb2_all8 - gb2_up.astype(F32)).astype(BF16)
    ar3[d, 0 : 2 * M, :] = jnp.zeros((2 * M, LP), F32)

    def grad_w2(b, _):
        at = pl.multiple_of(b * LP, LP)
        g = dot_nt(B[pl.ds(at, LP), :], slo2[...])
        w16 = W2[b, :, pl.ds(pl.multiple_of(m * LP, LP), LP)][:, :U]
        w = w16.astype(F32)
        ar3[d, pl.ds(b, 1), :U] = dot_nt(gb2_up, w16)[0:1] + dot_nt(gb2_low, w16)[0:1]
        ar3[d, pl.ds(b + M, 1), :] = rowsum(w * g[:U])
        g = g * col[b, :, 1:2] + col[b, :, 2:3] * gb2[:, :U]
        B[pl.ds(at, LP), pl.ds(L1, U)] = g.astype(BF16)
        B[pl.ds(at, LP), pl.ds(L1 + U // 128 * 128, LP - U // 128 * 128)] = jnp.where(
            lax.broadcasted_iota(I32, (LP, LP - U // 128 * 128), 1) < U - U // 128 * 128,
            B[pl.ds(at, LP), pl.ds(L1 + U // 128 * 128, LP - U // 128 * 128)].astype(F32),
            0.0,
        ).astype(BF16)
        return 0

    lax.fori_loop(0, M, grad_w2, 0)
    cps3 = all_dp(ar3, a3s, a3r)
    for n, dev in ((0, core_dev), (1, hi_dev), (2, lo_dev)):
        pl.semaphore_signal(free.at[n], inc=1, device_id=dev, device_id_type=MESH)
    for k in range(1, M):
        pl.semaphore_signal(free.at[2 + k], inc=1, device_id=(d, up[k]), device_id_type=MESH)

    HALF = {0: (1 - c) * 4, 1: 4 * c + 2 * (1 - hi), 2: 4 * c + 2 * hi + 1 - lo}
    KEEP = {0: 4 * c, 1: 4 * c + 2 * hi, 2: p}
    START = {0: 0, 1: 4, 2: 6}
    PARTNER = {0: core_dev, 1: hi_dev, 2: lo_dev}
    g2cp = {}

    def b_rows(b, at, size, lane):
        return B.at[pl.ds(pl.multiple_of(b * LP + at * S8, 16), size * S8), pl.ds(lane, LP)]

    def g2_send(n):
        pl.semaphore_wait(free.at[n], 1)
        for b in range(M):
            g2cp[n, b].start()

    def g2_add(n):
        for b in range(M):
            g2cp[n, b].wait_recv()
            size = (4 >> n) * S8
            keep = pl.ds(pl.multiple_of(b * LP + KEEP[n] * S8, 16), size)
            came = pl.ds(b * LP + START[n] * S8, size)
            B[keep, pl.ds(L1, LP)] = (
                B[keep, pl.ds(L1, LP)].astype(F32) + B[came, pl.ds(LR, LP)].astype(F32)
            ).astype(BF16)

    def l2_of(z):
        return pl.multiple_of(lax.rem(z + 2, M) * Q, 128)

    L2 = l2_of(m)
    for b in range(M):
        for n in range(3):
            g2cp[n, b] = remote(
                b_rows(b, HALF[n], 4 >> n, L1), b_rows(b, START[n], 4 >> n, LR), g2s.at[n, b], g2r.at[n, b], PARTNER[n]
            )
        for n, at, size, dev in ((4, p, 1, lo_dev), (5, 4 * c + 2 * hi, 2, hi_dev), (6, 4 * c, 4, core_dev)):
            part = b_rows(b, at, size, L2)
            g2cp[n, b] = remote(part, part, g2s.at[n, b], g2r.at[n, b], dev)
        if b:
            g2cp[3, b] = remote(
                b_rows(up[b], p, 1, L1),
                B.at[pl.ds(pl.multiple_of(m * LP + p * S8, 16), S8), pl.ds(l2_of(up[b]), LP)],
                g2s.at[3, b], g2r.at[3, b], (d, up[b]),
            )

    if G > 1:
        x1, x2, x1s, x1r, x2s, x2r = extra

    def g2_groups():
        cps = []
        for k in range(1, G):
            to = (lax.rem(d + 8 * k, D), m)
            for b in range(M):
                cps.append(send(b_rows(b, p, 1, L1), x2.at[d // 8, b], x2s.at[k, b], x2r.at[k, b], to))
        for b in range(M):
            x2[d // 8, b] = B[pl.ds(pl.multiple_of(b * LP + p * S8, 16), S8), pl.ds(L1, LP)]
        for cp in cps:
            cp.wait_recv()
        for cp in cps:
            gone(cp)
        for b in range(M):
            v = x2[0, b].astype(F32)
            for k in range(1, G):
                v = v + x2[k, b].astype(F32)
            B[pl.ds(pl.multiple_of(b * LP + p * S8, 16), S8), pl.ds(L1, LP)] = v.astype(BF16)

    def g2_z():
        if G > 1:
            g2_groups()
        for k in range(1, M):
            pl.semaphore_wait(free.at[2 + M - k], 1)
            g2cp[3, k].start()
        mine = pl.ds(pl.multiple_of(m * LP + p * S8, 16), S8)
        B[mine, pl.ds(L2, LP)] = B[mine, pl.ds(L1, LP)]

    def g2_gather(n):
        for b in range(1 if n == 4 else 0, M):
            g2cp[n - 1, b].wait_recv()
        for b in range(M):
            g2cp[n, b].start()

    g2_send(0)
    lax.fori_loop(2, M, own_loop, 0)
    tot = total(ar3, cps3)
    ar3z[m] = tot[: 2 * M]
    gb2_all = tot[2 * M : 2 * M + 1]
    cps3z = [send(ar3z.at[m], ar3z.at[m], a3zs.at[k], a3zr.at[k], (d, up[k])) for k in range(1, M)]
    g2_add(0)
    g2_send(1)
    encode(m, to_e1)
    for cp in cps2z:
        cp.wait_recv()
    for b in range(M):
        RW[b, 16:24] = ar2z[b]
    for cp in cps3z:
        cp.wait_recv()
    tot = ar3z[0]
    for b in range(1, M):
        tot = tot + ar3z[b]
    for b in range(M):
        k1 = pv[b, 1:2] * RW[b, 9:10]
        RW[b, 24:25] = k1
        RW[b, 25:26] = -k1 * tot[M + b : M + b + 1] / N
        RW[b, 26:27] = -k1 * tot[b : b + 1] / N
    make_cols()
    pick = lax.broadcasted_iota(I32, (2 * M, 1), 0)
    vec_ref[0:1, :] = jnp.zeros((1, LP), F32)
    vec_ref[1:2, :] = jnp.sum(jnp.where(pick == M + m, tot, 0.0), axis=0, keepdims=True)
    vec_ref[2:3, :] = jnp.sum(jnp.where(pick == m, tot, 0.0), axis=0, keepdims=True)
    vec_ref[3:4, :] = gb2_all
    vec_ref[4:5, :] = ar2z[m, 6:7]
    vec_ref[5:6, :] = ar2z[m, 5:6]
    vec_ref[6:8, :] = jnp.zeros((2, LP), F32)

    PADAT = U // 16 * 16

    def put_grad(b, value, at, size):
        slot, row = a_at(NA, b)
        A[slot, pl.ds(row, U), pl.ds(at, size)] = value

    for b in range(M):
        slot, row = NA + b // PER, (b % PER) * LP
        A[slot, row + PADAT : row + LP, :] = jnp.where(
            lax.broadcasted_iota(I32, (LP - PADAT, Q), 0) < U - PADAT,
            A[slot, row + PADAT : row + LP, :].astype(F32),
            0.0,
        ).astype(BF16)
    cot_loc.wait()

    def back2_own(b):
        act_at, row = a_at(0, b)

        def step(t, _):
            at = pl.multiple_of(t * TL, TL)
            a = A[act_at, pl.ds(row, U), pl.ds(at, TL)].astype(F32)
            s = A[act_at + NA, pl.ds(row, U), pl.ds(at, TL)].astype(F32)
            g = F[b, :, pl.ds(at, TL)].astype(F32)
            grad = (g * col[b, :U, 16:17] + a * col[b, :U, 17:18] + col[b, :U, 18:19]) * s
            A[act_at + NA, pl.ds(row, U), pl.ds(at, TL)] = grad.astype(BF16)
            return 0

        lax.fori_loop(0, NT, step, 0)

    def copy_own(t, _):
        at = pl.multiple_of(t * TL, TL)
        put_grad(m, slo2[:, pl.ds(pl.multiple_of(m * Q + t * TL, TL), TL)], at, TL)
        return 0

    lax.fori_loop(0, NT, copy_own, 0)
    for k in range(1, M):
        ct[k].wait_recv()
        back2_own(down[k])

    g2_add(1)
    g2_send(2)

    def back1(b):
        def step(t, _):
            at = pl.multiple_of(t * TL, TL)
            dh = dot(W2[b, :, 0:K], A[NA, :, pl.ds(at, TL)])
            for n in range(1, NA):
                dh = dh + dot(W2[b, :, n * K : (n + 1) * K], A[NA + n, :, pl.ds(at, TL)])
            norm = B[pl.ds(pl.multiple_of(b * LP, LP), U), pl.ds(pl.multiple_of(m * Q + t * TL, TL), TL)].astype(F32)
            grad = dh * col[b, :U, 24:25] + norm * col[b, :U, 25:26] + col[b, :U, 26:27]
            grad = (grad * H[b, :, pl.ds(at, TL)].astype(F32)).astype(BF16)
            H[b, :, pl.ds(at, TL)] = grad
            acc[0, :U] += lane_part(grad.astype(F32))
            return 0

        lax.fori_loop(0, NT, step, 0)
        ar4[d, pl.ds(b, 1), :] = row_of(0)
        acc[0:1] = jnp.zeros((1, LP, 128), F32)

        def mm(t, _):
            F[b, :, pl.ds(pl.multiple_of(t * LP, LP), LP)] = dot_nt(
                H[b], E1[:, pl.ds(pl.multiple_of(t * Q, Q), Q)]
            ).astype(BF16)
            return 0

        lax.fori_loop(0, PER, mm, 0)

    acc[0:1] = jnp.zeros((1, LP, 128), F32)
    ar4[d] = jnp.zeros((ar4.shape[1], LP), F32)
    K2 = 4 * K8
    FROM = {0: 0, 1: K2, 2: K2 + 2 * K8}
    order = [up[(j + 1) % M] for j in range(M)]
    def g1_cp(n, j):
        b = lax.rem(m + 1 + j, M)
        if n == 3:
            return remote(
                lanes(F.at[b], p * K8, K8), C.at[m, :, pl.ds(K - K8, K8)], g1s.at[3, j + 1], g1r.at[3, j + 1], (d, b)
            )
        return remote(
            lanes(F.at[b], HALF[n] * K8, K2 >> n), lanes(C.at[b], FROM[n], K2 >> n), g1s.at[n, j], g1r.at[n, j], PARTNER[n]
        )

    def g1_groups(b, j):
        mine = pl.ds(pl.multiple_of(p * K8, 128), K8)
        cps = []
        for k in range(1, G):
            to = (lax.rem(d + 8 * k, D), m)
            cps.append(send(lanes(F.at[b], p * K8, K8), x1.at[d // 8, j], x1s.at[k, j], x1r.at[k, j], to))
        x1[d // 8, j] = F[b, :, mine]
        for cp in cps:
            cp.wait_recv()
        for cp in cps:
            gone(cp)
        v = x1[0, j].astype(F32)
        for k in range(1, G):
            v = v + x1[k, j].astype(F32)
        F[b, :, mine] = v.astype(BF16)

    def g1_stage(n, j):
        b = lax.rem(m + 1 + j, M)
        g1_cp(n - 1, j).wait_recv()
        keep = pl.ds(pl.multiple_of(KEEP[n - 1] * K8, 128), K2 >> (n - 1))
        came = C[b, :, FROM[n - 1] : FROM[n - 1] + (K2 >> (n - 1))]
        F[b, :, keep] = (F[b, :, keep].astype(F32) + came.astype(F32)).astype(BF16)
        if n == 3 and G > 1:
            g1_groups(b, j)
        if n < 3 or not isinstance(j, int) or j < M - 1:
            g1_cp(n, j).start()
        else:
            C[m, :, K - K8 : K] = F[m, :, pl.ds(pl.multiple_of(p * K8, 128), K8)]

    def block(j, _):
        back1(lax.rem(m + 1 + j, M))
        g1_cp(0, j).start()
        for n in (3, 2, 1):
            pl.when(j >= n)(functools.partial(g1_stage, n, j - n))

        @pl.when(j == 1)
        def _():
            g2_add(2)
            g2_z()

        pl.when(j == 2)(functools.partial(g2_gather, 4))
        pl.when(j == 3)(functools.partial(g2_gather, 5))
        return 0

    lax.fori_loop(0, M, block, 0)
    cps4 = all_dp(ar4, a4s, a4r)
    for n in (3, 2, 1):
        g1_stage(n, M - n)
    g2_gather(6)

    def finish(t, _):
        at = pl.multiple_of(t * TL, TL)
        a = act2[:, pl.ds(at, TL)].astype(F32)
        act2[:, pl.ds(at, TL)] = (a * col[m, :U, 19:20] + col[m, :U, 20:21]).astype(BF16)
        return 0

    lax.fori_loop(0, M * NT, finish, 0)
    out_copy = pltpu.make_async_copy(act2, out_ref, loc.at[0])
    out_copy.start()
    tot4 = total(ar4, cps4)
    for b in range(M):
        ar4s[b] = jnp.broadcast_to(tot4[b : b + 1], (8, LP))
    ar4z[m] = ar4s[m]
    cps4z = [send(ar4s.at[up[k]], ar4z.at[m], a4zs.at[k], a4zr.at[k], (d, up[k])) for k in range(1, M)]
    g1_stage(3, M - 2)
    g1_stage(2, M - 1)
    g1_stage(3, M - 1)
    for b in range(M):
        g2cp[6, b].wait_recv()
    for b in range(M):
        slo2[:, b * U : (b + 1) * U] = B[b * LP : b * LP + U, pl.ds(L2, LP)][:, :U]
    gw2_copy = pltpu.make_async_copy(lanes(slo2, 0, gw2_ref.shape[1]), gw2_ref, loc.at[2])
    gw2_copy.start()
    for j in range(M - 1):
        g1_cp(3, j).wait_recv()
    v = C[0, :, K - K8 : K].astype(F32)
    for b in range(1, M):
        v = v + C[b, :, K - K8 : K].astype(F32)
    G1[:, pl.ds(pl.multiple_of(p * K8, 128), K8)] = v.astype(BF16)
    ga = send(lanes(G1, p * K8, K8), lanes(G1, p * K8, K8), g1s.at[4, 0], g1r.at[4, 0], lo_dev)
    ga.wait_recv()
    part = lanes(G1, (4 * c + 2 * hi) * K8, 2 * K8)
    ga = send(part, part, g1s.at[4, 1], g1r.at[4, 1], hi_dev)
    ga.wait_recv()
    part = lanes(G1, 4 * c * K8, K2)
    ga = send(part, part, g1s.at[4, 2], g1r.at[4, 2], core_dev)
    for cp in cps4z:
        cp.wait_recv()
    v = ar4z[0]
    for b in range(1, M):
        v = v + ar4z[b]
    vec_ref[0:1, :] = v[0:1]
    ga.wait_recv()
    gw1_copy = pltpu.make_async_copy(lanes(G1, 0, K), gw1_ref, loc.at[1])
    gw1_copy.start()
    for cp in [*ag2.values(), *g2cp.values(), *(g1_cp(n, j) for n in range(4) for j in range(M - n // 3))]:
        cp.wait_send()
    out_copy.wait()
    gw1_copy.wait()
    gw2_copy.wait()
    for cp in sent:
        cp.wait_send()


def per_device(ids, hash_mult, hash_add, w1, b1, s1, t1, w2, b2, s2, t2, cot):
    D, M = lax.axis_size("dp"), lax.axis_size("mp")
    U, K = w1.shape
    R = ids.shape[0]
    Q = R // M
    LP = -(-U // 128) * 128
    G = D // 8
    par = jnp.pad(jnp.stack([b1, s1, t1, b2, s2, t2]), ((0, 2), (0, LP - U)))
    dma = pltpu.SemaphoreType.DMA
    vmem = pl.BlockSpec(memory_space=pltpu.VMEM)
    hbm = pl.BlockSpec(memory_space=pl.ANY)
    AR = -(-2 * M // 8) * 8
    scratch = [
        pltpu.VMEM((M, K, Q), BF16),
        pltpu.VMEM((M * LP, R), BF16),
        pltpu.VMEM((M, U, max(K, Q)), BF16),
        pltpu.VMEM((M, U, M * LP), BF16),
        pltpu.VMEM((U, max(K, M * U)), BF16),
        pltpu.VMEM((LP, M * LP), BF16),
        pltpu.VMEM((M, U, max(K, Q)), BF16),
        pltpu.VMEM((M, U, Q), BF16),
        pltpu.VMEM((U, R), BF16),
        pltpu.VMEM((U, R), BF16),
        pltpu.VMEM((M, LP, 128), F32),
        pltpu.VMEM((M, 32, LP), F32),
        pltpu.VMEM((4, LP, 128), F32),
        pltpu.VMEM((K, 128), F32),
        pltpu.VMEM((M, 8, LP), F32),
        pltpu.VMEM((D, AR, LP), F32),
        pltpu.VMEM((D, 8, LP), F32),
        pltpu.VMEM((M, 8, LP), F32),
        pltpu.VMEM((D, AR + 8, LP), F32),
        pltpu.VMEM((M, AR, LP), F32),
        pltpu.VMEM((D, 8, LP), F32),
        pltpu.VMEM((M, 8, LP), F32),
        pltpu.VMEM((M, 8, LP), F32),
        dma((4, M)), dma((4, M)), dma((4, M)), dma((4, M)),
        dma((M,)), dma((M,)), dma((M,)), dma((M,)), dma((3 + M,)),
        dma((D,)), dma((D,)), dma((D,)), dma((D,)), dma((M,)), dma((M,)),
        dma((D,)), dma((D,)), dma((M,)), dma((M,)), dma((D,)), dma((D,)), dma((M,)), dma((M,)),
        dma((5, M)), dma((5, M)), dma((7, M)), dma((7, M)), pltpu.SemaphoreType.REGULAR((2 + M,)),
    ]
    if G > 1:
        scratch += [
            pltpu.VMEM((G, M, U, K // 8), BF16),
            pltpu.VMEM((G, M, LP // 8, LP), BF16),
            dma((G, M)), dma((G, M)), dma((G, M)), dma((G, M)),
        ]
    out, gw1, gw2, vec = pl.pallas_call(
        functools.partial(kernel, D, M, U, LP, K, R),
        out_shape=[
            jax.ShapeDtypeStruct((U, R), BF16),
            jax.ShapeDtypeStruct((U, K), BF16),
            jax.ShapeDtypeStruct((U, -(-M * U // 128) * 128), BF16),
            jax.ShapeDtypeStruct((8, LP), F32),
        ],
        in_specs=[vmem] * 4 + [hbm, hbm, hbm],
        out_specs=[hbm, hbm, hbm, vmem],
        scratch_shapes=scratch,
        compiler_params=pltpu.CompilerParams(
            collective_id=0, has_side_effects=True, vmem_limit_bytes=64 * 2**20 - 2**16
        ),
    )(ids[None, :], hash_mult[None, :], hash_add[None, :], par, w1, w2, cot)
    v = vec[:, :U]
    return (out, gw1.astype(F32), v[0], v[1], v[2], gw2[:, : M * U].astype(F32), v[3], v[4], v[5])


def solution(mesh):
    return jax.shard_map(
        per_device,
        mesh=mesh,
        in_specs=(
            P("dp"), P(), P(), P("mp", None), P("mp"), P("mp"), P("mp"),
            P("mp", None), P("mp"), P("mp"), P("mp"), P("mp", "dp"),
        ),
        out_specs=(
            P("mp", "dp"), P("mp", None), P("mp"), P("mp"), P("mp"),
            P("mp", None), P("mp"), P("mp"), P("mp"),
        ),
        check_vma=False,
    )
```

```python
import functools

import jax
import jax.numpy as jnp
from jax import lax
from jax.experimental import pallas as pl
from jax.experimental.pallas import tpu as pltpu
from jax.sharding import PartitionSpec as P

MESH = pl.DeviceIdType.MESH
F32, BF16, I32 = jnp.float32, jnp.bfloat16, jnp.int32
epsilon = 1e-05


def dot(a, b):
    return lax.dot_general(a, b, (((1,), (0,)), ((), ())), preferred_element_type=F32)


def dot_nt(a, b):
    return lax.dot_general(a, b, (((1,), (1,)), ((), ())), preferred_element_type=F32)


def mish_parts(v):
    u = jnp.exp(jnp.minimum(v, 20.0))
    n = u * (u + 2.0)
    d = n + 2.0
    r = pl.reciprocal(d, approx=True)
    t = n * r
    return v * t, t + v * ((4.0 * (n - u) * r) * r)


def mish(v):
    u = jnp.exp(jnp.minimum(v, 20.0))
    n = u * (u + 2.0)
    d = n + 2.0
    r = pl.reciprocal(d, approx=True)
    return v * (n * r)


def lane_part(x):
    out = x[:, :128]
    for at in range(128, x.shape[1], 128):
        out = out + x[:, at : at + 128]
    return out


def kernel(
    D, M, U, LP, K, R,
    ids_ref, mult_ref, add_ref, b1_ref, s1_ref, t1_ref, b2_ref, s2_ref, t2_ref, w1_ref, w2_ref, cot_ref,
    out_ref, gw1_ref, gw2_ref, vec_ref,
    A, B, C, W2, G1, E1, F, H, act2, slo2, col, RW, acc, hcol,
    pv, ar1, ar2, ar2z, ar3, ar3z, ar4, ar4s, ar4z,
    w1s, w1r, w2s, w2r, pvs, pvr, cts, ctr, loc,
    a1s, a1r, a2s, a2r, a2zs, a2zr, a3s, a3r, a3zs, a3zr, a4s, a4r, a4zs, a4zr,
    g1s, g1r, g2s, g2r, free, *extra,
):
    Q = R // M
    G = D // 8
    TL = min(512, Q)
    NT = Q // TL
    PER = K // LP
    NA = M // PER
    K8 = K // 8
    J8 = M * LP // 8
    S8 = LP // 8
    N = float(R * D)
    d = lax.axis_index("dp")
    m = lax.axis_index("mp")
    i = lax.rem(d, 8)
    c = lax.rem(i, 2)
    x = lax.rem(i // 2, 2)
    y = i // 4
    hi = (1 - c) * x + c * y
    lo = (1 - c) * y + c * x
    p = 4 * c + 2 * hi + lo
    core_dev = (d + 1 - 2 * c, m)
    flip_x = d + 2 - 4 * x
    flip_y = d + 4 - 8 * y
    hi_dev = ((1 - c) * flip_x + c * flip_y, m)
    lo_dev = ((1 - c) * flip_y + c * flip_x, m)
    up = [lax.rem(m + k, M) for k in range(M)]
    down = [lax.rem(m - k + M, M) for k in range(M)]
    others = [lax.rem(d + k, D) for k in range(D)]
    sent = []

    def remote(src, dst, ss, rs, dev):
        cp = pltpu.make_async_remote_copy(
            src_ref=src, dst_ref=dst, send_sem=ss, recv_sem=rs, device_id=dev, device_id_type=MESH
        )
        return cp

    def send(src, dst, ss, rs, dev):
        cp = remote(src, dst, ss, rs, dev)
        cp.start()
        sent.append(cp)
        return cp

    def gone(cp):
        cp.wait_send()
        sent[:] = [other for other in sent if other is not cp]

    def lanes(ref, at, size):
        return ref.at[:, pl.ds(pl.multiple_of(at, 128), size)]

    def rows(ref, at, size):
        return ref.at[pl.ds(pl.multiple_of(at, 16), size)]

    bar = pltpu.get_barrier_semaphore()
    greeted = [core_dev, hi_dev, lo_dev] if G == 1 else [(others[k], m) for k in range(1, D)]
    greeted += [(d, up[k]) for k in range(1, M)]
    for dev in greeted:
        pl.semaphore_signal(bar, inc=1, device_id=dev, device_id_type=MESH)

    w2_loc = pltpu.make_async_copy(w2_ref, G1, loc.at[1])
    w2_loc.start()
    w1_loc = pltpu.make_async_copy(w1_ref, C.at[m], loc.at[0])
    w1_loc.start()
    cot_loc = pltpu.make_async_copy(lanes(cot_ref, m * Q, Q), lanes(F.at[m], 0, Q), loc.at[2])
    pv[m] = jnp.zeros((8, LP), F32)
    for n, ref in enumerate((b1_ref, s1_ref, t1_ref, b2_ref, s2_ref, t2_ref)):
        pv[m, n : n + 1, :U] = ref[...]
    pl.semaphore_wait(bar, len(greeted))

    ag1, ag2, agp, ct = {}, {}, {}, {}
    for k in range(1, M):
        agp[k] = send(pv.at[m], pv.at[m], pvs.at[k], pvr.at[k], (d, up[k]))
    for ag, own, buf, size, ss, rs in ((ag1, w1_ref, C, K8, w1s, w1r), (ag2, None, W2, J8, w2s, w2r)):
        for k in range(1, M):
            part = lanes(buf.at[m], p * size, size)
            mine = part if own is None else lanes(own, p * size, size)
            ag[0, k] = remote(mine, part, ss.at[0, k], rs.at[0, k], (d, up[k]))
            for step, dev, at, width in (
                (1, lo_dev, p, 1), (2, hi_dev, 4 * c + 2 * hi, 2), (3, core_dev, 4 * c, 4)
            ):
                part = lanes(buf.at[down[k]], at * size, width * size)
                ag[step, k] = remote(part, part, ss.at[step, k], rs.at[step, k], dev)
    for k in range(1, M):
        ag1[0, k].start()
    w2_loc.wait()
    for b in range(M):
        W2[m, :, (b + 1) * LP - 128 : (b + 1) * LP] = jnp.zeros((U, 128), BF16)
        W2[m, :, b * LP : b * LP + U] = G1[:, b * U : (b + 1) * U]

    def gather_stage(step, ag):
        for k in range(1, M):
            ag[step - 1, k].wait_recv()
            ag[step, k].start()

    def stage1(step):
        gather_stage(step, ag1)

    def stage2(step):
        gather_stage(step, ag2)

    hrow = jnp.concatenate(
        [mult_ref[...].astype(F32), add_ref[...].astype(F32), jnp.zeros((126, K), F32)], axis=0
    )
    hcol[...] = hrow.T

    HT = 128

    def encode(q, put):
        def step(t, _):
            at = pl.multiple_of(t * HT, HT)
            both = hcol[pl.ds(at, HT), :].astype(I32)
            v = both[:, 0:1] * ids_ref[:, pl.ds(pl.multiple_of(q * Q, 128), Q)] + both[:, 1:2]
            for _ in range(2):
                top = lax.shift_right_logical(v, 16)
                v = (v & 65535) + ((top << 4) - top)
            v = jnp.where(v >= 65521, v - 65521, v)
            put(t, (v.astype(F32) * (2.0 / 65520.0) - 1.0).astype(BF16))
            return 0

        lax.fori_loop(0, K // HT, step, 0)

    def make_col(b):
        col[b] = jnp.concatenate([RW[b], jnp.zeros((128 - RW.shape[1], LP), F32)], axis=0).T

    def make_cols():
        def step(b, _):
            make_col(b)
            return 0

        lax.fori_loop(0, M, step, 0)

    def to_a(q):
        def put(t, value):
            A[q, pl.ds(pl.multiple_of(t * HT, HT), HT), :] = value

        return put

    def to_e1(t, value):
        E1[pl.ds(pl.multiple_of(lax.rem(t, LP // HT) * HT, HT), HT), pl.ds(pl.multiple_of(t // (LP // HT) * Q, 128), Q)] = value

    def row_of(slot):
        return jnp.sum(acc[slot].T, axis=0, keepdims=True)

    acc[...] = jnp.zeros_like(acc)
    for b in range(M):
        B[pl.ds(b * LP + U // 16 * 16, LP - U // 16 * 16), :] = jnp.zeros((LP - U // 16 * 16, R), BF16)

    RW[...] = jnp.zeros_like(RW)
    RW[m, 0:8] = pv[m]
    make_col(m)
    encode(m, to_a(m))
    w1_loc.wait()

    def mm1_own(b):
        def step(t, _):
            at = pl.multiple_of(t * TL, TL)
            act, slope = mish_parts(dot(C[b], A[m, :, pl.ds(at, TL)]) + col[b, :U, 0:1])
            H[b, :, pl.ds(at, TL)] = slope.astype(BF16)
            B[pl.ds(pl.multiple_of(b * LP, LP), U), pl.ds(pl.multiple_of(m * Q + t * TL, TL), TL)] = act.astype(BF16)
            acc[0, :U] += lane_part(act)
            acc[1, :U] += lane_part(act * act)
            return 0

        lax.fori_loop(0, NT, step, 0)

    def mm1_rest(b):
        def step(t, _):
            q = lax.rem(m + t, M)
            act = mish(dot(C[b], A[q]) + col[b, :U, 0:1])
            B[pl.ds(pl.multiple_of(b * LP, LP), U), pl.ds(pl.multiple_of(q * Q, Q), Q)] = act.astype(BF16)
            acc[0, :U] += lane_part(act)
            acc[1, :U] += lane_part(act * act)
            return 0

        lax.fori_loop(1, M, step, 0)

    def mm1_sums(b):
        ar1[d, pl.ds(b, 1), :] = row_of(0)
        ar1[d, pl.ds(b + M, 1), :] = row_of(1)
        acc[0:2] = jnp.zeros((2, LP, 128), F32)

    mm1_own(m)
    stage1(1)
    for k in range(1, M):
        ag2[0, k].start()

    def enc_step(k, _):
        q = lax.rem(m + M - k, M)
        encode(q, to_a(q))
        return 0

    lax.fori_loop(1, M, enc_step, 0)
    stage1(2)
    mm1_rest(m)
    mm1_sums(m)
    stage2(1)
    cot_loc.start()
    for q in range(1, M):
        ct[q] = send(
            lanes(cot_ref, up[q] * Q, Q), lanes(F.at[m], 0, Q), cts.at[q], ctr.at[q], (d, up[q])
        )
    stage1(3)
    for k in range(1, M):
        agp[k].wait_recv()
    for b in range(M):
        RW[b, 0:8] = pv[b]
    make_cols()
    def mm1_other(k, _):
        b = lax.rem(m + M - k, M)
        part = lanes(C.at[b], 4 * c * K8, 4 * K8)
        remote(part, part, w1s.at[3, k], w1r.at[3, k], core_dev).wait_recv()
        mm1_own(b)
        mm1_rest(b)
        mm1_sums(b)
        pl.when(k == 1)(functools.partial(stage2, 2))
        return 0

    lax.fori_loop(1, M, mm1_other, 0)

    def all_dp(buf, ss, rs):
        cps = []
        for k in range(1, D):
            cps.append(send(buf.at[d], buf.at[d], ss.at[k], rs.at[k], (others[k], m)))
        return cps

    def total(buf, cps):
        for cp in cps:
            cp.wait_recv()
        out = buf[0]
        for k in range(1, D):
            out = out + buf[k]
        return out

    cps1 = all_dp(ar1, a1s, a1r)
    stage2(3)
    for cp in ag1.values():
        cp.wait_send()
    cot_all = []
    for q in range(M):
        cp = pltpu.make_async_copy(lanes(cot_ref, q * Q, Q), lanes(C.at[q], 0, Q), loc.at[3 + q])
        cot_all.append(cp)
        cp.start()
    for k in range(1, M):
        ag2[3, k].wait_recv()

    def make_e1(b):
        def step(h, _):
            part = W2[h, :, pl.ds(pl.multiple_of(b * LP, LP), LP)].astype(F32) * col[h, :U, 1:2]
            for n in range(LP // 128):
                acc[n, :U] = part[:, n * 128 : (n + 1) * 128]
            for n in range(LP // 128):
                E1[n * 128 : (n + 1) * 128, pl.ds(pl.multiple_of(h * LP, LP), LP)] = acc[n].T.astype(BF16)
            return 0

        lax.fori_loop(0, M, step, 0)
        acc[...] = jnp.zeros_like(acc)

    const = jnp.zeros((8, M * LP), F32)
    for b in range(M):
        shift = jnp.broadcast_to(pv[b, 2:3, :U], (8, U))
        upper = shift.astype(BF16)
        lower = (shift - upper.astype(F32)).astype(BF16)
        const = const + dot(upper, W2[b]) + dot(lower, W2[b])
    for b in range(M):
        RW[b, 8:9] = const[0:1, b * LP : (b + 1) * LP] + pv[b, 3:4]
    make_e1(m)

    tot = total(ar1, cps1)
    mean = tot[:M] / N
    inv = lax.rsqrt(tot[M:] / N - mean * mean + epsilon)
    for b in range(M):
        RW[b, 9:10] = inv[b : b + 1]
        RW[b, 10:11] = -mean[b : b + 1] * inv[b : b + 1]
    make_cols()
    for cp in cot_all:
        cp.wait()

    def mm2(t, _):
        at = pl.multiple_of(t * TL, TL)
        for b in range(M):
            part = B[b * LP : b * LP + U, pl.ds(at, TL)].astype(F32)
            B[b * LP : b * LP + U, pl.ds(at, TL)] = (part * col[b, :U, 9:10] + col[b, :U, 10:11]).astype(BF16)
        v = dot(E1[:U], B[:, pl.ds(at, TL)]) + col[m, :U, 8:9]
        act, slope = mish_parts(v)
        act2[:, pl.ds(at, TL)] = act.astype(BF16)
        slo2[:, pl.ds(at, TL)] = slope.astype(BF16)
        g = C[t // NT, :, pl.ds(pl.multiple_of(lax.rem(t, NT) * TL, TL), TL)].astype(F32)
        acc[0, :U] += lane_part(act)
        acc[1, :U] += lane_part(act * act)
        acc[2, :U] += lane_part(g)
        acc[3, :U] += lane_part(g * act)
        return 0

    lax.fori_loop(0, M * NT, mm2, 0)
    for s in range(4):
        ar2[d, s : s + 1, :] = row_of(s)
    ar2[d, 4:8, :] = jnp.zeros((4, LP), F32)
    acc[...] = jnp.zeros_like(acc)
    cps2 = all_dp(ar2, a2s, a2r)

    def a_at(base, b):
        return base + b // PER, pl.multiple_of(lax.rem(b, PER) * LP, LP)

    def mm2_own(b):
        make_e1(b)
        act_at, row = a_at(0, b)
        v = dot(E1[:U], B[:, pl.ds(pl.multiple_of(m * Q, Q), Q)]) + col[b, :U, 8:9]
        act, slope = mish_parts(v)
        A[act_at, pl.ds(row, U)] = act.astype(BF16)
        A[act_at + NA, pl.ds(row, U)] = slope.astype(BF16)

    def own_loop(k, _):
        mm2_own(lax.rem(m + k, M))
        return 0

    mm2_own(up[1])
    tot = total(ar2, cps2)
    mean = tot[0:1] / N
    inv = lax.rsqrt(tot[1:2] / N - mean * mean + epsilon)
    sum_g = tot[2:3]
    sum_gn = inv * (tot[3:4] - mean * sum_g)
    k1 = pv[m, 4:5] * inv
    k2 = -k1 * inv * sum_gn / N
    k3 = -k1 * sum_g / N - mean * k2
    ar2z[m, 0:1] = k1
    ar2z[m, 1:2] = k2
    ar2z[m, 2:3] = k3
    ar2z[m, 3:4] = k1
    ar2z[m, 4:5] = pv[m, 5:6] - mean * k1
    ar2z[m, 5:6] = sum_g
    ar2z[m, 6:7] = sum_gn
    ar2z[m, 7:8] = jnp.zeros((1, LP), F32)
    cps2z = [send(ar2z.at[m], ar2z.at[m], a2zs.at[k], a2zr.at[k], (d, up[k])) for k in range(1, M)]
    RW[m, 16:24] = ar2z[m]
    make_col(m)

    def back2(t, _):
        at = pl.multiple_of(t * TL, TL)
        a = act2[:, pl.ds(at, TL)].astype(F32)
        g = C[t // NT, :, pl.ds(pl.multiple_of(lax.rem(t, NT) * TL, TL), TL)].astype(F32)
        grad = (g * col[m, :U, 16:17] + a * col[m, :U, 17:18] + col[m, :U, 18:19]) * slo2[:, pl.ds(at, TL)].astype(F32)
        grad = grad.astype(BF16)
        slo2[:, pl.ds(at, TL)] = grad
        acc[0, :U] += lane_part(grad.astype(F32))
        return 0

    lax.fori_loop(0, M * NT, back2, 0)
    gb2 = row_of(0)
    ar3[d, 2 * M : 2 * M + 1, :] = gb2
    ar3[d, 2 * M + 1 : 2 * M + 8, :] = jnp.zeros((7, LP), F32)
    acc[0:1] = jnp.zeros((1, LP, 128), F32)

    L1 = pl.multiple_of(lax.rem(m + 1, M) * Q, 128)
    LR = pl.multiple_of(L1 + LP, 128)

    def rowsum(x):
        acc[0, :U] = lane_part(x[:, : U // 128 * 128]) + jnp.where(
            lax.broadcasted_iota(I32, (U, 128), 1) >= 128 - U % 128, x[:, U - 128 :], 0.0
        )
        return row_of(0)

    gb2_all8 = jnp.broadcast_to(gb2[:, :U], (8, U))
    gb2_up = gb2_all8.astype(BF16)
    gb2_low = (gb2_all8 - gb2_up.astype(F32)).astype(BF16)
    ar3[d, 0 : 2 * M, :] = jnp.zeros((2 * M, LP), F32)

    def grad_w2(b, _):
        at = pl.multiple_of(b * LP, LP)
        g = dot_nt(B[pl.ds(at, LP), :], slo2[...])
        w16 = W2[b, :, pl.ds(pl.multiple_of(m * LP, LP), LP)][:, :U]
        w = w16.astype(F32)
        ar3[d, pl.ds(b, 1), :U] = dot_nt(gb2_up, w16)[0:1] + dot_nt(gb2_low, w16)[0:1]
        ar3[d, pl.ds(b + M, 1), :] = rowsum(w * g[:U])
        g = g * col[b, :, 1:2] + col[b, :, 2:3] * gb2[:, :U]
        B[pl.ds(at, LP), pl.ds(L1, U)] = g.astype(BF16)
        B[pl.ds(at, LP), pl.ds(L1 + U // 128 * 128, LP - U // 128 * 128)] = jnp.where(
            lax.broadcasted_iota(I32, (LP, LP - U // 128 * 128), 1) < U - U // 128 * 128,
            B[pl.ds(at, LP), pl.ds(L1 + U // 128 * 128, LP - U // 128 * 128)].astype(F32),
            0.0,
        ).astype(BF16)
        return 0

    lax.fori_loop(0, M, grad_w2, 0)
    cps3 = all_dp(ar3, a3s, a3r)
    for n, dev in ((0, core_dev), (1, hi_dev), (2, lo_dev)):
        pl.semaphore_signal(free.at[n], inc=1, device_id=dev, device_id_type=MESH)
    for k in range(1, M):
        pl.semaphore_signal(free.at[2 + k], inc=1, device_id=(d, up[k]), device_id_type=MESH)

    HALF = {0: (1 - c) * 4, 1: 4 * c + 2 * (1 - hi), 2: 4 * c + 2 * hi + 1 - lo}
    KEEP = {0: 4 * c, 1: 4 * c + 2 * hi, 2: p}
    START = {0: 0, 1: 4, 2: 6}
    PARTNER = {0: core_dev, 1: hi_dev, 2: lo_dev}
    g2cp = {}

    def b_rows(b, at, size, lane):
        return B.at[pl.ds(pl.multiple_of(b * LP + at * S8, 16), size * S8), pl.ds(lane, LP)]

    def g2_send(n):
        pl.semaphore_wait(free.at[n], 1)
        for b in range(M):
            g2cp[n, b].start()

    def g2_add(n):
        for b in range(M):
            g2cp[n, b].wait_recv()
            size = (4 >> n) * S8
            keep = pl.ds(pl.multiple_of(b * LP + KEEP[n] * S8, 16), size)
            came = pl.ds(b * LP + START[n] * S8, size)
            B[keep, pl.ds(L1, LP)] = (
                B[keep, pl.ds(L1, LP)].astype(F32) + B[came, pl.ds(LR, LP)].astype(F32)
            ).astype(BF16)

    def l2_of(z):
        return pl.multiple_of(lax.rem(z + 2, M) * Q, 128)

    L2 = l2_of(m)
    for b in range(M):
        for n in range(3):
            g2cp[n, b] = remote(
                b_rows(b, HALF[n], 4 >> n, L1), b_rows(b, START[n], 4 >> n, LR), g2s.at[n, b], g2r.at[n, b], PARTNER[n]
            )
        for n, at, size, dev in ((4, p, 1, lo_dev), (5, 4 * c + 2 * hi, 2, hi_dev), (6, 4 * c, 4, core_dev)):
            part = b_rows(b, at, size, L2)
            g2cp[n, b] = remote(part, part, g2s.at[n, b], g2r.at[n, b], dev)
        if b:
            g2cp[3, b] = remote(
                b_rows(up[b], p, 1, L1),
                B.at[pl.ds(pl.multiple_of(m * LP + p * S8, 16), S8), pl.ds(l2_of(up[b]), LP)],
                g2s.at[3, b], g2r.at[3, b], (d, up[b]),
            )

    if G > 1:
        x1, x2, x1s, x1r, x2s, x2r = extra

    def g2_groups():
        cps = []
        for k in range(1, G):
            to = (lax.rem(d + 8 * k, D), m)
            for b in range(M):
                cps.append(send(b_rows(b, p, 1, L1), x2.at[d // 8, b], x2s.at[k, b], x2r.at[k, b], to))
        for b in range(M):
            x2[d // 8, b] = B[pl.ds(pl.multiple_of(b * LP + p * S8, 16), S8), pl.ds(L1, LP)]
        for cp in cps:
            cp.wait_recv()
        for cp in cps:
            gone(cp)
        for b in range(M):
            v = x2[0, b].astype(F32)
            for k in range(1, G):
                v = v + x2[k, b].astype(F32)
            B[pl.ds(pl.multiple_of(b * LP + p * S8, 16), S8), pl.ds(L1, LP)] = v.astype(BF16)

    def g2_z():
        if G > 1:
            g2_groups()
        for k in range(1, M):
            pl.semaphore_wait(free.at[2 + M - k], 1)
            g2cp[3, k].start()
        mine = pl.ds(pl.multiple_of(m * LP + p * S8, 16), S8)
        B[mine, pl.ds(L2, LP)] = B[mine, pl.ds(L1, LP)]

    def g2_gather(n):
        for b in range(1 if n == 4 else 0, M):
            g2cp[n - 1, b].wait_recv()
        for b in range(M):
            g2cp[n, b].start()

    g2_send(0)
    lax.fori_loop(2, M, own_loop, 0)
    tot = total(ar3, cps3)
    ar3z[m] = tot[: 2 * M]
    gb2_all = tot[2 * M : 2 * M + 1]
    cps3z = [send(ar3z.at[m], ar3z.at[m], a3zs.at[k], a3zr.at[k], (d, up[k])) for k in range(1, M)]
    g2_add(0)
    g2_send(1)
    encode(m, to_e1)
    for cp in cps2z:
        cp.wait_recv()
    for b in range(M):
        RW[b, 16:24] = ar2z[b]
    for cp in cps3z:
        cp.wait_recv()
    tot = ar3z[0]
    for b in range(1, M):
        tot = tot + ar3z[b]
    for b in range(M):
        k1 = pv[b, 1:2] * RW[b, 9:10]
        RW[b, 24:25] = k1
        RW[b, 25:26] = -k1 * tot[M + b : M + b + 1] / N
        RW[b, 26:27] = -k1 * tot[b : b + 1] / N
    make_cols()
    pick = lax.broadcasted_iota(I32, (2 * M, 1), 0)
    vec_ref[0:1, :] = jnp.zeros((1, LP), F32)
    vec_ref[1:2, :] = jnp.sum(jnp.where(pick == M + m, tot, 0.0), axis=0, keepdims=True)
    vec_ref[2:3, :] = jnp.sum(jnp.where(pick == m, tot, 0.0), axis=0, keepdims=True)
    vec_ref[3:4, :] = gb2_all
    vec_ref[4:5, :] = ar2z[m, 6:7]
    vec_ref[5:6, :] = ar2z[m, 5:6]
    vec_ref[6:8, :] = jnp.zeros((2, LP), F32)

    PADAT = U // 16 * 16

    def put_grad(b, value, at, size):
        slot, row = a_at(NA, b)
        A[slot, pl.ds(row, U), pl.ds(at, size)] = value

    for b in range(M):
        slot, row = NA + b // PER, (b % PER) * LP
        A[slot, row + PADAT : row + LP, :] = jnp.where(
            lax.broadcasted_iota(I32, (LP - PADAT, Q), 0) < U - PADAT,
            A[slot, row + PADAT : row + LP, :].astype(F32),
            0.0,
        ).astype(BF16)
    cot_loc.wait()

    def back2_own(b):
        act_at, row = a_at(0, b)

        def step(t, _):
            at = pl.multiple_of(t * TL, TL)
            a = A[act_at, pl.ds(row, U), pl.ds(at, TL)].astype(F32)
            s = A[act_at + NA, pl.ds(row, U), pl.ds(at, TL)].astype(F32)
            g = F[b, :, pl.ds(at, TL)].astype(F32)
            grad = (g * col[b, :U, 16:17] + a * col[b, :U, 17:18] + col[b, :U, 18:19]) * s
            A[act_at + NA, pl.ds(row, U), pl.ds(at, TL)] = grad.astype(BF16)
            return 0

        lax.fori_loop(0, NT, step, 0)

    def copy_own(t, _):
        at = pl.multiple_of(t * TL, TL)
        put_grad(m, slo2[:, pl.ds(pl.multiple_of(m * Q + t * TL, TL), TL)], at, TL)
        return 0

    lax.fori_loop(0, NT, copy_own, 0)
    for k in range(1, M):
        ct[k].wait_recv()
        back2_own(down[k])

    g2_add(1)
    g2_send(2)

    def back1(b):
        def step(t, _):
            at = pl.multiple_of(t * TL, TL)
            dh = dot(W2[b, :, 0:K], A[NA, :, pl.ds(at, TL)])
            for n in range(1, NA):
                dh = dh + dot(W2[b, :, n * K : (n + 1) * K], A[NA + n, :, pl.ds(at, TL)])
            norm = B[pl.ds(pl.multiple_of(b * LP, LP), U), pl.ds(pl.multiple_of(m * Q + t * TL, TL), TL)].astype(F32)
            grad = dh * col[b, :U, 24:25] + norm * col[b, :U, 25:26] + col[b, :U, 26:27]
            grad = (grad * H[b, :, pl.ds(at, TL)].astype(F32)).astype(BF16)
            H[b, :, pl.ds(at, TL)] = grad
            acc[0, :U] += lane_part(grad.astype(F32))
            return 0

        lax.fori_loop(0, NT, step, 0)
        ar4[d, pl.ds(b, 1), :] = row_of(0)
        acc[0:1] = jnp.zeros((1, LP, 128), F32)

        def mm(t, _):
            F[b, :, pl.ds(pl.multiple_of(t * LP, LP), LP)] = dot_nt(
                H[b], E1[:, pl.ds(pl.multiple_of(t * Q, Q), Q)]
            ).astype(BF16)
            return 0

        lax.fori_loop(0, PER, mm, 0)

    acc[0:1] = jnp.zeros((1, LP, 128), F32)
    ar4[d] = jnp.zeros((ar4.shape[1], LP), F32)
    K2 = 4 * K8
    FROM = {0: 0, 1: K2, 2: K2 + 2 * K8}
    order = [up[(j + 1) % M] for j in range(M)]
    def g1_cp(n, j):
        b = lax.rem(m + 1 + j, M)
        if n == 3:
            return remote(
                lanes(F.at[b], p * K8, K8), C.at[m, :, pl.ds(K - K8, K8)], g1s.at[3, j + 1], g1r.at[3, j + 1], (d, b)
            )
        return remote(
            lanes(F.at[b], HALF[n] * K8, K2 >> n), lanes(C.at[b], FROM[n], K2 >> n), g1s.at[n, j], g1r.at[n, j], PARTNER[n]
        )

    def g1_groups(b, j):
        mine = pl.ds(pl.multiple_of(p * K8, 128), K8)
        cps = []
        for k in range(1, G):
            to = (lax.rem(d + 8 * k, D), m)
            cps.append(send(lanes(F.at[b], p * K8, K8), x1.at[d // 8, j], x1s.at[k, j], x1r.at[k, j], to))
        x1[d // 8, j] = F[b, :, mine]
        for cp in cps:
            cp.wait_recv()
        for cp in cps:
            gone(cp)
        v = x1[0, j].astype(F32)
        for k in range(1, G):
            v = v + x1[k, j].astype(F32)
        F[b, :, mine] = v.astype(BF16)

    def g1_stage(n, j):
        b = lax.rem(m + 1 + j, M)
        g1_cp(n - 1, j).wait_recv()
        keep = pl.ds(pl.multiple_of(KEEP[n - 1] * K8, 128), K2 >> (n - 1))
        came = C[b, :, FROM[n - 1] : FROM[n - 1] + (K2 >> (n - 1))]
        F[b, :, keep] = (F[b, :, keep].astype(F32) + came.astype(F32)).astype(BF16)
        if n == 3 and G > 1:
            g1_groups(b, j)
        if n < 3 or not isinstance(j, int) or j < M - 1:
            g1_cp(n, j).start()
        else:
            C[m, :, K - K8 : K] = F[m, :, pl.ds(pl.multiple_of(p * K8, 128), K8)]

    def block(j, _):
        back1(lax.rem(m + 1 + j, M))
        g1_cp(0, j).start()
        for n in (3, 2, 1):
            pl.when(j >= n)(functools.partial(g1_stage, n, j - n))

        @pl.when(j == 1)
        def _():
            g2_add(2)
            g2_z()

        pl.when(j == 2)(functools.partial(g2_gather, 4))
        pl.when(j == 3)(functools.partial(g2_gather, 5))
        return 0

    lax.fori_loop(0, M, block, 0)
    cps4 = all_dp(ar4, a4s, a4r)
    for n in (3, 2, 1):
        g1_stage(n, M - n)
    g2_gather(6)

    def finish(t, _):
        at = pl.multiple_of(t * TL, TL)
        a = act2[:, pl.ds(at, TL)].astype(F32)
        act2[:, pl.ds(at, TL)] = (a * col[m, :U, 19:20] + col[m, :U, 20:21]).astype(BF16)
        return 0

    lax.fori_loop(0, M * NT, finish, 0)
    out_copy = pltpu.make_async_copy(act2, out_ref, loc.at[0])
    out_copy.start()
    tot4 = total(ar4, cps4)
    for b in range(M):
        ar4s[b] = jnp.broadcast_to(tot4[b : b + 1], (8, LP))
    ar4z[m] = ar4s[m]
    cps4z = [send(ar4s.at[up[k]], ar4z.at[m], a4zs.at[k], a4zr.at[k], (d, up[k])) for k in range(1, M)]
    g1_stage(3, M - 2)
    g1_stage(2, M - 1)
    g1_stage(3, M - 1)
    for b in range(M):
        g2cp[6, b].wait_recv()
    for b in range(M):
        slo2[:, b * U : (b + 1) * U] = B[b * LP : b * LP + U, pl.ds(L2, LP)][:, :U]
    gw2_copy = pltpu.make_async_copy(lanes(slo2, 0, gw2_ref.shape[1]), gw2_ref, loc.at[2])
    gw2_copy.start()
    for j in range(M - 1):
        g1_cp(3, j).wait_recv()
    v = C[0, :, K - K8 : K].astype(F32)
    for b in range(1, M):
        v = v + C[b, :, K - K8 : K].astype(F32)
    G1[:, pl.ds(pl.multiple_of(p * K8, 128), K8)] = v.astype(BF16)
    ga = send(lanes(G1, p * K8, K8), lanes(G1, p * K8, K8), g1s.at[4, 0], g1r.at[4, 0], lo_dev)
    ga.wait_recv()
    part = lanes(G1, (4 * c + 2 * hi) * K8, 2 * K8)
    ga = send(part, part, g1s.at[4, 1], g1r.at[4, 1], hi_dev)
    ga.wait_recv()
    part = lanes(G1, 4 * c * K8, K2)
    ga = send(part, part, g1s.at[4, 2], g1r.at[4, 2], core_dev)
    for cp in cps4z:
        cp.wait_recv()
    v = ar4z[0]
    for b in range(1, M):
        v = v + ar4z[b]
    vec_ref[0:1, :] = v[0:1]
    ga.wait_recv()
    gw1_copy = pltpu.make_async_copy(lanes(G1, 0, K), gw1_ref, loc.at[1])
    gw1_copy.start()
    for cp in [*ag2.values(), *g2cp.values(), *(g1_cp(n, j) for n in range(4) for j in range(M - n // 3))]:
        cp.wait_send()
    out_copy.wait()
    gw1_copy.wait()
    gw2_copy.wait()
    for cp in sent:
        cp.wait_send()


def finish(U, out_in, gw1_in, gw2_in, vec_in, out_ref, gw1_ref, gw2_ref, *tail):
    *vecs, held, held1, held2, wide1, wide2, sem_in, sem_out = tail
    n = 4
    width = held.shape[1] // n
    pieces = [pl.ds(k * width, width) for k in range(n)]
    ins = [
        pltpu.make_async_copy(gw2_in, held2, sem_in.at[n]),
        pltpu.make_async_copy(gw1_in, held1, sem_in.at[n + 1]),
    ] + [pltpu.make_async_copy(out_in.at[:, at], held.at[:, at], sem_in.at[k]) for k, at in enumerate(pieces)]
    for cp in ins:
        cp.start()
    outs = [
        pltpu.make_async_copy(wide2, gw2_ref, sem_out.at[n]),
        pltpu.make_async_copy(wide1, gw1_ref, sem_out.at[n + 1]),
    ] + [pltpu.make_async_copy(held.at[:, at], out_ref.at[:, at], sem_out.at[k]) for k, at in enumerate(pieces)]
    ins[0].wait()
    wide2[...] = held2[:, : wide2.shape[1]].astype(F32)
    outs[0].start()
    ins[1].wait()
    wide1[...] = held1[...].astype(F32)
    outs[1].start()
    for k in range(n):
        ins[2 + k].wait()
        outs[2 + k].start()
    for k, ref in enumerate(vecs):
        ref[...] = vec_in[k : k + 1, :U]
    for cp in outs:
        cp.wait()


def per_device(ids, hash_mult, hash_add, w1, b1, s1, t1, w2, b2, s2, t2, cot):
    D, M = lax.axis_size("dp"), lax.axis_size("mp")
    U, K = w1.shape
    R = ids.shape[0]
    Q = R // M
    LP = -(-U // 128) * 128
    G = D // 8
    par = [x[None, :] for x in (b1, s1, t1, b2, s2, t2)]
    dma = pltpu.SemaphoreType.DMA
    vmem = pl.BlockSpec(memory_space=pltpu.VMEM)
    hbm = pl.BlockSpec(memory_space=pl.ANY)
    AR = -(-2 * M // 8) * 8
    scratch = [
        pltpu.VMEM((M, K, Q), BF16),
        pltpu.VMEM((M * LP, R), BF16),
        pltpu.VMEM((M, U, max(K, Q)), BF16),
        pltpu.VMEM((M, U, M * LP), BF16),
        pltpu.VMEM((U, max(K, M * U)), BF16),
        pltpu.VMEM((LP, M * LP), BF16),
        pltpu.VMEM((M, U, max(K, Q)), BF16),
        pltpu.VMEM((M, U, Q), BF16),
        pltpu.VMEM((U, R), BF16),
        pltpu.VMEM((U, R), BF16),
        pltpu.VMEM((M, LP, 128), F32),
        pltpu.VMEM((M, 32, LP), F32),
        pltpu.VMEM((4, LP, 128), F32),
        pltpu.VMEM((K, 128), F32),
        pltpu.VMEM((M, 8, LP), F32),
        pltpu.VMEM((D, AR, LP), F32),
        pltpu.VMEM((D, 8, LP), F32),
        pltpu.VMEM((M, 8, LP), F32),
        pltpu.VMEM((D, AR + 8, LP), F32),
        pltpu.VMEM((M, AR, LP), F32),
        pltpu.VMEM((D, 8, LP), F32),
        pltpu.VMEM((M, 8, LP), F32),
        pltpu.VMEM((M, 8, LP), F32),
        dma((4, M)), dma((4, M)), dma((4, M)), dma((4, M)),
        dma((M,)), dma((M,)), dma((M,)), dma((M,)), dma((3 + M,)),
        dma((D,)), dma((D,)), dma((D,)), dma((D,)), dma((M,)), dma((M,)),
        dma((D,)), dma((D,)), dma((M,)), dma((M,)), dma((D,)), dma((D,)), dma((M,)), dma((M,)),
        dma((5, M)), dma((5, M)), dma((7, M)), dma((7, M)), pltpu.SemaphoreType.REGULAR((2 + M,)),
    ]
    if G > 1:
        scratch += [
            pltpu.VMEM((G, M, U, K // 8), BF16),
            pltpu.VMEM((G, M, LP // 8, LP), BF16),
            dma((G, M)), dma((G, M)), dma((G, M)), dma((G, M)),
        ]
    out, gw1, gw2, vec = pl.pallas_call(
        functools.partial(kernel, D, M, U, LP, K, R),
        out_shape=[
            jax.ShapeDtypeStruct((U, R), BF16),
            jax.ShapeDtypeStruct((U, K), BF16),
            jax.ShapeDtypeStruct((U, -(-M * U // 128) * 128), BF16),
            jax.ShapeDtypeStruct((8, LP), F32),
        ],
        in_specs=[vmem] * 9 + [hbm, hbm, hbm],
        out_specs=[hbm, hbm, hbm, vmem],
        scratch_shapes=scratch,
        compiler_params=pltpu.CompilerParams(
            collective_id=0, has_side_effects=True, vmem_limit_bytes=64 * 2**20 - 2**16
        ),
    )(ids[None, :], hash_mult[None, :], hash_add[None, :], *par, w1, w2, cot)
    out, gw1, gw2, *v = pl.pallas_call(
        functools.partial(finish, U),
        out_shape=[
            jax.ShapeDtypeStruct((U, R), BF16),
            jax.ShapeDtypeStruct((U, K), F32),
            jax.ShapeDtypeStruct((U, M * U), F32),
        ]
        + [jax.ShapeDtypeStruct((1, U), F32)] * 6,
        in_specs=[hbm, hbm, hbm, vmem],
        out_specs=[hbm, hbm, hbm] + [vmem] * 6,
        scratch_shapes=[
            pltpu.VMEM((U, R), BF16),
            pltpu.VMEM((U, K), BF16),
            pltpu.VMEM(gw2.shape, BF16),
            pltpu.VMEM((U, K), F32),
            pltpu.VMEM((U, M * U), F32),
            dma((6,)),
            dma((6,)),
        ],
        compiler_params=pltpu.CompilerParams(vmem_limit_bytes=63 * 2**20),
    )(out, gw1, gw2, vec)
    v = [x[0] for x in v]
    return (out, gw1, v[0], v[1], v[2], gw2, v[3], v[4], v[5])


def solution(mesh):
    return jax.shard_map(
        per_device,
        mesh=mesh,
        in_specs=(
            P("dp"), P(), P(), P("mp", None), P("mp"), P("mp"), P("mp"),
            P("mp", None), P("mp"), P("mp"), P("mp"), P("mp", "dp"),
        ),
        out_specs=(
            P("mp", "dp"), P("mp", None), P("mp"), P("mp"), P("mp"),
            P("mp", None), P("mp"), P("mp"), P("mp"),
        ),
        check_vma=False,
    )
```

```python
import functools

import jax
import jax.numpy as jnp
from jax import lax
from jax.experimental import pallas as pl
from jax.experimental.pallas import tpu as pltpu
from jax.sharding import PartitionSpec as P

MESH = pl.DeviceIdType.MESH
F32, BF16, I32 = jnp.float32, jnp.bfloat16, jnp.int32
epsilon = 1e-05


def dot(a, b):
    return lax.dot_general(a, b, (((1,), (0,)), ((), ())), preferred_element_type=F32)


def dot_nt(a, b):
    return lax.dot_general(a, b, (((1,), (1,)), ((), ())), preferred_element_type=F32)


def mish_parts(v):
    u = jnp.exp(jnp.minimum(v, 20.0))
    n = u * (u + 2.0)
    d = n + 2.0
    r = pl.reciprocal(d, approx=True)
    t = n * r
    return v * t, t + v * ((4.0 * (n - u) * r) * r)


def mish(v):
    u = jnp.exp(jnp.minimum(v, 20.0))
    n = u * (u + 2.0)
    d = n + 2.0
    r = pl.reciprocal(d, approx=True)
    return v * (n * r)


def lane_part(x):
    out = x[:, :128]
    for at in range(128, x.shape[1], 128):
        out = out + x[:, at : at + 128]
    return out


def kernel(
    D, M, U, LP, K, R,
    ids_ref, mult_ref, add_ref, b1_ref, s1_ref, t1_ref, b2_ref, s2_ref, t2_ref, w1_ref, w2_ref, cot_ref,
    out_ref, gw1_ref, gw2_ref, vec_ref,
    A, B, C, W2, G1, E1, F, H, act2, slo2, col, RW, acc, hcol,
    pv, ar1, ar2, ar2z, ar3, ar3z, ar4, ar4s, ar4z,
    w1s, w1r, w2s, w2r, pvs, pvr, cts, ctr, loc,
    a1s, a1r, a2s, a2r, a2zs, a2zr, a3s, a3r, a3zs, a3zr, a4s, a4r, a4zs, a4zr,
    g1s, g1r, g2s, g2r, free, *extra,
):
    Q = R // M
    G = D // 8
    TL = min(512, Q)
    NT = Q // TL
    PER = K // LP
    NA = M // PER
    K8 = K // 8
    J8 = M * LP // 8
    S8 = LP // 8
    N = float(R * D)
    d = lax.axis_index("dp")
    m = lax.axis_index("mp")
    i = lax.rem(d, 8)
    c = lax.rem(i, 2)
    x = lax.rem(i // 2, 2)
    y = i // 4
    hi = (1 - c) * x + c * y
    lo = (1 - c) * y + c * x
    p = 4 * c + 2 * hi + lo
    core_dev = (d + 1 - 2 * c, m)
    flip_x = d + 2 - 4 * x
    flip_y = d + 4 - 8 * y
    hi_dev = ((1 - c) * flip_x + c * flip_y, m)
    lo_dev = ((1 - c) * flip_y + c * flip_x, m)
    up = [lax.rem(m + k, M) for k in range(M)]
    down = [lax.rem(m - k + M, M) for k in range(M)]
    others = [lax.rem(d + k, D) for k in range(D)]
    sent = []

    def remote(src, dst, ss, rs, dev):
        cp = pltpu.make_async_remote_copy(
            src_ref=src, dst_ref=dst, send_sem=ss, recv_sem=rs, device_id=dev, device_id_type=MESH
        )
        return cp

    def send(src, dst, ss, rs, dev):
        cp = remote(src, dst, ss, rs, dev)
        cp.start()
        sent.append(cp)
        return cp

    def gone(cp):
        cp.wait_send()
        sent[:] = [other for other in sent if other is not cp]

    def lanes(ref, at, size):
        return ref.at[:, pl.ds(pl.multiple_of(at, 128), size)]

    def rows(ref, at, size):
        return ref.at[pl.ds(pl.multiple_of(at, 16), size)]

    bar = pltpu.get_barrier_semaphore()
    greeted = [core_dev, hi_dev, lo_dev] if G == 1 else [(others[k], m) for k in range(1, D)]
    greeted += [(d, up[k]) for k in range(1, M)]
    for dev in greeted:
        pl.semaphore_signal(bar, inc=1, device_id=dev, device_id_type=MESH)

    w2_loc = pltpu.make_async_copy(w2_ref, G1, loc.at[1])
    w2_loc.start()
    w1_loc = pltpu.make_async_copy(w1_ref, C.at[m], loc.at[0])
    w1_loc.start()
    cot_loc = pltpu.make_async_copy(lanes(cot_ref, m * Q, Q), lanes(F.at[m], 0, Q), loc.at[2])
    pv[m] = jnp.zeros((8, LP), F32)
    for n, ref in enumerate((b1_ref, s1_ref, t1_ref, b2_ref, s2_ref, t2_ref)):
        pv[m, n : n + 1, :U] = ref[...]
    pl.semaphore_wait(bar, len(greeted))

    ag1, ag2, agp, ct = {}, {}, {}, {}
    for k in range(1, M):
        agp[k] = send(pv.at[m], pv.at[m], pvs.at[k], pvr.at[k], (d, up[k]))
    for ag, own, buf, size, ss, rs in ((ag1, w1_ref, C, K8, w1s, w1r), (ag2, None, W2, J8, w2s, w2r)):
        for k in range(1, M):
            part = lanes(buf.at[m], p * size, size)
            mine = part if own is None else lanes(own, p * size, size)
            ag[0, k] = remote(mine, part, ss.at[0, k], rs.at[0, k], (d, up[k]))
            for step, dev, at, width in (
                (1, lo_dev, p, 1), (2, hi_dev, 4 * c + 2 * hi, 2), (3, core_dev, 4 * c, 4)
            ):
                part = lanes(buf.at[down[k]], at * size, width * size)
                ag[step, k] = remote(part, part, ss.at[step, k], rs.at[step, k], dev)
    for k in range(1, M):
        ag1[0, k].start()
    w2_loc.wait()
    for b in range(M):
        W2[m, :, (b + 1) * LP - 128 : (b + 1) * LP] = jnp.zeros((U, 128), BF16)
        W2[m, :, b * LP : b * LP + U] = G1[:, b * U : (b + 1) * U]

    def gather_stage(step, ag):
        for k in range(1, M):
            ag[step - 1, k].wait_recv()
            ag[step, k].start()

    def stage1(step):
        gather_stage(step, ag1)

    def stage2(step):
        gather_stage(step, ag2)

    hrow = jnp.concatenate(
        [mult_ref[...].astype(F32), add_ref[...].astype(F32), jnp.zeros((126, K), F32)], axis=0
    )
    hcol[...] = hrow.T

    HT = 128

    def encode(q, put):
        def step(t, _):
            at = pl.multiple_of(t * HT, HT)
            both = hcol[pl.ds(at, HT), :].astype(I32)
            v = both[:, 0:1] * ids_ref[:, pl.ds(pl.multiple_of(q * Q, 128), Q)] + both[:, 1:2]
            for _ in range(2):
                top = lax.shift_right_logical(v, 16)
                v = (v & 65535) + ((top << 4) - top)
            v = jnp.where(v >= 65521, v - 65521, v)
            put(t, (v.astype(F32) * (2.0 / 65520.0) - 1.0).astype(BF16))
            return 0

        lax.fori_loop(0, K // HT, step, 0)

    def make_col(b):
        col[b] = jnp.concatenate([RW[b], jnp.zeros((128 - RW.shape[1], LP), F32)], axis=0).T

    def make_cols():
        def step(b, _):
            make_col(b)
            return 0

        lax.fori_loop(0, M, step, 0)

    def to_a(q):
        def put(t, value):
            A[q, pl.ds(pl.multiple_of(t * HT, HT), HT), :] = value

        return put

    def to_e1(t, value):
        E1[pl.ds(pl.multiple_of(lax.rem(t, LP // HT) * HT, HT), HT), pl.ds(pl.multiple_of(t // (LP // HT) * Q, 128), Q)] = value

    def row_of(slot):
        return jnp.sum(acc[slot].T, axis=0, keepdims=True)

    acc[...] = jnp.zeros_like(acc)
    for b in range(M):
        B[pl.ds(b * LP + U // 16 * 16, LP - U // 16 * 16), :] = jnp.zeros((LP - U // 16 * 16, R), BF16)

    RW[...] = jnp.zeros_like(RW)
    RW[m, 0:8] = pv[m]
    make_col(m)
    encode(m, to_a(m))
    w1_loc.wait()

    def mm1_own(b):
        def step(t, _):
            at = pl.multiple_of(t * TL, TL)
            act, slope = mish_parts(dot(C[b], A[m, :, pl.ds(at, TL)]) + col[b, :U, 0:1])
            H[b, :, pl.ds(at, TL)] = slope.astype(BF16)
            B[pl.ds(pl.multiple_of(b * LP, LP), U), pl.ds(pl.multiple_of(m * Q + t * TL, TL), TL)] = act.astype(BF16)
            acc[0, :U] += lane_part(act)
            acc[1, :U] += lane_part(act * act)
            return 0

        lax.fori_loop(0, NT, step, 0)

    def mm1_rest(b):
        def step(t, _):
            q = lax.rem(m + t, M)
            act = mish(dot(C[b], A[q]) + col[b, :U, 0:1])
            B[pl.ds(pl.multiple_of(b * LP, LP), U), pl.ds(pl.multiple_of(q * Q, Q), Q)] = act.astype(BF16)
            acc[0, :U] += lane_part(act)
            acc[1, :U] += lane_part(act * act)
            return 0

        lax.fori_loop(1, M, step, 0)

    def mm1_sums(b):
        ar1[d, pl.ds(b, 1), :] = row_of(0)
        ar1[d, pl.ds(b + M, 1), :] = row_of(1)
        acc[0:2] = jnp.zeros((2, LP, 128), F32)

    mm1_own(m)
    stage1(1)
    for k in range(1, M):
        ag2[0, k].start()

    def enc_step(k, _):
        q = lax.rem(m + M - k, M)
        encode(q, to_a(q))
        return 0

    lax.fori_loop(1, M, enc_step, 0)
    stage1(2)
    mm1_rest(m)
    mm1_sums(m)
    stage2(1)
    cot_loc.start()
    for q in range(1, M):
        ct[q] = send(
            lanes(cot_ref, up[q] * Q, Q), lanes(F.at[m], 0, Q), cts.at[q], ctr.at[q], (d, up[q])
        )
    stage1(3)
    for k in range(1, M):
        agp[k].wait_recv()
    for b in range(M):
        RW[b, 0:8] = pv[b]
    make_cols()
    def mm1_other(k, _):
        b = lax.rem(m + M - k, M)
        part = lanes(C.at[b], 4 * c * K8, 4 * K8)
        remote(part, part, w1s.at[3, k], w1r.at[3, k], core_dev).wait_recv()
        mm1_own(b)
        mm1_rest(b)
        mm1_sums(b)
        pl.when(k == 1)(functools.partial(stage2, 2))
        return 0

    lax.fori_loop(1, M, mm1_other, 0)

    def all_dp(buf, ss, rs):
        cps = []
        for k in range(1, D):
            cps.append(send(buf.at[d], buf.at[d], ss.at[k], rs.at[k], (others[k], m)))
        return cps

    def total(buf, cps):
        for cp in cps:
            cp.wait_recv()
        out = buf[0]
        for k in range(1, D):
            out = out + buf[k]
        return out

    cps1 = all_dp(ar1, a1s, a1r)
    stage2(3)
    for cp in ag1.values():
        cp.wait_send()
    cot_all = []
    for q in range(M):
        cp = pltpu.make_async_copy(lanes(cot_ref, q * Q, Q), lanes(C.at[q], 0, Q), loc.at[3 + q])
        cot_all.append(cp)
        cp.start()
    for k in range(1, M):
        ag2[3, k].wait_recv()

    def make_e1(b):
        def step(h, _):
            part = W2[h, :, pl.ds(pl.multiple_of(b * LP, LP), LP)].astype(F32) * col[h, :U, 1:2]
            for n in range(LP // 128):
                acc[n, :U] = part[:, n * 128 : (n + 1) * 128]
            for n in range(LP // 128):
                E1[n * 128 : (n + 1) * 128, pl.ds(pl.multiple_of(h * LP, LP), LP)] = acc[n].T.astype(BF16)
            return 0

        lax.fori_loop(0, M, step, 0)
        acc[...] = jnp.zeros_like(acc)

    const = jnp.zeros((8, M * LP), F32)
    for b in range(M):
        shift = jnp.broadcast_to(pv[b, 2:3, :U], (8, U))
        upper = shift.astype(BF16)
        lower = (shift - upper.astype(F32)).astype(BF16)
        const = const + dot(upper, W2[b]) + dot(lower, W2[b])
    for b in range(M):
        RW[b, 8:9] = const[0:1, b * LP : (b + 1) * LP] + pv[b, 3:4]
    make_e1(m)

    tot = total(ar1, cps1)
    mean = tot[:M] / N
    inv = lax.rsqrt(tot[M:] / N - mean * mean + epsilon)
    for b in range(M):
        RW[b, 9:10] = inv[b : b + 1]
        RW[b, 10:11] = -mean[b : b + 1] * inv[b : b + 1]
    make_cols()
    for cp in cot_all:
        cp.wait()

    def mm2(t, _):
        at = pl.multiple_of(t * TL, TL)
        for b in range(M):
            part = B[b * LP : b * LP + U, pl.ds(at, TL)].astype(F32)
            B[b * LP : b * LP + U, pl.ds(at, TL)] = (part * col[b, :U, 9:10] + col[b, :U, 10:11]).astype(BF16)
        v = dot(E1[:U], B[:, pl.ds(at, TL)]) + col[m, :U, 8:9]
        act, slope = mish_parts(v)
        act2[:, pl.ds(at, TL)] = act.astype(BF16)
        slo2[:, pl.ds(at, TL)] = slope.astype(BF16)
        g = C[t // NT, :, pl.ds(pl.multiple_of(lax.rem(t, NT) * TL, TL), TL)].astype(F32)
        acc[0, :U] += lane_part(act)
        acc[1, :U] += lane_part(act * act)
        acc[2, :U] += lane_part(g)
        acc[3, :U] += lane_part(g * act)
        return 0

    lax.fori_loop(0, M * NT, mm2, 0)
    for s in range(4):
        ar2[d, s : s + 1, :] = row_of(s)
    ar2[d, 4:8, :] = jnp.zeros((4, LP), F32)
    acc[...] = jnp.zeros_like(acc)
    cps2 = all_dp(ar2, a2s, a2r)

    def a_at(base, b):
        return base + b // PER, pl.multiple_of(lax.rem(b, PER) * LP, LP)

    def mm2_own(b):
        make_e1(b)
        act_at, row = a_at(0, b)
        v = dot(E1[:U], B[:, pl.ds(pl.multiple_of(m * Q, Q), Q)]) + col[b, :U, 8:9]
        act, slope = mish_parts(v)
        A[act_at, pl.ds(row, U)] = act.astype(BF16)
        A[act_at + NA, pl.ds(row, U)] = slope.astype(BF16)

    def own_loop(k, _):
        mm2_own(lax.rem(m + k, M))
        return 0

    mm2_own(up[1])
    tot = total(ar2, cps2)
    mean = tot[0:1] / N
    inv = lax.rsqrt(tot[1:2] / N - mean * mean + epsilon)
    sum_g = tot[2:3]
    sum_gn = inv * (tot[3:4] - mean * sum_g)
    k1 = pv[m, 4:5] * inv
    k2 = -k1 * inv * sum_gn / N
    k3 = -k1 * sum_g / N - mean * k2
    ar2z[m, 0:1] = k1
    ar2z[m, 1:2] = k2
    ar2z[m, 2:3] = k3
    ar2z[m, 3:4] = k1
    ar2z[m, 4:5] = pv[m, 5:6] - mean * k1
    ar2z[m, 5:6] = sum_g
    ar2z[m, 6:7] = sum_gn
    ar2z[m, 7:8] = jnp.zeros((1, LP), F32)
    cps2z = [send(ar2z.at[m], ar2z.at[m], a2zs.at[k], a2zr.at[k], (d, up[k])) for k in range(1, M)]
    RW[m, 16:24] = ar2z[m]
    make_col(m)

    def back2(t, _):
        at = pl.multiple_of(t * TL, TL)
        a = act2[:, pl.ds(at, TL)].astype(F32)
        g = C[t // NT, :, pl.ds(pl.multiple_of(lax.rem(t, NT) * TL, TL), TL)].astype(F32)
        grad = (g * col[m, :U, 16:17] + a * col[m, :U, 17:18] + col[m, :U, 18:19]) * slo2[:, pl.ds(at, TL)].astype(F32)
        grad = grad.astype(BF16)
        slo2[:, pl.ds(at, TL)] = grad
        acc[0, :U] += lane_part(grad.astype(F32))
        return 0

    lax.fori_loop(0, M * NT, back2, 0)
    gb2 = row_of(0)
    ar3[d, 2 * M : 2 * M + 1, :] = gb2
    ar3[d, 2 * M + 1 : 2 * M + 8, :] = jnp.zeros((7, LP), F32)
    acc[0:1] = jnp.zeros((1, LP, 128), F32)

    L1 = pl.multiple_of(lax.rem(m + 1, M) * Q, 128)
    LR = pl.multiple_of(L1 + LP, 128)

    def rowsum(x):
        acc[0, :U] = lane_part(x[:, : U // 128 * 128]) + jnp.where(
            lax.broadcasted_iota(I32, (U, 128), 1) >= 128 - U % 128, x[:, U - 128 :], 0.0
        )
        return row_of(0)

    gb2_all8 = jnp.broadcast_to(gb2[:, :U], (8, U))
    gb2_up = gb2_all8.astype(BF16)
    gb2_low = (gb2_all8 - gb2_up.astype(F32)).astype(BF16)
    ar3[d, 0 : 2 * M, :] = jnp.zeros((2 * M, LP), F32)

    def grad_w2(b, _):
        at = pl.multiple_of(b * LP, LP)
        g = dot_nt(B[pl.ds(at, LP), :], slo2[...])
        w16 = W2[b, :, pl.ds(pl.multiple_of(m * LP, LP), LP)][:, :U]
        w = w16.astype(F32)
        ar3[d, pl.ds(b, 1), :U] = dot_nt(gb2_up, w16)[0:1] + dot_nt(gb2_low, w16)[0:1]
        ar3[d, pl.ds(b + M, 1), :] = rowsum(w * g[:U])
        g = g * col[b, :, 1:2] + col[b, :, 2:3] * gb2[:, :U]
        B[pl.ds(at, LP), pl.ds(L1, U)] = g.astype(BF16)
        B[pl.ds(at, LP), pl.ds(L1 + U // 128 * 128, LP - U // 128 * 128)] = jnp.where(
            lax.broadcasted_iota(I32, (LP, LP - U // 128 * 128), 1) < U - U // 128 * 128,
            B[pl.ds(at, LP), pl.ds(L1 + U // 128 * 128, LP - U // 128 * 128)].astype(F32),
            0.0,
        ).astype(BF16)
        return 0

    lax.fori_loop(0, M, grad_w2, 0)
    cps3 = all_dp(ar3, a3s, a3r)
    for n, dev in ((0, core_dev), (1, hi_dev), (2, lo_dev)):
        pl.semaphore_signal(free.at[n], inc=1, device_id=dev, device_id_type=MESH)
    for k in range(1, M):
        pl.semaphore_signal(free.at[2 + k], inc=1, device_id=(d, up[k]), device_id_type=MESH)

    HALF = {0: (1 - c) * 4, 1: 4 * c + 2 * (1 - hi), 2: 4 * c + 2 * hi + 1 - lo}
    KEEP = {0: 4 * c, 1: 4 * c + 2 * hi, 2: p}
    START = {0: 0, 1: 4, 2: 6}
    PARTNER = {0: core_dev, 1: hi_dev, 2: lo_dev}
    g2cp = {}

    def b_rows(b, at, size, lane):
        return B.at[pl.ds(pl.multiple_of(b * LP + at * S8, 16), size * S8), pl.ds(lane, LP)]

    def g2_send(n):
        pl.semaphore_wait(free.at[n], 1)
        for b in range(M):
            g2cp[n, b].start()

    def g2_add(n):
        for b in range(M):
            g2cp[n, b].wait_recv()
            size = (4 >> n) * S8
            keep = pl.ds(pl.multiple_of(b * LP + KEEP[n] * S8, 16), size)
            came = pl.ds(b * LP + START[n] * S8, size)
            B[keep, pl.ds(L1, LP)] = (
                B[keep, pl.ds(L1, LP)].astype(F32) + B[came, pl.ds(LR, LP)].astype(F32)
            ).astype(BF16)

    def l2_of(z):
        return pl.multiple_of(lax.rem(z + 2, M) * Q, 128)

    L2 = l2_of(m)
    for b in range(M):
        for n in range(3):
            g2cp[n, b] = remote(
                b_rows(b, HALF[n], 4 >> n, L1), b_rows(b, START[n], 4 >> n, LR), g2s.at[n, b], g2r.at[n, b], PARTNER[n]
            )
        for n, at, size, dev in ((4, p, 1, lo_dev), (5, 4 * c + 2 * hi, 2, hi_dev), (6, 4 * c, 4, core_dev)):
            part = b_rows(b, at, size, L2)
            g2cp[n, b] = remote(part, part, g2s.at[n, b], g2r.at[n, b], dev)
        if b:
            g2cp[3, b] = remote(
                b_rows(up[b], p, 1, L1),
                B.at[pl.ds(pl.multiple_of(m * LP + p * S8, 16), S8), pl.ds(l2_of(up[b]), LP)],
                g2s.at[3, b], g2r.at[3, b], (d, up[b]),
            )

    if G > 1:
        x1, x2, x1s, x1r, x2s, x2r = extra

    def g2_groups():
        cps = []
        for k in range(1, G):
            to = (lax.rem(d + 8 * k, D), m)
            for b in range(M):
                cps.append(send(b_rows(b, p, 1, L1), x2.at[d // 8, b], x2s.at[k, b], x2r.at[k, b], to))
        for b in range(M):
            x2[d // 8, b] = B[pl.ds(pl.multiple_of(b * LP + p * S8, 16), S8), pl.ds(L1, LP)]
        for cp in cps:
            cp.wait_recv()
        for cp in cps:
            gone(cp)
        for b in range(M):
            v = x2[0, b].astype(F32)
            for k in range(1, G):
                v = v + x2[k, b].astype(F32)
            B[pl.ds(pl.multiple_of(b * LP + p * S8, 16), S8), pl.ds(L1, LP)] = v.astype(BF16)

    def g2_z():
        if G > 1:
            g2_groups()
        for k in range(1, M):
            pl.semaphore_wait(free.at[2 + M - k], 1)
            g2cp[3, k].start()
        mine = pl.ds(pl.multiple_of(m * LP + p * S8, 16), S8)
        B[mine, pl.ds(L2, LP)] = B[mine, pl.ds(L1, LP)]

    def g2_gather(n):
        for b in range(1 if n == 4 else 0, M):
            g2cp[n - 1, b].wait_recv()
        for b in range(M):
            g2cp[n, b].start()

    g2_send(0)
    lax.fori_loop(2, M, own_loop, 0)
    tot = total(ar3, cps3)
    ar3z[m] = tot[: 2 * M]
    gb2_all = tot[2 * M : 2 * M + 1]
    cps3z = [send(ar3z.at[m], ar3z.at[m], a3zs.at[k], a3zr.at[k], (d, up[k])) for k in range(1, M)]
    g2_add(0)
    g2_send(1)
    encode(m, to_e1)
    for cp in cps2z:
        cp.wait_recv()
    for b in range(M):
        RW[b, 16:24] = ar2z[b]
    for cp in cps3z:
        cp.wait_recv()
    tot = ar3z[0]
    for b in range(1, M):
        tot = tot + ar3z[b]
    for b in range(M):
        k1 = pv[b, 1:2] * RW[b, 9:10]
        RW[b, 24:25] = k1
        RW[b, 25:26] = -k1 * tot[M + b : M + b + 1] / N
        RW[b, 26:27] = -k1 * tot[b : b + 1] / N
    make_cols()
    pick = lax.broadcasted_iota(I32, (2 * M, 1), 0)
    vec_ref[0:1, :] = jnp.zeros((1, LP), F32)
    vec_ref[1:2, :] = jnp.sum(jnp.where(pick == M + m, tot, 0.0), axis=0, keepdims=True)
    vec_ref[2:3, :] = jnp.sum(jnp.where(pick == m, tot, 0.0), axis=0, keepdims=True)
    vec_ref[3:4, :] = gb2_all
    vec_ref[4:5, :] = ar2z[m, 6:7]
    vec_ref[5:6, :] = ar2z[m, 5:6]
    vec_ref[6:8, :] = jnp.zeros((2, LP), F32)

    PADAT = U // 16 * 16

    def put_grad(b, value, at, size):
        slot, row = a_at(NA, b)
        A[slot, pl.ds(row, U), pl.ds(at, size)] = value

    for b in range(M):
        slot, row = NA + b // PER, (b % PER) * LP
        A[slot, row + PADAT : row + LP, :] = jnp.where(
            lax.broadcasted_iota(I32, (LP - PADAT, Q), 0) < U - PADAT,
            A[slot, row + PADAT : row + LP, :].astype(F32),
            0.0,
        ).astype(BF16)
    cot_loc.wait()

    def back2_own(b):
        act_at, row = a_at(0, b)

        def step(t, _):
            at = pl.multiple_of(t * TL, TL)
            a = A[act_at, pl.ds(row, U), pl.ds(at, TL)].astype(F32)
            s = A[act_at + NA, pl.ds(row, U), pl.ds(at, TL)].astype(F32)
            g = F[b, :, pl.ds(at, TL)].astype(F32)
            grad = (g * col[b, :U, 16:17] + a * col[b, :U, 17:18] + col[b, :U, 18:19]) * s
            A[act_at + NA, pl.ds(row, U), pl.ds(at, TL)] = grad.astype(BF16)
            return 0

        lax.fori_loop(0, NT, step, 0)

    def copy_own(t, _):
        at = pl.multiple_of(t * TL, TL)
        put_grad(m, slo2[:, pl.ds(pl.multiple_of(m * Q + t * TL, TL), TL)], at, TL)
        return 0

    lax.fori_loop(0, NT, copy_own, 0)
    for k in range(1, M):
        ct[k].wait_recv()
        back2_own(down[k])


    def back1(b):
        def step(t, _):
            at = pl.multiple_of(t * TL, TL)
            dh = dot(W2[b, :, 0:K], A[NA, :, pl.ds(at, TL)])
            for n in range(1, NA):
                dh = dh + dot(W2[b, :, n * K : (n + 1) * K], A[NA + n, :, pl.ds(at, TL)])
            norm = B[pl.ds(pl.multiple_of(b * LP, LP), U), pl.ds(pl.multiple_of(m * Q + t * TL, TL), TL)].astype(F32)
            grad = dh * col[b, :U, 24:25] + norm * col[b, :U, 25:26] + col[b, :U, 26:27]
            grad = (grad * H[b, :, pl.ds(at, TL)].astype(F32)).astype(BF16)
            H[b, :, pl.ds(at, TL)] = grad
            acc[0, :U] += lane_part(grad.astype(F32))
            return 0

        lax.fori_loop(0, NT, step, 0)
        ar4[d, pl.ds(b, 1), :] = row_of(0)
        acc[0:1] = jnp.zeros((1, LP, 128), F32)

        def mm(t, _):
            F[b, :, pl.ds(pl.multiple_of(t * LP, LP), LP)] = dot_nt(
                H[b], E1[:, pl.ds(pl.multiple_of(t * Q, Q), Q)]
            ).astype(BF16)
            return 0

        lax.fori_loop(0, PER, mm, 0)

    acc[0:1] = jnp.zeros((1, LP, 128), F32)
    ar4[d] = jnp.zeros((ar4.shape[1], LP), F32)
    K2 = 4 * K8
    FROM = {0: 0, 1: K2, 2: K2 + 2 * K8}
    order = [up[(j + 1) % M] for j in range(M)]
    def g1_cp(n, j):
        b = lax.rem(m + 1 + j, M)
        if n == 3:
            return remote(
                lanes(F.at[b], p * K8, K8), C.at[m, :, pl.ds(K - K8, K8)], g1s.at[3, j + 1], g1r.at[3, j + 1], (d, b)
            )
        return remote(
            lanes(F.at[b], HALF[n] * K8, K2 >> n), lanes(C.at[b], FROM[n], K2 >> n), g1s.at[n, j], g1r.at[n, j], PARTNER[n]
        )

    def g1_groups(b, j):
        mine = pl.ds(pl.multiple_of(p * K8, 128), K8)
        cps = []
        for k in range(1, G):
            to = (lax.rem(d + 8 * k, D), m)
            cps.append(send(lanes(F.at[b], p * K8, K8), x1.at[d // 8, j], x1s.at[k, j], x1r.at[k, j], to))
        x1[d // 8, j] = F[b, :, mine]
        for cp in cps:
            cp.wait_recv()
        for cp in cps:
            gone(cp)
        v = x1[0, j].astype(F32)
        for k in range(1, G):
            v = v + x1[k, j].astype(F32)
        F[b, :, mine] = v.astype(BF16)

    def g1_stage(n, j):
        b = lax.rem(m + 1 + j, M)
        g1_cp(n - 1, j).wait_recv()
        keep = pl.ds(pl.multiple_of(KEEP[n - 1] * K8, 128), K2 >> (n - 1))
        came = C[b, :, FROM[n - 1] : FROM[n - 1] + (K2 >> (n - 1))]
        F[b, :, keep] = (F[b, :, keep].astype(F32) + came.astype(F32)).astype(BF16)
        if n == 3 and G > 1:
            g1_groups(b, j)
        if n < 3 or not isinstance(j, int) or j < M - 1:
            g1_cp(n, j).start()
        else:
            C[m, :, K - K8 : K] = F[m, :, pl.ds(pl.multiple_of(p * K8, 128), K8)]

    def block(j, _):
        back1(lax.rem(m + 1 + j, M))
        g1_cp(0, j).start()
        for n in (3, 2, 1):
            pl.when(j >= n)(functools.partial(g1_stage, n, j - n))

        @pl.when(j == 0)
        def _():
            g2_add(1)
            g2_send(2)

        @pl.when(j == 1)
        def _():
            g2_add(2)
            g2_z()

        pl.when(j == 2)(functools.partial(g2_gather, 4))
        pl.when(j == 3)(functools.partial(g2_gather, 5))
        return 0

    lax.fori_loop(0, M, block, 0)
    cps4 = all_dp(ar4, a4s, a4r)
    for n in (3, 2, 1):
        g1_stage(n, M - n)
    g2_gather(6)

    def finish(t, _):
        at = pl.multiple_of(t * TL, TL)
        a = act2[:, pl.ds(at, TL)].astype(F32)
        act2[:, pl.ds(at, TL)] = (a * col[m, :U, 19:20] + col[m, :U, 20:21]).astype(BF16)
        return 0

    lax.fori_loop(0, M * NT, finish, 0)
    out_copy = pltpu.make_async_copy(act2, out_ref, loc.at[0])
    out_copy.start()
    tot4 = total(ar4, cps4)
    for b in range(M):
        ar4s[b] = jnp.broadcast_to(tot4[b : b + 1], (8, LP))
    ar4z[m] = ar4s[m]
    cps4z = [send(ar4s.at[up[k]], ar4z.at[m], a4zs.at[k], a4zr.at[k], (d, up[k])) for k in range(1, M)]
    g1_stage(3, M - 2)
    g1_stage(2, M - 1)
    g1_stage(3, M - 1)
    for b in range(M):
        g2cp[6, b].wait_recv()
    for b in range(M):
        slo2[:, b * U : (b + 1) * U] = B[b * LP : b * LP + U, pl.ds(L2, LP)][:, :U]
    gw2_copy = pltpu.make_async_copy(lanes(slo2, 0, gw2_ref.shape[1]), gw2_ref, loc.at[2])
    gw2_copy.start()
    for j in range(M - 1):
        g1_cp(3, j).wait_recv()
    v = C[0, :, K - K8 : K].astype(F32)
    for b in range(1, M):
        v = v + C[b, :, K - K8 : K].astype(F32)
    G1[:, pl.ds(pl.multiple_of(p * K8, 128), K8)] = v.astype(BF16)
    diag_dev = (d + 2 - 4 * x + 4 - 8 * y, m)
    mine = lanes(G1, p * K8, K8)
    ga = [send(mine, mine, g1s.at[4, n], g1r.at[4, n], dev) for n, dev in enumerate((diag_dev, hi_dev, lo_dev))]
    for cp in ga:
        cp.wait_recv()
    part = lanes(G1, 4 * c * K8, K2)
    ga = send(part, part, g1s.at[4, 3], g1r.at[4, 3], core_dev)
    for cp in cps4z:
        cp.wait_recv()
    v = ar4z[0]
    for b in range(1, M):
        v = v + ar4z[b]
    vec_ref[0:1, :] = v[0:1]
    ga.wait_recv()
    gw1_copy = pltpu.make_async_copy(lanes(G1, 0, K), gw1_ref, loc.at[1])
    gw1_copy.start()
    for cp in [*ag2.values(), *g2cp.values(), *(g1_cp(n, j) for n in range(4) for j in range(M - n // 3))]:
        cp.wait_send()
    out_copy.wait()
    gw1_copy.wait()
    gw2_copy.wait()
    for cp in sent:
        cp.wait_send()


def finish(U, out_in, gw1_in, gw2_in, vec_in, out_ref, gw1_ref, gw2_ref, *tail):
    *vecs, held, held1, held2, wide1, wide2, sem_in, sem_out = tail
    n = 4
    width = held.shape[1] // n
    pieces = [pl.ds(k * width, width) for k in range(n)]
    ins = [
        pltpu.make_async_copy(gw2_in, held2, sem_in.at[n]),
        pltpu.make_async_copy(gw1_in, held1, sem_in.at[n + 1]),
    ] + [pltpu.make_async_copy(out_in.at[:, at], held.at[:, at], sem_in.at[k]) for k, at in enumerate(pieces)]
    for cp in ins:
        cp.start()
    outs = [
        pltpu.make_async_copy(wide2, gw2_ref, sem_out.at[n]),
        pltpu.make_async_copy(wide1, gw1_ref, sem_out.at[n + 1]),
    ] + [pltpu.make_async_copy(held.at[:, at], out_ref.at[:, at], sem_out.at[k]) for k, at in enumerate(pieces)]
    ins[0].wait()
    wide2[...] = held2[:, : wide2.shape[1]].astype(F32)
    outs[0].start()
    ins[1].wait()
    wide1[...] = held1[...].astype(F32)
    outs[1].start()
    for k in range(n):
        ins[2 + k].wait()
        outs[2 + k].start()
    for k, ref in enumerate(vecs):
        ref[...] = vec_in[k : k + 1, :U]
    for cp in outs:
        cp.wait()


def per_device(ids, hash_mult, hash_add, w1, b1, s1, t1, w2, b2, s2, t2, cot):
    D, M = lax.axis_size("dp"), lax.axis_size("mp")
    U, K = w1.shape
    R = ids.shape[0]
    Q = R // M
    LP = -(-U // 128) * 128
    G = D // 8
    par = [x[None, :] for x in (b1, s1, t1, b2, s2, t2)]
    dma = pltpu.SemaphoreType.DMA
    vmem = pl.BlockSpec(memory_space=pltpu.VMEM)
    hbm = pl.BlockSpec(memory_space=pl.ANY)
    AR = -(-2 * M // 8) * 8
    scratch = [
        pltpu.VMEM((M, K, Q), BF16),
        pltpu.VMEM((M * LP, R), BF16),
        pltpu.VMEM((M, U, max(K, Q)), BF16),
        pltpu.VMEM((M, U, M * LP), BF16),
        pltpu.VMEM((U, max(K, M * U)), BF16),
        pltpu.VMEM((LP, M * LP), BF16),
        pltpu.VMEM((M, U, max(K, Q)), BF16),
        pltpu.VMEM((M, U, Q), BF16),
        pltpu.VMEM((U, R), BF16),
        pltpu.VMEM((U, R), BF16),
        pltpu.VMEM((M, LP, 128), F32),
        pltpu.VMEM((M, 32, LP), F32),
        pltpu.VMEM((4, LP, 128), F32),
        pltpu.VMEM((K, 128), F32),
        pltpu.VMEM((M, 8, LP), F32),
        pltpu.VMEM((D, AR, LP), F32),
        pltpu.VMEM((D, 8, LP), F32),
        pltpu.VMEM((M, 8, LP), F32),
        pltpu.VMEM((D, AR + 8, LP), F32),
        pltpu.VMEM((M, AR, LP), F32),
        pltpu.VMEM((D, 8, LP), F32),
        pltpu.VMEM((M, 8, LP), F32),
        pltpu.VMEM((M, 8, LP), F32),
        dma((4, M)), dma((4, M)), dma((4, M)), dma((4, M)),
        dma((M,)), dma((M,)), dma((M,)), dma((M,)), dma((3 + M,)),
        dma((D,)), dma((D,)), dma((D,)), dma((D,)), dma((M,)), dma((M,)),
        dma((D,)), dma((D,)), dma((M,)), dma((M,)), dma((D,)), dma((D,)), dma((M,)), dma((M,)),
        dma((5, M)), dma((5, M)), dma((7, M)), dma((7, M)), pltpu.SemaphoreType.REGULAR((2 + M,)),
    ]
    if G > 1:
        scratch += [
            pltpu.VMEM((G, M, U, K // 8), BF16),
            pltpu.VMEM((G, M, LP // 8, LP), BF16),
            dma((G, M)), dma((G, M)), dma((G, M)), dma((G, M)),
        ]
    out, gw1, gw2, vec = pl.pallas_call(
        functools.partial(kernel, D, M, U, LP, K, R),
        out_shape=[
            jax.ShapeDtypeStruct((U, R), BF16),
            jax.ShapeDtypeStruct((U, K), BF16),
            jax.ShapeDtypeStruct((U, -(-M * U // 128) * 128), BF16),
            jax.ShapeDtypeStruct((8, LP), F32),
        ],
        in_specs=[vmem] * 9 + [hbm, hbm, hbm],
        out_specs=[hbm, hbm, hbm, vmem],
        scratch_shapes=scratch,
        compiler_params=pltpu.CompilerParams(
            collective_id=0, has_side_effects=True, vmem_limit_bytes=64 * 2**20 - 2**16
        ),
    )(ids[None, :], hash_mult[None, :], hash_add[None, :], *par, w1, w2, cot)
    out, gw1, gw2, *v = pl.pallas_call(
        functools.partial(finish, U),
        out_shape=[
            jax.ShapeDtypeStruct((U, R), BF16),
            jax.ShapeDtypeStruct((U, K), F32),
            jax.ShapeDtypeStruct((U, M * U), F32),
        ]
        + [jax.ShapeDtypeStruct((1, U), F32)] * 6,
        in_specs=[hbm, hbm, hbm, vmem],
        out_specs=[hbm, hbm, hbm] + [vmem] * 6,
        scratch_shapes=[
            pltpu.VMEM((U, R), BF16),
            pltpu.VMEM((U, K), BF16),
            pltpu.VMEM(gw2.shape, BF16),
            pltpu.VMEM((U, K), F32),
            pltpu.VMEM((U, M * U), F32),
            dma((6,)),
            dma((6,)),
        ],
        compiler_params=pltpu.CompilerParams(vmem_limit_bytes=63 * 2**20),
    )(out, gw1, gw2, vec)
    v = [x[0] for x in v]
    return (out, gw1, v[0], v[1], v[2], gw2, v[3], v[4], v[5])


def solution(mesh):
    return jax.shard_map(
        per_device,
        mesh=mesh,
        in_specs=(
            P("dp"), P(), P(), P("mp", None), P("mp"), P("mp"), P("mp"),
            P("mp", None), P("mp"), P("mp"), P("mp"), P("mp", "dp"),
        ),
        out_specs=(
            P("mp", "dp"), P("mp", None), P("mp"), P("mp"), P("mp"),
            P("mp", None), P("mp"), P("mp"), P("mp"),
        ),
        check_vma=False,
    )
```

```python
import functools

import jax
import jax.numpy as jnp
from jax import lax
from jax.experimental import pallas as pl
from jax.experimental.pallas import tpu as pltpu
from jax.sharding import PartitionSpec as P

MESH = pl.DeviceIdType.MESH
F32, BF16, I32 = jnp.float32, jnp.bfloat16, jnp.int32
epsilon = 1e-05


def dot(a, b):
    return lax.dot_general(a, b, (((1,), (0,)), ((), ())), preferred_element_type=F32)


def dot_nt(a, b):
    return lax.dot_general(a, b, (((1,), (1,)), ((), ())), preferred_element_type=F32)


def mish_parts(v):
    u = jnp.exp(jnp.minimum(v, 20.0))
    n = u * (u + 2.0)
    d = n + 2.0
    r = pl.reciprocal(d, approx=True)
    t = n * r
    return v * t, t + v * ((4.0 * (n - u) * r) * r)


def mish(v):
    u = jnp.exp(jnp.minimum(v, 20.0))
    n = u * (u + 2.0)
    d = n + 2.0
    r = pl.reciprocal(d, approx=True)
    return v * (n * r)


def lane_part(x):
    out = x[:, :128]
    for at in range(128, x.shape[1], 128):
        out = out + x[:, at : at + 128]
    return out


def kernel(
    D, M, U, LP, K, R,
    ids_ref, mult_ref, add_ref, b1_ref, s1_ref, t1_ref, b2_ref, s2_ref, t2_ref, w1_ref, w2_ref, cot_ref,
    out_ref, gw1_ref, gw2_ref, vec_ref,
    A, B, C, W2, G1, E1, F, H, act2, slo2, col, RW, acc, hcol,
    pv, ar1, ar2, ar2z, ar3, ar3z, ar4, ar4s, ar4z,
    w1s, w1r, w2s, w2r, pvs, pvr, cts, ctr, loc,
    a1s, a1r, a2s, a2r, a2zs, a2zr, a3s, a3r, a3zs, a3zr, a4s, a4r, a4zs, a4zr,
    g1s, g1r, g2s, g2r, free, *extra,
):
    Q = R // M
    G = D // 8
    TL = min(512, Q)
    NT = Q // TL
    PER = K // LP
    NA = M // PER
    K8 = K // 8
    J8 = M * LP // 8
    S8 = LP // 8
    N = float(R * D)
    d = lax.axis_index("dp")
    m = lax.axis_index("mp")
    i = lax.rem(d, 8)
    c = lax.rem(i, 2)
    x = lax.rem(i // 2, 2)
    y = i // 4
    hi = (1 - c) * x + c * y
    lo = (1 - c) * y + c * x
    p = 4 * c + 2 * hi + lo
    core_dev = (d + 1 - 2 * c, m)
    flip_x = d + 2 - 4 * x
    flip_y = d + 4 - 8 * y
    hi_dev = ((1 - c) * flip_x + c * flip_y, m)
    lo_dev = ((1 - c) * flip_y + c * flip_x, m)
    up = [lax.rem(m + k, M) for k in range(M)]
    down = [lax.rem(m - k + M, M) for k in range(M)]
    others = [lax.rem(d + k, D) for k in range(D)]
    sent = []

    def remote(src, dst, ss, rs, dev):
        cp = pltpu.make_async_remote_copy(
            src_ref=src, dst_ref=dst, send_sem=ss, recv_sem=rs, device_id=dev, device_id_type=MESH
        )
        return cp

    def send(src, dst, ss, rs, dev):
        cp = remote(src, dst, ss, rs, dev)
        cp.start()
        sent.append(cp)
        return cp

    def gone(cp):
        cp.wait_send()
        sent[:] = [other for other in sent if other is not cp]

    def lanes(ref, at, size):
        return ref.at[:, pl.ds(pl.multiple_of(at, 128), size)]

    def rows(ref, at, size):
        return ref.at[pl.ds(pl.multiple_of(at, 16), size)]

    bar = pltpu.get_barrier_semaphore()
    greeted = [core_dev, hi_dev, lo_dev] if G == 1 else [(others[k], m) for k in range(1, D)]
    greeted += [(d, up[k]) for k in range(1, M)]
    for dev in greeted:
        pl.semaphore_signal(bar, inc=1, device_id=dev, device_id_type=MESH)

    w2_loc = pltpu.make_async_copy(w2_ref, G1, loc.at[1])
    w2_loc.start()
    w1_loc = pltpu.make_async_copy(w1_ref, C.at[m], loc.at[0])
    w1_loc.start()
    cot_loc = pltpu.make_async_copy(lanes(cot_ref, m * Q, Q), lanes(F.at[m], 0, Q), loc.at[2])
    pv[m] = jnp.zeros((8, LP), F32)
    for n, ref in enumerate((b1_ref, s1_ref, t1_ref, b2_ref, s2_ref, t2_ref)):
        pv[m, n : n + 1, :U] = ref[...]
    pl.semaphore_wait(bar, len(greeted))

    ag1, ag2, agp, ct = {}, {}, {}, {}
    for k in range(1, M):
        agp[k] = send(pv.at[m], pv.at[m], pvs.at[k], pvr.at[k], (d, up[k]))
    for ag, own, buf, size, ss, rs in ((ag1, w1_ref, C, K8, w1s, w1r), (ag2, None, W2, J8, w2s, w2r)):
        for k in range(1, M):
            part = lanes(buf.at[m], p * size, size)
            mine = part if own is None else lanes(own, p * size, size)
            ag[0, k] = remote(mine, part, ss.at[0, k], rs.at[0, k], (d, up[k]))
            for step, dev, at, width in (
                (1, lo_dev, p, 1), (2, hi_dev, 4 * c + 2 * hi, 2), (3, core_dev, 4 * c, 4)
            ):
                part = lanes(buf.at[down[k]], at * size, width * size)
                ag[step, k] = remote(part, part, ss.at[step, k], rs.at[step, k], dev)
    for k in range(1, M):
        ag1[0, k].start()
    w2_loc.wait()
    for b in range(M):
        W2[m, :, (b + 1) * LP - 128 : (b + 1) * LP] = jnp.zeros((U, 128), BF16)
        W2[m, :, b * LP : b * LP + U] = G1[:, b * U : (b + 1) * U]

    def gather_stage(step, ag):
        for k in range(1, M):
            ag[step - 1, k].wait_recv()
            ag[step, k].start()

    def stage1(step):
        gather_stage(step, ag1)

    def stage2(step):
        gather_stage(step, ag2)

    hrow = jnp.concatenate(
        [mult_ref[...].astype(F32), add_ref[...].astype(F32), jnp.zeros((126, K), F32)], axis=0
    )
    hcol[...] = hrow.T

    HT = 128

    def encode(q, put):
        def step(t, _):
            at = pl.multiple_of(t * HT, HT)
            both = hcol[pl.ds(at, HT), :].astype(I32)
            v = both[:, 0:1] * ids_ref[:, pl.ds(pl.multiple_of(q * Q, 128), Q)] + both[:, 1:2]
            for _ in range(2):
                top = lax.shift_right_logical(v, 16)
                v = (v & 65535) + ((top << 4) - top)
            v = jnp.where(v >= 65521, v - 65521, v)
            put(t, (v.astype(F32) * (2.0 / 65520.0) - 1.0).astype(BF16))
            return 0

        lax.fori_loop(0, K // HT, step, 0)

    def make_col(b):
        col[b] = jnp.concatenate([RW[b], jnp.zeros((128 - RW.shape[1], LP), F32)], axis=0).T

    def make_cols():
        def step(b, _):
            make_col(b)
            return 0

        lax.fori_loop(0, M, step, 0)

    def to_a(q):
        def put(t, value):
            A[q, pl.ds(pl.multiple_of(t * HT, HT), HT), :] = value

        return put

    def to_e1(t, value):
        E1[pl.ds(pl.multiple_of(lax.rem(t, LP // HT) * HT, HT), HT), pl.ds(pl.multiple_of(t // (LP // HT) * Q, 128), Q)] = value

    def row_of(slot):
        return jnp.sum(acc[slot].T, axis=0, keepdims=True)

    acc[...] = jnp.zeros_like(acc)
    for b in range(M):
        B[pl.ds(b * LP + U // 16 * 16, LP - U // 16 * 16), :] = jnp.zeros((LP - U // 16 * 16, R), BF16)

    RW[...] = jnp.zeros_like(RW)
    RW[m, 0:8] = pv[m]
    make_col(m)
    encode(m, to_a(m))
    w1_loc.wait()

    def mm1_own(b):
        def step(t, _):
            at = pl.multiple_of(t * TL, TL)
            act, slope = mish_parts(dot(C[b], A[m, :, pl.ds(at, TL)]) + col[b, :U, 0:1])
            H[b, :, pl.ds(at, TL)] = slope.astype(BF16)
            B[pl.ds(pl.multiple_of(b * LP, LP), U), pl.ds(pl.multiple_of(m * Q + t * TL, TL), TL)] = act.astype(BF16)
            acc[0, :U] += lane_part(act)
            acc[1, :U] += lane_part(act * act)
            return 0

        lax.fori_loop(0, NT, step, 0)

    def mm1_rest(b):
        def step(t, _):
            q = lax.rem(m + t, M)
            act = mish(dot(C[b], A[q]) + col[b, :U, 0:1])
            B[pl.ds(pl.multiple_of(b * LP, LP), U), pl.ds(pl.multiple_of(q * Q, Q), Q)] = act.astype(BF16)
            acc[0, :U] += lane_part(act)
            acc[1, :U] += lane_part(act * act)
            return 0

        lax.fori_loop(1, M, step, 0)

    def mm1_sums(b):
        ar1[d, pl.ds(b, 1), :] = row_of(0)
        ar1[d, pl.ds(b + M, 1), :] = row_of(1)
        acc[0:2] = jnp.zeros((2, LP, 128), F32)

    mm1_own(m)
    stage1(1)
    for k in range(1, M):
        ag2[0, k].start()

    def enc_step(k, _):
        q = lax.rem(m + M - k, M)
        encode(q, to_a(q))
        return 0

    lax.fori_loop(1, M, enc_step, 0)
    stage1(2)
    mm1_rest(m)
    mm1_sums(m)
    stage2(1)
    cot_loc.start()
    for q in range(1, M):
        ct[q] = send(
            lanes(cot_ref, up[q] * Q, Q), lanes(F.at[m], 0, Q), cts.at[q], ctr.at[q], (d, up[q])
        )
    stage1(3)
    for k in range(1, M):
        agp[k].wait_recv()
    for b in range(M):
        RW[b, 0:8] = pv[b]
    make_cols()
    def mm1_other(k, _):
        b = lax.rem(m + M - k, M)
        part = lanes(C.at[b], 4 * c * K8, 4 * K8)
        remote(part, part, w1s.at[3, k], w1r.at[3, k], core_dev).wait_recv()
        mm1_own(b)
        mm1_rest(b)
        mm1_sums(b)
        pl.when(k == 1)(functools.partial(stage2, 2))
        return 0

    lax.fori_loop(1, M, mm1_other, 0)

    def all_dp(buf, ss, rs):
        cps = []
        for k in range(1, D):
            cps.append(send(buf.at[d], buf.at[d], ss.at[k], rs.at[k], (others[k], m)))
        return cps

    def total(buf, cps):
        for cp in cps:
            cp.wait_recv()
        out = buf[0]
        for k in range(1, D):
            out = out + buf[k]
        return out

    cps1 = all_dp(ar1, a1s, a1r)
    stage2(3)
    for cp in ag1.values():
        cp.wait_send()
    cot_all = []
    for q in range(M):
        cp = pltpu.make_async_copy(lanes(cot_ref, q * Q, Q), lanes(C.at[q], 0, Q), loc.at[3 + q])
        cot_all.append(cp)
        cp.start()
    for k in range(1, M):
        ag2[3, k].wait_recv()

    def make_e1(b):
        def step(h, _):
            part = W2[h, :, pl.ds(pl.multiple_of(b * LP, LP), LP)].astype(F32) * col[h, :U, 1:2]
            for n in range(LP // 128):
                acc[n, :U] = part[:, n * 128 : (n + 1) * 128]
            for n in range(LP // 128):
                E1[n * 128 : (n + 1) * 128, pl.ds(pl.multiple_of(h * LP, LP), LP)] = acc[n].T.astype(BF16)
            return 0

        lax.fori_loop(0, M, step, 0)
        acc[...] = jnp.zeros_like(acc)

    const = jnp.zeros((8, M * LP), F32)
    for b in range(M):
        shift = jnp.broadcast_to(pv[b, 2:3, :U], (8, U))
        upper = shift.astype(BF16)
        lower = (shift - upper.astype(F32)).astype(BF16)
        const = const + dot(upper, W2[b]) + dot(lower, W2[b])
    for b in range(M):
        RW[b, 8:9] = const[0:1, b * LP : (b + 1) * LP] + pv[b, 3:4]
    make_e1(m)

    tot = total(ar1, cps1)
    mean = tot[:M] / N
    inv = lax.rsqrt(tot[M:] / N - mean * mean + epsilon)
    for b in range(M):
        RW[b, 9:10] = inv[b : b + 1]
        RW[b, 10:11] = -mean[b : b + 1] * inv[b : b + 1]
    make_cols()
    for cp in cot_all:
        cp.wait()

    def mm2(t, _):
        at = pl.multiple_of(t * TL, TL)
        for b in range(M):
            part = B[b * LP : b * LP + U, pl.ds(at, TL)].astype(F32)
            B[b * LP : b * LP + U, pl.ds(at, TL)] = (part * col[b, :U, 9:10] + col[b, :U, 10:11]).astype(BF16)
        v = dot(E1[:U], B[:, pl.ds(at, TL)]) + col[m, :U, 8:9]
        act, slope = mish_parts(v)
        act2[:, pl.ds(at, TL)] = act.astype(BF16)
        slo2[:, pl.ds(at, TL)] = slope.astype(BF16)
        g = C[t // NT, :, pl.ds(pl.multiple_of(lax.rem(t, NT) * TL, TL), TL)].astype(F32)
        acc[0, :U] += lane_part(act)
        acc[1, :U] += lane_part(act * act)
        acc[2, :U] += lane_part(g)
        acc[3, :U] += lane_part(g * act)
        return 0

    lax.fori_loop(0, M * NT, mm2, 0)
    for s in range(4):
        ar2[d, s : s + 1, :] = row_of(s)
    ar2[d, 4:8, :] = jnp.zeros((4, LP), F32)
    acc[...] = jnp.zeros_like(acc)
    cps2 = all_dp(ar2, a2s, a2r)

    def a_at(base, b):
        return base + b // PER, pl.multiple_of(lax.rem(b, PER) * LP, LP)

    def mm2_own(b):
        make_e1(b)
        act_at, row = a_at(0, b)
        v = dot(E1[:U], B[:, pl.ds(pl.multiple_of(m * Q, Q), Q)]) + col[b, :U, 8:9]
        act, slope = mish_parts(v)
        A[act_at, pl.ds(row, U)] = act.astype(BF16)
        A[act_at + NA, pl.ds(row, U)] = slope.astype(BF16)

    def own_loop(k, _):
        mm2_own(lax.rem(m + k, M))
        return 0

    mm2_own(up[1])
    tot = total(ar2, cps2)
    mean = tot[0:1] / N
    inv = lax.rsqrt(tot[1:2] / N - mean * mean + epsilon)
    sum_g = tot[2:3]
    sum_gn = inv * (tot[3:4] - mean * sum_g)
    k1 = pv[m, 4:5] * inv
    k2 = -k1 * inv * sum_gn / N
    k3 = -k1 * sum_g / N - mean * k2
    ar2z[m, 0:1] = k1
    ar2z[m, 1:2] = k2
    ar2z[m, 2:3] = k3
    ar2z[m, 3:4] = k1
    ar2z[m, 4:5] = pv[m, 5:6] - mean * k1
    ar2z[m, 5:6] = sum_g
    ar2z[m, 6:7] = sum_gn
    ar2z[m, 7:8] = jnp.zeros((1, LP), F32)
    cps2z = [send(ar2z.at[m], ar2z.at[m], a2zs.at[k], a2zr.at[k], (d, up[k])) for k in range(1, M)]
    RW[m, 16:24] = ar2z[m]
    make_col(m)

    def back2(t, _):
        at = pl.multiple_of(t * TL, TL)
        a = act2[:, pl.ds(at, TL)].astype(F32)
        g = C[t // NT, :, pl.ds(pl.multiple_of(lax.rem(t, NT) * TL, TL), TL)].astype(F32)
        grad = (g * col[m, :U, 16:17] + a * col[m, :U, 17:18] + col[m, :U, 18:19]) * slo2[:, pl.ds(at, TL)].astype(F32)
        grad = grad.astype(BF16)
        slo2[:, pl.ds(at, TL)] = grad
        acc[0, :U] += lane_part(grad.astype(F32))
        return 0

    lax.fori_loop(0, M * NT, back2, 0)
    gb2 = row_of(0)
    ar3[d, 2 * M : 2 * M + 1, :] = gb2
    ar3[d, 2 * M + 1 : 2 * M + 8, :] = jnp.zeros((7, LP), F32)
    acc[0:1] = jnp.zeros((1, LP, 128), F32)

    L1 = pl.multiple_of(lax.rem(m + 1, M) * Q, 128)
    LR = pl.multiple_of(L1 + LP, 128)

    def rowsum(x):
        acc[0, :U] = lane_part(x[:, : U // 128 * 128]) + jnp.where(
            lax.broadcasted_iota(I32, (U, 128), 1) >= 128 - U % 128, x[:, U - 128 :], 0.0
        )
        return row_of(0)

    gb2_all8 = jnp.broadcast_to(gb2[:, :U], (8, U))
    gb2_up = gb2_all8.astype(BF16)
    gb2_low = (gb2_all8 - gb2_up.astype(F32)).astype(BF16)
    ar3[d, 0 : 2 * M, :] = jnp.zeros((2 * M, LP), F32)

    def grad_w2(b, _):
        at = pl.multiple_of(b * LP, LP)
        g = dot_nt(B[pl.ds(at, LP), :], slo2[...])
        w16 = W2[b, :, pl.ds(pl.multiple_of(m * LP, LP), LP)][:, :U]
        w = w16.astype(F32)
        ar3[d, pl.ds(b, 1), :U] = dot_nt(gb2_up, w16)[0:1] + dot_nt(gb2_low, w16)[0:1]
        ar3[d, pl.ds(b + M, 1), :] = rowsum(w * g[:U])
        g = g * col[b, :, 1:2] + col[b, :, 2:3] * gb2[:, :U]
        B[pl.ds(at, LP), pl.ds(L1, U)] = g.astype(BF16)
        B[pl.ds(at, LP), pl.ds(L1 + U // 128 * 128, LP - U // 128 * 128)] = jnp.where(
            lax.broadcasted_iota(I32, (LP, LP - U // 128 * 128), 1) < U - U // 128 * 128,
            B[pl.ds(at, LP), pl.ds(L1 + U // 128 * 128, LP - U // 128 * 128)].astype(F32),
            0.0,
        ).astype(BF16)
        return 0

    lax.fori_loop(0, M, grad_w2, 0)
    cps3 = all_dp(ar3, a3s, a3r)
    for n, dev in ((0, core_dev), (1, hi_dev), (2, lo_dev)):
        pl.semaphore_signal(free.at[n], inc=1, device_id=dev, device_id_type=MESH)
    for k in range(1, M):
        pl.semaphore_signal(free.at[2 + k], inc=1, device_id=(d, up[k]), device_id_type=MESH)

    HALF = {0: (1 - c) * 4, 1: 4 * c + 2 * (1 - hi), 2: 4 * c + 2 * hi + 1 - lo}
    KEEP = {0: 4 * c, 1: 4 * c + 2 * hi, 2: p}
    START = {0: 0, 1: 4, 2: 6}
    PARTNER = {0: core_dev, 1: hi_dev, 2: lo_dev}
    g2cp = {}

    def b_rows(b, at, size, lane):
        return B.at[pl.ds(pl.multiple_of(b * LP + at * S8, 16), size * S8), pl.ds(lane, LP)]

    def g2_send(n):
        pl.semaphore_wait(free.at[n], 1)
        for b in range(M):
            g2cp[n, b].start()

    def g2_add(n):
        for b in range(M):
            g2cp[n, b].wait_recv()
            size = (4 >> n) * S8
            keep = pl.ds(pl.multiple_of(b * LP + KEEP[n] * S8, 16), size)
            came = pl.ds(b * LP + START[n] * S8, size)
            B[keep, pl.ds(L1, LP)] = (
                B[keep, pl.ds(L1, LP)].astype(F32) + B[came, pl.ds(LR, LP)].astype(F32)
            ).astype(BF16)

    def l2_of(z):
        return pl.multiple_of(lax.rem(z + 2, M) * Q, 128)

    L2 = l2_of(m)
    for b in range(M):
        for n in range(3):
            g2cp[n, b] = remote(
                b_rows(b, HALF[n], 4 >> n, L1), b_rows(b, START[n], 4 >> n, LR), g2s.at[n, b], g2r.at[n, b], PARTNER[n]
            )
        for n, at, size, dev in ((4, p, 1, lo_dev), (5, 4 * c + 2 * hi, 2, hi_dev), (6, 4 * c, 4, core_dev)):
            part = b_rows(b, at, size, L2)
            g2cp[n, b] = remote(part, part, g2s.at[n, b], g2r.at[n, b], dev)
        if b:
            g2cp[3, b] = remote(
                b_rows(up[b], p, 1, L1),
                B.at[pl.ds(pl.multiple_of(m * LP + p * S8, 16), S8), pl.ds(l2_of(up[b]), LP)],
                g2s.at[3, b], g2r.at[3, b], (d, up[b]),
            )

    if G > 1:
        x1, x2, x1s, x1r, x2s, x2r = extra

    def g2_groups():
        cps = []
        for k in range(1, G):
            to = (lax.rem(d + 8 * k, D), m)
            for b in range(M):
                cps.append(send(b_rows(b, p, 1, L1), x2.at[d // 8, b], x2s.at[k, b], x2r.at[k, b], to))
        for b in range(M):
            x2[d // 8, b] = B[pl.ds(pl.multiple_of(b * LP + p * S8, 16), S8), pl.ds(L1, LP)]
        for cp in cps:
            cp.wait_recv()
        for cp in cps:
            gone(cp)
        for b in range(M):
            v = x2[0, b].astype(F32)
            for k in range(1, G):
                v = v + x2[k, b].astype(F32)
            B[pl.ds(pl.multiple_of(b * LP + p * S8, 16), S8), pl.ds(L1, LP)] = v.astype(BF16)

    def g2_z():
        if G > 1:
            g2_groups()
        for k in range(1, M):
            pl.semaphore_wait(free.at[2 + M - k], 1)
            g2cp[3, k].start()
        mine = pl.ds(pl.multiple_of(m * LP + p * S8, 16), S8)
        B[mine, pl.ds(L2, LP)] = B[mine, pl.ds(L1, LP)]

    def g2_gather(n):
        for b in range(1 if n == 4 else 0, M):
            g2cp[n - 1, b].wait_recv()
        for b in range(M):
            g2cp[n, b].start()

    g2_send(0)
    lax.fori_loop(2, M, own_loop, 0)
    tot = total(ar3, cps3)
    ar3z[m] = tot[: 2 * M]
    gb2_all = tot[2 * M : 2 * M + 1]
    cps3z = [send(ar3z.at[m], ar3z.at[m], a3zs.at[k], a3zr.at[k], (d, up[k])) for k in range(1, M)]
    g2_add(0)
    g2_send(1)
    encode(m, to_e1)
    for cp in cps2z:
        cp.wait_recv()
    for b in range(M):
        RW[b, 16:24] = ar2z[b]
    for cp in cps3z:
        cp.wait_recv()
    tot = ar3z[0]
    for b in range(1, M):
        tot = tot + ar3z[b]
    for b in range(M):
        k1 = pv[b, 1:2] * RW[b, 9:10]
        RW[b, 24:25] = k1
        RW[b, 25:26] = -k1 * tot[M + b : M + b + 1] / N
        RW[b, 26:27] = -k1 * tot[b : b + 1] / N
    make_cols()
    pick = lax.broadcasted_iota(I32, (2 * M, 1), 0)
    vec_ref[0:1, :] = jnp.zeros((1, LP), F32)
    vec_ref[1:2, :] = jnp.sum(jnp.where(pick == M + m, tot, 0.0), axis=0, keepdims=True)
    vec_ref[2:3, :] = jnp.sum(jnp.where(pick == m, tot, 0.0), axis=0, keepdims=True)
    vec_ref[3:4, :] = gb2_all
    vec_ref[4:5, :] = ar2z[m, 6:7]
    vec_ref[5:6, :] = ar2z[m, 5:6]
    vec_ref[6:8, :] = jnp.zeros((2, LP), F32)

    PADAT = U // 16 * 16

    def put_grad(b, value, at, size):
        slot, row = a_at(NA, b)
        A[slot, pl.ds(row, U), pl.ds(at, size)] = value

    for b in range(M):
        slot, row = NA + b // PER, (b % PER) * LP
        A[slot, row + PADAT : row + LP, :] = jnp.where(
            lax.broadcasted_iota(I32, (LP - PADAT, Q), 0) < U - PADAT,
            A[slot, row + PADAT : row + LP, :].astype(F32),
            0.0,
        ).astype(BF16)
    cot_loc.wait()

    def back2_own(b):
        act_at, row = a_at(0, b)

        def step(t, _):
            at = pl.multiple_of(t * TL, TL)
            a = A[act_at, pl.ds(row, U), pl.ds(at, TL)].astype(F32)
            s = A[act_at + NA, pl.ds(row, U), pl.ds(at, TL)].astype(F32)
            g = F[b, :, pl.ds(at, TL)].astype(F32)
            grad = (g * col[b, :U, 16:17] + a * col[b, :U, 17:18] + col[b, :U, 18:19]) * s
            A[act_at + NA, pl.ds(row, U), pl.ds(at, TL)] = grad.astype(BF16)
            return 0

        lax.fori_loop(0, NT, step, 0)

    def copy_own(t, _):
        at = pl.multiple_of(t * TL, TL)
        put_grad(m, slo2[:, pl.ds(pl.multiple_of(m * Q + t * TL, TL), TL)], at, TL)
        return 0

    lax.fori_loop(0, NT, copy_own, 0)
    for k in range(1, M):
        ct[k].wait_recv()
        back2_own(down[k])


    def back1(b):
        def step(t, _):
            at = pl.multiple_of(t * TL, TL)
            dh = dot(W2[b, :, 0:K], A[NA, :, pl.ds(at, TL)])
            for n in range(1, NA):
                dh = dh + dot(W2[b, :, n * K : (n + 1) * K], A[NA + n, :, pl.ds(at, TL)])
            norm = B[pl.ds(pl.multiple_of(b * LP, LP), U), pl.ds(pl.multiple_of(m * Q + t * TL, TL), TL)].astype(F32)
            grad = dh * col[b, :U, 24:25] + norm * col[b, :U, 25:26] + col[b, :U, 26:27]
            grad = (grad * H[b, :, pl.ds(at, TL)].astype(F32)).astype(BF16)
            H[b, :, pl.ds(at, TL)] = grad
            acc[0, :U] += lane_part(grad.astype(F32))
            return 0

        lax.fori_loop(0, NT, step, 0)
        ar4[d, pl.ds(b, 1), :] = row_of(0)
        acc[0:1] = jnp.zeros((1, LP, 128), F32)

        def mm(t, _):
            F[b, :, pl.ds(pl.multiple_of(t * LP, LP), LP)] = dot_nt(
                H[b], E1[:, pl.ds(pl.multiple_of(t * Q, Q), Q)]
            ).astype(BF16)
            return 0

        lax.fori_loop(0, PER, mm, 0)

    acc[0:1] = jnp.zeros((1, LP, 128), F32)
    ar4[d] = jnp.zeros((ar4.shape[1], LP), F32)
    K2 = 4 * K8
    FROM = {0: 0, 1: K2, 2: K2 + 2 * K8}
    order = [up[(j + 1) % M] for j in range(M)]
    def g1_cp(n, j):
        b = lax.rem(m + 1 + j, M)
        if n == 3:
            return remote(
                lanes(F.at[b], p * K8, K8), C.at[m, :, pl.ds(K - K8, K8)], g1s.at[3, j + 1], g1r.at[3, j + 1], (d, b)
            )
        return remote(
            lanes(F.at[b], HALF[n] * K8, K2 >> n), lanes(C.at[b], FROM[n], K2 >> n), g1s.at[n, j], g1r.at[n, j], PARTNER[n]
        )

    def g1_groups(b, j):
        mine = pl.ds(pl.multiple_of(p * K8, 128), K8)
        cps = []
        for k in range(1, G):
            to = (lax.rem(d + 8 * k, D), m)
            cps.append(send(lanes(F.at[b], p * K8, K8), x1.at[d // 8, j], x1s.at[k, j], x1r.at[k, j], to))
        x1[d // 8, j] = F[b, :, mine]
        for cp in cps:
            cp.wait_recv()
        for cp in cps:
            gone(cp)
        v = x1[0, j].astype(F32)
        for k in range(1, G):
            v = v + x1[k, j].astype(F32)
        F[b, :, mine] = v.astype(BF16)

    def g1_stage(n, j):
        b = lax.rem(m + 1 + j, M)
        g1_cp(n - 1, j).wait_recv()
        keep = pl.ds(pl.multiple_of(KEEP[n - 1] * K8, 128), K2 >> (n - 1))
        came = C[b, :, FROM[n - 1] : FROM[n - 1] + (K2 >> (n - 1))]
        F[b, :, keep] = (F[b, :, keep].astype(F32) + came.astype(F32)).astype(BF16)
        if n == 3 and G > 1:
            g1_groups(b, j)
        if n < 3 or not isinstance(j, int) or j < M - 1:
            g1_cp(n, j).start()
        else:
            C[m, :, K - K8 : K] = F[m, :, pl.ds(pl.multiple_of(p * K8, 128), K8)]

    def block(j, _):
        back1(lax.rem(m + 1 + j, M))
        g1_cp(0, j).start()
        for n in (3, 2, 1):
            pl.when(j >= n)(functools.partial(g1_stage, n, j - n))

        @pl.when(j == 0)
        def _():
            g2_add(1)
            g2_send(2)

        @pl.when(j == 1)
        def _():
            g2_add(2)
            g2_z()

        pl.when(j == 2)(functools.partial(g2_gather, 4))
        pl.when(j == 3)(functools.partial(g2_gather, 5))
        return 0

    lax.fori_loop(0, M, block, 0)
    cps4 = all_dp(ar4, a4s, a4r)
    for n in (3, 2, 1):
        g1_stage(n, M - n)
    g2_gather(6)

    tot4 = total(ar4, cps4)
    for b in range(M):
        ar4s[b] = jnp.broadcast_to(tot4[b : b + 1], (8, LP))
    ar4z[m] = ar4s[m]
    cps4z = [send(ar4s.at[up[k]], ar4z.at[m], a4zs.at[k], a4zr.at[k], (d, up[k])) for k in range(1, M)]
    g1_stage(3, M - 2)
    g1_stage(2, M - 1)
    def finish(t, _):
        at = pl.multiple_of(t * TL, TL)
        a = act2[:, pl.ds(at, TL)].astype(F32)
        act2[:, pl.ds(at, TL)] = (a * col[m, :U, 19:20] + col[m, :U, 20:21]).astype(BF16)
        return 0

    lax.fori_loop(0, M * NT, finish, 0)
    out_copy = pltpu.make_async_copy(act2, out_ref, loc.at[0])
    out_copy.start()
    g1_stage(3, M - 1)
    for b in range(M):
        g2cp[6, b].wait_recv()
    for b in range(M):
        slo2[:, b * U : (b + 1) * U] = B[b * LP : b * LP + U, pl.ds(L2, LP)][:, :U]
    gw2_copy = pltpu.make_async_copy(lanes(slo2, 0, gw2_ref.shape[1]), gw2_ref, loc.at[2])
    gw2_copy.start()
    for j in range(M - 1):
        g1_cp(3, j).wait_recv()
    v = C[0, :, K - K8 : K].astype(F32)
    for b in range(1, M):
        v = v + C[b, :, K - K8 : K].astype(F32)
    G1[:, pl.ds(pl.multiple_of(p * K8, 128), K8)] = v.astype(BF16)
    diag_dev = (d + 2 - 4 * x + 4 - 8 * y, m)
    mine = lanes(G1, p * K8, K8)
    ga = [send(mine, mine, g1s.at[4, n], g1r.at[4, n], dev) for n, dev in enumerate((diag_dev, hi_dev, lo_dev))]
    for cp in ga:
        cp.wait_recv()
    part = lanes(G1, 4 * c * K8, K2)
    ga = send(part, part, g1s.at[4, 3], g1r.at[4, 3], core_dev)
    for cp in cps4z:
        cp.wait_recv()
    v = ar4z[0]
    for b in range(1, M):
        v = v + ar4z[b]
    vec_ref[0:1, :] = v[0:1]
    ga.wait_recv()
    gw1_copy = pltpu.make_async_copy(lanes(G1, 0, K), gw1_ref, loc.at[1])
    gw1_copy.start()
    for cp in [*ag2.values(), *g2cp.values(), *(g1_cp(n, j) for n in range(4) for j in range(M - n // 3))]:
        cp.wait_send()
    out_copy.wait()
    gw1_copy.wait()
    gw2_copy.wait()
    for cp in sent:
        cp.wait_send()


def finish(U, out_in, gw1_in, gw2_in, vec_in, out_ref, gw1_ref, gw2_ref, *tail):
    *vecs, held, held1, held2, wide1, wide2, sem_in, sem_out = tail
    n = 4
    width = held.shape[1] // n
    pieces = [pl.ds(k * width, width) for k in range(n)]
    ins = [
        pltpu.make_async_copy(gw2_in, held2, sem_in.at[n]),
        pltpu.make_async_copy(gw1_in, held1, sem_in.at[n + 1]),
    ] + [pltpu.make_async_copy(out_in.at[:, at], held.at[:, at], sem_in.at[k]) for k, at in enumerate(pieces)]
    for cp in ins:
        cp.start()
    outs = [
        pltpu.make_async_copy(wide2, gw2_ref, sem_out.at[n]),
        pltpu.make_async_copy(wide1, gw1_ref, sem_out.at[n + 1]),
    ] + [pltpu.make_async_copy(held.at[:, at], out_ref.at[:, at], sem_out.at[k]) for k, at in enumerate(pieces)]
    ins[0].wait()
    wide2[...] = held2[:, : wide2.shape[1]].astype(F32)
    outs[0].start()
    ins[1].wait()
    wide1[...] = held1[...].astype(F32)
    outs[1].start()
    for k in range(n):
        ins[2 + k].wait()
        outs[2 + k].start()
    for k, ref in enumerate(vecs):
        ref[...] = vec_in[k : k + 1, :U]
    for cp in outs:
        cp.wait()


def per_device(ids, hash_mult, hash_add, w1, b1, s1, t1, w2, b2, s2, t2, cot):
    D, M = lax.axis_size("dp"), lax.axis_size("mp")
    U, K = w1.shape
    R = ids.shape[0]
    Q = R // M
    LP = -(-U // 128) * 128
    G = D // 8
    par = [x[None, :] for x in (b1, s1, t1, b2, s2, t2)]
    dma = pltpu.SemaphoreType.DMA
    vmem = pl.BlockSpec(memory_space=pltpu.VMEM)
    hbm = pl.BlockSpec(memory_space=pl.ANY)
    AR = -(-2 * M // 8) * 8
    scratch = [
        pltpu.VMEM((M, K, Q), BF16),
        pltpu.VMEM((M * LP, R), BF16),
        pltpu.VMEM((M, U, max(K, Q)), BF16),
        pltpu.VMEM((M, U, M * LP), BF16),
        pltpu.VMEM((U, max(K, M * U)), BF16),
        pltpu.VMEM((LP, M * LP), BF16),
        pltpu.VMEM((M, U, max(K, Q)), BF16),
        pltpu.VMEM((M, U, Q), BF16),
        pltpu.VMEM((U, R), BF16),
        pltpu.VMEM((U, R), BF16),
        pltpu.VMEM((M, LP, 128), F32),
        pltpu.VMEM((M, 32, LP), F32),
        pltpu.VMEM((4, LP, 128), F32),
        pltpu.VMEM((K, 128), F32),
        pltpu.VMEM((M, 8, LP), F32),
        pltpu.VMEM((D, AR, LP), F32),
        pltpu.VMEM((D, 8, LP), F32),
        pltpu.VMEM((M, 8, LP), F32),
        pltpu.VMEM((D, AR + 8, LP), F32),
        pltpu.VMEM((M, AR, LP), F32),
        pltpu.VMEM((D, 8, LP), F32),
        pltpu.VMEM((M, 8, LP), F32),
        pltpu.VMEM((M, 8, LP), F32),
        dma((4, M)), dma((4, M)), dma((4, M)), dma((4, M)),
        dma((M,)), dma((M,)), dma((M,)), dma((M,)), dma((3 + M,)),
        dma((D,)), dma((D,)), dma((D,)), dma((D,)), dma((M,)), dma((M,)),
        dma((D,)), dma((D,)), dma((M,)), dma((M,)), dma((D,)), dma((D,)), dma((M,)), dma((M,)),
        dma((5, M)), dma((5, M)), dma((7, M)), dma((7, M)), pltpu.SemaphoreType.REGULAR((2 + M,)),
    ]
    if G > 1:
        scratch += [
            pltpu.VMEM((G, M, U, K // 8), BF16),
            pltpu.VMEM((G, M, LP // 8, LP), BF16),
            dma((G, M)), dma((G, M)), dma((G, M)), dma((G, M)),
        ]
    out, gw1, gw2, vec = pl.pallas_call(
        functools.partial(kernel, D, M, U, LP, K, R),
        out_shape=[
            jax.ShapeDtypeStruct((U, R), BF16),
            jax.ShapeDtypeStruct((U, K), BF16),
            jax.ShapeDtypeStruct((U, -(-M * U // 128) * 128), BF16),
            jax.ShapeDtypeStruct((8, LP), F32),
        ],
        in_specs=[vmem] * 9 + [hbm, hbm, hbm],
        out_specs=[hbm, hbm, hbm, vmem],
        scratch_shapes=scratch,
        compiler_params=pltpu.CompilerParams(
            collective_id=0, has_side_effects=True, vmem_limit_bytes=64 * 2**20 - 2**16
        ),
    )(ids[None, :], hash_mult[None, :], hash_add[None, :], *par, w1, w2, cot)
    out, gw1, gw2, *v = pl.pallas_call(
        functools.partial(finish, U),
        out_shape=[
            jax.ShapeDtypeStruct((U, R), BF16),
            jax.ShapeDtypeStruct((U, K), F32),
            jax.ShapeDtypeStruct((U, M * U), F32),
        ]
        + [jax.ShapeDtypeStruct((1, U), F32)] * 6,
        in_specs=[hbm, hbm, hbm, vmem],
        out_specs=[hbm, hbm, hbm] + [vmem] * 6,
        scratch_shapes=[
            pltpu.VMEM((U, R), BF16),
            pltpu.VMEM((U, K), BF16),
            pltpu.VMEM(gw2.shape, BF16),
            pltpu.VMEM((U, K), F32),
            pltpu.VMEM((U, M * U), F32),
            dma((6,)),
            dma((6,)),
        ],
        compiler_params=pltpu.CompilerParams(vmem_limit_bytes=63 * 2**20),
    )(out, gw1, gw2, vec)
    v = [x[0] for x in v]
    return (out, gw1, v[0], v[1], v[2], gw2, v[3], v[4], v[5])


def solution(mesh):
    return jax.shard_map(
        per_device,
        mesh=mesh,
        in_specs=(
            P("dp"), P(), P(), P("mp", None), P("mp"), P("mp"), P("mp"),
            P("mp", None), P("mp"), P("mp"), P("mp"), P("mp", "dp"),
        ),
        out_specs=(
            P("mp", "dp"), P("mp", None), P("mp"), P("mp"), P("mp"),
            P("mp", None), P("mp"), P("mp"), P("mp"),
        ),
        check_vma=False,
    )
```
